256 devices in a mesh: gx: 32 (over z, x_lo, core), gy: 8 (over x_hi, y).
Axes of the slice: x: 4 (x_hi: 2, x_lo: 2; x = x_hi * 2 + x_lo), y: 4, z: 8, core: 2. Of those that a mesh axis runs over, the one named last changes fastest.
Arguments:
- field: bfloat16 [64, 64, 8, 384], P('gx', 'gy'), may hold values from -54 to 54
- cotangent: bfloat16 [64, 64, 8, 384], P('gx', 'gy'), may hold values from -6 to 6
- win_qkv: bfloat16 [384, 1152], replicated, may hold values from -2 to 2
- win_out: bfloat16 [384, 384], replicated, may hold values from -0.3125 to 0.3125
- axial_qkv: bfloat16 [384, 1152], replicated, may hold values from -2 to 2
- axial_out: bfloat16 [384, 384], replicated, may hold values from -0.3125 to 0.3125
- mlp_in: bfloat16 [384, 1536], replicated, may hold values from -0.3125 to 0.3125
- mlp_out: bfloat16 [1536, 384], replicated, may hold values from -0.15625 to 0.15625
- pattern: int32 [6, 3], replicated, may hold values from 0 to 7, as said below
Outputs:
- layer_output: bfloat16 [64, 64, 8, 384], P('gx', 'gy')
- field_grad: float32 [64, 64, 8, 384], P('gx', 'gy')
The draws below stay inside these ranges and needn't reach their ends.
Inputs may be any that keep to these rules, and one draw needn't show every extreme that they name: `pattern`: row h holds (base + dilation * j) mod 8 for j = 0 to 2, with a base per head and a dilation of 1 to 3 per head.
All inputs are finite; a program needn't handle non-finite values.
Results may differ from the reference program's by a relative error of at most 0.02.
The reference program's roundings to bfloat16 on the way count: a program that leaves them out, or rounds other values in their place, can miss the bound.
Values may be sent and summed in bfloat16 or wider, within the bound.
A program may use at most 128 MiB of HBM per device.

```python
import math
import jax
import jax.numpy as jnp
from jax import lax

C = 384
HEADS = 6
FF = 1536
X = 64
Y = 64
ZS = 8
YB = 8
NB = 8
NOFF = 3


def textured(key):
    subkeys = jax.random.split(key, 4)
    rough = jnp.clip(jax.random.normal(subkeys[0], (X, Y, ZS, C), jnp.float32), -6.0, 6.0)
    token_scale = jnp.exp(jax.random.uniform(subkeys[2], (X, Y, ZS, 1), jnp.float32, math.log(0.3), math.log(3.0)))
    channel_scale = jnp.exp(jax.random.uniform(subkeys[3], (1, 1, 1, C), jnp.float32, math.log(0.3), math.log(3.0)))
    blended = rough
    return (blended * token_scale * channel_scale).astype(jnp.bfloat16)


def drawn_weights(key):
    subkeys = jax.random.split(key, 1)
    drawn = jnp.clip(jax.random.normal(subkeys[0], (C, 3 * C), jnp.float32), -4.0, 4.0) / math.sqrt(C)
    queries = drawn[:, :C]
    keyed = drawn[:, C:2 * C]
    return jnp.concatenate([queries, keyed, drawn[:, 2 * C:]], axis=1).astype(jnp.bfloat16)


def draw_field(key, part):
    key = jax.random.fold_in(key, 5)
    return textured(key)


def draw_win_qkv(key, part):
    key = jax.random.fold_in(key, 21)
    return drawn_weights(key)


def draw_axial_qkv(key, part):
    key = jax.random.fold_in(key, 22)
    return drawn_weights(key)


def draw_pattern(key, part):
    key = jax.random.fold_in(key, 11)
    subkeys = jax.random.split(key, 2)
    starts = jax.random.randint(subkeys[0], (HEADS, 1), 0, NB, jnp.int32)
    dilation = 1 + jax.random.permutation(subkeys[1], HEADS).astype(jnp.int32) % 3
    counter = jnp.arange(NOFF, dtype=jnp.int32)[None, :]
    return ((starts + dilation[:, None] * counter) % NB).astype(jnp.int32)


def steps_of(rng, extent, cuts, low, high):
    def one(axis_at, shards_of):
        draws = jax.random.uniform(jax.random.fold_in(jax.random.fold_in(rng, 6), axis_at), (shards_of,), jnp.float32, low / len(cuts), high / len(cuts))
        return jnp.repeat(jnp.exp(draws), extent[axis_at] // shards_of).reshape((-1,) + (1,) * (len(extent) - axis_at - 1))

    factor_of = one(*cuts[0])
    for cut in cuts[1:]:
        factor_of = factor_of * one(*cut)
    return factor_of


def bell_draw(stream_key, extent, width, most, cuts=(), kind=jnp.bfloat16):
    array = jax.random.normal(stream_key, extent, jnp.float32) * width
    if len(cuts) > 0:
        array = steps_of(stream_key, extent, cuts, -0.22, 0.18) * array
    return jnp.clip(array, min=-most, max=most).astype(kind)


def setup_inputs(seed: int = 0) -> dict:
    key_of = jax.random.split(jax.random.key(seed), 10)
    field = draw_field(jax.random.fold_in(key_of[9], 71), 0)
    cotangent = bell_draw(key_of[1], (X, Y, ZS, C), 1.0, 6.0, ((0, 32), (1, 8)))
    win_qkv = draw_win_qkv(jax.random.fold_in(key_of[9], 71), 0)
    win_out = bell_draw(key_of[3], (C, C), C ** -0.5, 0.3125)
    axial_qkv = draw_axial_qkv(jax.random.fold_in(key_of[9], 71), 0)
    axial_out = bell_draw(key_of[5], (C, C), C ** -0.5, 0.3125)
    mlp_in = bell_draw(key_of[6], (C, FF), C ** -0.5, 0.3125)
    mlp_out = bell_draw(key_of[7], (FF, C), FF ** -0.5, 0.15625)
    pattern = draw_pattern(jax.random.fold_in(key_of[9], 71), 0)
    return dict(field=field, cotangent=cotangent, win_qkv=win_qkv, win_out=win_out, axial_qkv=axial_qkv, axial_out=axial_out, mlp_in=mlp_in, mlp_out=mlp_out, pattern=pattern)


HIGH = lax.Precision.HIGHEST
EPSILON = 1e-06

def normalize(values):
    return values * lax.rsqrt(lax.optimization_barrier(jnp.mean(values * values, axis=-1, keepdims=True)) + EPSILON)

def matmul(left_side, right_side):
    old_shape = left_side.shape
    flattened = left_side.reshape(-1, old_shape[-1])
    product = jnp.dot(flattened, right_side, precision=HIGH, preferred_element_type=jnp.float32)
    return product.reshape(old_shape[:-1] + (right_side.shape[1],))

def flat_coords(count_a, count_b, depth, lift):
    coord_a = jnp.broadcast_to(jnp.arange(count_a, dtype=jnp.int32)[:, None, None] + lift, (count_a, count_b, depth)).reshape(-1)
    coord_b = jnp.broadcast_to(jnp.arange(count_b, dtype=jnp.int32)[None, :, None] + lift, (count_a, count_b, depth)).reshape(-1)
    coord_z = jnp.broadcast_to(jnp.arange(depth, dtype=jnp.int32)[None, None, :], (count_a, count_b, depth)).reshape(-1)
    return (coord_a, coord_b, coord_z)

def window_core(queries, keys_pad, vals_pad, rounded):
    count_a, count_b, depth, features = queries.shape
    pad_a, pad_b = (keys_pad.shape[0], keys_pad.shape[1])
    head_size = features // HEADS
    query_heads = queries.reshape(count_a * count_b * depth, HEADS, head_size)
    key_heads = keys_pad.reshape(pad_a * pad_b * depth, HEADS, head_size)
    val_heads = vals_pad.reshape(pad_a * pad_b * depth, HEADS, head_size)
    scores = jnp.einsum('qhd,khd->hqk', query_heads, key_heads, precision=HIGH, preferred_element_type=jnp.float32) / math.sqrt(head_size)
    query_a, query_b, query_z = flat_coords(count_a, count_b, depth, 2)
    key_a, key_b, key_z = flat_coords(pad_a, pad_b, depth, 0)
    depth_gap = (key_z[None, :] - query_z[:, None]) % depth
    near = (jnp.abs(key_a[None, :] - query_a[:, None]) <= 2) & (jnp.abs(key_b[None, :] - query_b[:, None]) <= 2) & ((depth_gap <= 2) | (depth_gap >= depth - 2))
    scores = jnp.where(near[None], scores, -1e+30)
    weights = jax.nn.softmax(scores, axis=-1)
    if rounded:
        weights = lax.optimization_barrier(weights.astype(jnp.bfloat16)).astype(jnp.float32)
    result = jnp.einsum('hqk,khd->qhd', weights, val_heads, precision=HIGH, preferred_element_type=jnp.float32)
    result = result.reshape(count_a, count_b, depth, features)
    if rounded:
        return result.astype(jnp.bfloat16)
    return result

def axial_core(queries, key_rows, val_rows, pattern, y_start, rounded):
    count_n, count_y, depth, features = queries.shape
    count_k = key_rows.shape[1]
    head_size = features // HEADS
    query_heads = queries.reshape(count_n, count_y, depth, HEADS, head_size)
    key_heads = key_rows.reshape(count_n, count_k, depth, HEADS, head_size)
    val_heads = val_rows.reshape(count_n, count_k, depth, HEADS, head_size)
    scores = jnp.einsum('nyzhd,nkzhd->nzhyk', query_heads, key_heads, precision=HIGH, preferred_element_type=jnp.float32) / math.sqrt(head_size)
    blocks_total = count_k // YB
    query_block = (y_start + jnp.arange(count_y, dtype=jnp.int32)) // YB
    key_block = jnp.arange(count_k, dtype=jnp.int32) // YB
    offsets = (key_block[None, :] - query_block[:, None]) % blocks_total
    allowed = jnp.any(offsets[None, None] == pattern[:, :, None, None], axis=1) | (offsets == 0)[None]
    scores = jnp.where(allowed[None, None], scores, -1e+30)
    weights = jax.nn.softmax(scores, axis=-1)
    if rounded:
        weights = lax.optimization_barrier(weights.astype(jnp.bfloat16)).astype(jnp.float32)
    result = jnp.einsum('nzhyk,nkzhd->nyzhd', weights, val_heads, precision=HIGH, preferred_element_type=jnp.float32)
    result = result.reshape(count_n, count_y, depth, features)
    if rounded:
        return result.astype(jnp.bfloat16)
    return result

def fold_wrap(padded):
    interior_y = padded[:, 2:-2]
    interior_y = interior_y.at[:, :2].add(padded[:, -2:]).at[:, -2:].add(padded[:, :2])
    interior = interior_y[2:-2]
    return interior.at[:2].add(interior_y[-2:]).at[-2:].add(interior_y[:2])

def reference(field, cotangent, win_qkv, win_out, axial_qkv, axial_out, mlp_in, mlp_out, pattern):
    planes = jnp.arange(X, dtype=jnp.int32)
    field_f32 = field.astype(jnp.float32)
    normed1 = normalize(field_f32).astype(jnp.bfloat16)
    triple1 = matmul(normed1, win_qkv).astype(jnp.bfloat16)
    query1 = triple1[..., :C]
    kv_pad = jnp.pad(triple1[..., C:], ((2, 2), (2, 2), (0, 0), (0, 0)), mode='wrap')

    def window_plane(position):
        queries = lax.dynamic_slice_in_dim(query1, position, 1, 0).astype(jnp.float32)
        beside_all = lax.dynamic_slice_in_dim(kv_pad, position, 5, 0).astype(jnp.float32)
        return window_core(queries, beside_all[..., :C], beside_all[..., C:], True)[0]
    attended1 = lax.map(window_plane, planes)
    stream1 = (field_f32 + matmul(attended1, win_out)).astype(jnp.bfloat16)
    stream1_f = stream1.astype(jnp.float32)
    normed2 = normalize(stream1_f).astype(jnp.bfloat16)
    triple2 = matmul(normed2, axial_qkv).astype(jnp.bfloat16)

    def axial_plane(position):
        line_block = lax.dynamic_slice_in_dim(triple2, position, 1, 0).astype(jnp.float32)
        return axial_core(line_block[..., :C], line_block[..., C:2 * C], line_block[..., 2 * C:], pattern, 0, True)[0]
    attended2 = lax.map(axial_plane, planes)
    stream2 = (stream1_f + matmul(attended2, axial_out)).astype(jnp.bfloat16)
    stream2_f = stream2.astype(jnp.float32)
    normed3 = normalize(stream2_f).astype(jnp.bfloat16)
    hidden = jax.nn.gelu(matmul(normed3, mlp_in)).astype(jnp.bfloat16)
    layer_output = (stream2_f + matmul(hidden, mlp_out)).astype(jnp.bfloat16)
    gradient = cotangent.astype(jnp.float32)
    in_f32 = mlp_in.astype(jnp.float32)
    out_f32 = mlp_out.astype(jnp.float32)

    def branch(values):
        return matmul(jax.nn.gelu(matmul(normalize(values), in_f32)), out_f32)

    def mlp_plane(position):
        values = lax.dynamic_slice_in_dim(stream2_f, position, 1, 0)
        upstream = lax.dynamic_slice_in_dim(gradient, position, 1, 0)
        _, pullback = jax.vjp(branch, values)
        return (upstream + pullback(upstream)[0])[0]
    grad2 = lax.map(mlp_plane, planes)
    back2 = matmul(grad2, axial_out.astype(jnp.float32).T)

    def axial_back(position):
        line_block = lax.dynamic_slice_in_dim(triple2, position, 1, 0).astype(jnp.float32)
        upstream = lax.dynamic_slice_in_dim(back2, position, 1, 0)

        def local_axial(first, second, third):
            return axial_core(first, second, third, pattern, 0, False)
        _, pullback = jax.vjp(local_axial, line_block[..., :C], line_block[..., C:2 * C], line_block[..., 2 * C:])
        return jnp.concatenate(pullback(upstream), axis=-1)[0]
    axial_grads = lax.map(axial_back, planes)
    normed_grad2 = matmul(axial_grads, axial_qkv.astype(jnp.float32).T)
    _, pullback = jax.vjp(normalize, stream1_f)
    grad1 = grad2 + pullback(normed_grad2)[0]
    back1 = matmul(grad1, win_out.astype(jnp.float32).T)
    query_f = query1.astype(jnp.float32)
    kv_pad_f = kv_pad.astype(jnp.float32)

    def window_back(carried, position):
        queries = lax.dynamic_slice_in_dim(query_f, position, 1, 0)
        beside_all = lax.dynamic_slice_in_dim(kv_pad_f, position, 5, 0)
        upstream = lax.dynamic_slice_in_dim(back1, position, 1, 0)

        def local_window(first, second, third):
            return window_core(first, second, third, False)
        _, pull_window = jax.vjp(local_window, queries, beside_all[..., :C], beside_all[..., C:])
        grad_query, grad_keys, grad_values = pull_window(upstream)
        joined = jnp.concatenate([grad_keys, grad_values], axis=-1)
        updated = lax.dynamic_slice_in_dim(carried, position, 5, 0) + joined
        return (lax.dynamic_update_slice_in_dim(carried, updated, position, 0), grad_query[0])
    zeroed = jnp.zeros((X + 4, Y + 4, ZS, 2 * C), jnp.float32)
    pad_grad, grad_query1 = lax.scan(window_back, zeroed, planes)
    window_grads = jnp.concatenate([grad_query1, fold_wrap(pad_grad)], axis=-1)
    normed_grad1 = matmul(window_grads, win_qkv.astype(jnp.float32).T)
    _, pullback = jax.vjp(normalize, field_f32)
    field_grad = grad1 + pullback(normed_grad1)[0]
    return (layer_output, field_grad)
```

```python
import functools

import jax
import jax.numpy as jnp
from jax import lax
from jax.experimental import pallas as pl
from jax.experimental.pallas import tpu as pltpu
from jax.sharding import PartitionSpec as P

F32 = jnp.float32
BF16 = jnp.bfloat16
C = 384
FF = 1536
PAIRS = 3
TOK = 128
KEYS = 576
EPSILON = 1e-06
MASKED = -1e30
MESH = pl.DeviceIdType.MESH

SIDES = [(1, 1), (-1, -1), (1, -1), (-1, 1), (0, 1), (0, -1), (1, 0), (-1, 0)]
PEERS = [3, 5, 2, 6, 4, 1, 7]


def nn(a, b):
    return lax.dot_general(a, b, (((1,), (0,)), ((), ())), preferred_element_type=F32)


def nt(a, b):
    return lax.dot_general(a, b, (((1,), (1,)), ((), ())), preferred_element_type=F32)


def inverse_rms(v):
    return lax.rsqrt(jnp.sum(v * v, axis=-1, keepdims=True) * (1.0 / C) + EPSILON)


def norm_back(v, r, upstream):
    inner = jnp.sum(v * upstream, axis=-1, keepdims=True) * (1.0 / C)
    return r * upstream - v * (r * r * r * inner)


def iota(shape, dim):
    return lax.broadcasted_iota(jnp.int32, shape, dim)


def stacked(pair):
    first = iota(pair.shape, 1) < 64
    upper = jnp.where(first, pair, 0.0)
    return jnp.concatenate([upper, pair - upper], axis=0).astype(BF16)


def diagonal(both):
    return jnp.concatenate([both[:64, :128], both[64:, 128:]], axis=0)


def softmax_keys(scores):
    e = jnp.exp(scores - jnp.max(scores, axis=0, keepdims=True))
    return e * (1.0 / jnp.sum(e, axis=0, keepdims=True))


def lanes(p, base=0):
    return slice(base + 128 * p, base + 128 * (p + 1))


def kernel(
    nx,
    ny,
    field,
    cot,
    win_qkv_h,
    win_out_h,
    axial_qkv_h,
    axial_out_h,
    mlp_in_h,
    mlp_out_h,
    pattern_h,
    out_ref,
    grad_ref,
    win_qkv,
    win_out,
    axial_qkv,
    axial_out,
    mlp_in,
    mlp_out,
    pattern,
    rim,
    cot_own,
    cot_send,
    cot_recv,
    s1_send,
    s1_recv,
    lo_send,
    lo_recv,
    g1_send,
    g1_recv,
    dn_send,
    rim_big,
    rim_small,
    weights1,
    kv1,
    kt1,
    bias1,
    q1,
    local_sem,
    halo_send,
    halo_recv,
    a2a_send,
    a2a_recv,
    push_send,
    push_recv,
):
    gx = lax.axis_index("gx")
    gy = lax.axis_index("gy")

    def step(index, by, size):
        moved = index + by
        if by > 0:
            return jnp.where(moved >= size, moved - size, moved)
        return jnp.where(moved < 0, moved + size, moved) if by else index

    def at(dx, dy):
        return (step(gx, dx, nx), step(gy, dy, ny))

    barrier = pltpu.get_barrier_semaphore()
    greeted = SIDES + [(0, d) for d in range(2, ny - 1)]
    for dx, dy in greeted:
        pl.semaphore_signal(barrier, inc=1, device_id=at(dx, dy), device_id_type=MESH)

    local = []
    for index, (src, dst) in enumerate(
        [
            (field, rim.at[2:4, 1:5]),
            (cot, cot_own),
            (win_qkv_h, win_qkv),
            (win_out_h, win_out),
            (axial_qkv_h, axial_qkv),
            (axial_out_h, axial_out),
            (mlp_in_h, mlp_in),
            (mlp_out_h, mlp_out),
            (pattern_h, pattern),
        ]
    ):
        copy = pltpu.make_async_copy(src, dst, local_sem.at[index])
        copy.start()
        local.append(copy)
    local[0].wait()
    pl.semaphore_wait(barrier, len(greeted))

    own_y = {0: slice(1, 5), 1: slice(4, 5), -1: slice(1, 2)}
    land_x = {1: slice(0, 2), 0: slice(2, 4), -1: slice(4, 6)}
    land_y = {1: slice(0, 1), 0: slice(1, 5), -1: slice(5, 6)}
    halo = []
    for index, (dx, dy) in enumerate(SIDES):
        copy = pltpu.make_async_remote_copy(
            src_ref=rim.at[2:4, own_y[dy]],
            dst_ref=rim.at[land_x[dx], land_y[dy]],
            send_sem=halo_send.at[index],
            recv_sem=halo_recv.at[index],
            device_id=at(dx, dy),
            device_id_type=MESH,
        )
        copy.start()
        halo.append(copy)

    def exchange(send, recv, group):
        copies = []
        for d in PEERS:
            peer = step(gy, d, ny)
            copy = pltpu.make_async_remote_copy(
                src_ref=send.at[peer],
                dst_ref=recv.at[gy],
                send_sem=a2a_send.at[group, d],
                recv_sem=a2a_recv.at[group, d],
                device_id=(gx, peer),
                device_id_type=MESH,
            )
            copy.start()
            copies.append(copy)
        recv[pl.ds(gy, 1)] = send[pl.ds(gy, 1)]
        return copies

    def arrived(send, recv, group):
        for d in PEERS:
            source = step(gy, -d, ny)
            pltpu.make_async_remote_copy(
                src_ref=send.at[source],
                dst_ref=recv.at[source],
                send_sem=a2a_send.at[group, d],
                recv_sem=a2a_recv.at[group, d],
                device_id=(gx, source),
                device_id_type=MESH,
            ).wait_recv()
        return recv[...].reshape(TOK, C)

    row, col = iota((TOK, TOK), 0), iota((TOK, TOK), 1)
    to_zxy = jnp.where(row == (col & 7) * 16 + (col >> 3), 1.0, 0.0).astype(BF16)
    to_xyz = jnp.where(col == (row & 7) * 16 + (row >> 3), 1.0, 0.0).astype(BF16)
    eye = jnp.where(row == col, 1.0, 0.0).astype(BF16)

    local[1].wait()
    cot_send[...] = nn(to_zxy, cot_own[...].reshape(TOK, C)).astype(BF16).reshape(8, 16, C)
    cot_copies = exchange(cot_send, cot_recv, 0)

    key, query = iota((96, TOK), 0), iota((96, TOK), 1)
    gap_y = (key >> 3) - 2 - (query & 7)
    gap_z = ((key & 7) - (query >> 4) + 2) & 7
    near = (jnp.abs(gap_y) <= 2) & (gap_z <= 4)
    second = (query >> 3) & 1
    plane_bias = jnp.where(near, 0.0, MASKED)
    for plane in range(6):
        block = plane_bias
        if plane == 0:
            block = jnp.where(second == 0, plane_bias, MASKED)
        if plane == 5:
            block = jnp.where(second == 1, plane_bias, MASKED)
        bias1[96 * plane : 96 * (plane + 1), :] = block

    field_own = rim[2:4, 1:5].reshape(TOK, C)
    field_f = field_own.astype(F32)
    r1 = inverse_rms(field_f)
    normed1_zxy = nn(to_zxy, (field_f * r1).astype(BF16)).astype(BF16)
    field_zxy = nn(to_zxy, field_own)
    local[2].wait()
    query1 = nn(normed1_zxy, win_qkv[:, 0:C]).astype(BF16).astype(F32) * 0.125
    for p in range(PAIRS):
        q1[p] = stacked(query1[:, lanes(p)])
    for copy in halo:
        copy.wait_recv()
    all_f = rim[...].reshape(KEYS, C).astype(F32)
    normed_all = (all_f * inverse_rms(all_f)).astype(BF16)
    kv1[...] = nn(normed_all, win_qkv[:, C : 3 * C]).astype(BF16)
    bias_both = jnp.concatenate([bias1[...], bias1[...]], axis=1)
    attended = []
    for p in range(PAIRS):
        weights = softmax_keys(nt(kv1[:, lanes(p)], q1[p]) + bias_both).astype(BF16)
        weights1[p] = weights
        vt = nt(eye, kv1[:, lanes(p, C)]).astype(BF16)
        attended.append(nt(eye, diagonal(nn(vt, weights)).astype(BF16)))
    attended = jnp.concatenate(attended, axis=1).astype(BF16)
    local[3].wait()
    s1_send[...] = (field_zxy + nn(attended, win_out[...])).astype(BF16).reshape(8, 16, C)
    s1_copies = exchange(s1_send, s1_recv, 1)

    for p in range(PAIRS):
        kt1[p] = nt(eye, kv1[:, lanes(p)]).astype(BF16)
    for copy in local[4:]:
        copy.wait()
    off = ((row >> 4) - (col >> 4)) & 7
    same_line = ((row ^ col) & 8) == 0
    bias2 = []
    for head in range(2 * PAIRS):
        hit = off == 0
        for j in range(3):
            hit = hit | (off == pattern[j, head])
        bias2.append(jnp.where(hit & same_line, 0.0, MASKED))

    gradient_bf = arrived(cot_send, cot_recv, 0)
    gradient = gradient_bf.astype(F32)
    d_hidden = [
        nt(gradient_bf, mlp_out[512 * c : 512 * (c + 1), :]) for c in range(FF // 512)
    ]
    stream1 = arrived(s1_send, s1_recv, 1).astype(F32)
    r2 = inverse_rms(stream1)
    triple2 = nn((stream1 * r2).astype(BF16), axial_qkv[...]).astype(BF16)
    query2 = triple2[:, 0:C].astype(F32) * 0.125
    q2 = [stacked(query2[:, lanes(p)]) for p in range(PAIRS)]
    weights2 = []
    attended2 = []
    for p in range(PAIRS):
        pair_bias = jnp.concatenate([bias2[2 * p], bias2[2 * p + 1]], axis=1)
        weights = softmax_keys(nt(triple2[:, lanes(p, C)], q2[p]) + pair_bias).astype(BF16)
        weights2.append(weights)
        vt = nt(eye, triple2[:, lanes(p, 2 * C)]).astype(BF16)
        attended2.append(nt(eye, diagonal(nn(vt, weights)).astype(BF16)))
    attended2 = jnp.concatenate(attended2, axis=1).astype(BF16)
    stream2 = (stream1 + nn(attended2, axial_out[...])).astype(BF16).astype(F32)

    r3 = inverse_rms(stream2)
    normed3 = (stream2 * r3).astype(BF16)
    hidden = []
    back = None
    for c in range(FF // 512):
        part = slice(512 * c, 512 * (c + 1))
        a = nn(normed3, mlp_in[:, part])
        square = a * a
        t = jnp.tanh(0.7978845608028654 * (a + 0.044715 * (a * square)))
        half = 0.5 * (1.0 + t)
        hidden.append((a * half).astype(BF16))
        slope = half + (0.5 * a) * (1.0 - t * t) * (
            0.7978845608028654 + (3 * 0.044715 * 0.7978845608028654) * square
        )
        term = nt((d_hidden[c] * slope).astype(BF16), mlp_in[:, part])
        back = term if back is None else back + term
    grad2 = gradient + norm_back(stream2, r3, back)

    back2 = nt(grad2.astype(BF16), axial_out[...])
    d_query, d_key, d_value = [], [], []
    for p in range(PAIRS):
        upstream = stacked(back2[:, lanes(p)])
        d_weights = nt(triple2[:, lanes(p, 2 * C)], upstream)
        weights = weights2[p].astype(F32)
        product = weights * d_weights
        delta = jnp.sum(product, axis=0, keepdims=True)
        d_scores = (product - weights * delta).astype(BF16)
        kt = nt(eye, triple2[:, lanes(p, C)]).astype(BF16)
        dqt = (diagonal(nn(kt, d_scores)) * 0.125).astype(BF16)
        d_query.append(nt(eye, dqt))
        d_key.append(nn(d_scores, q2[p]))
        d_value.append(nn(weights2[p], upstream))
    d_triple2 = jnp.concatenate(d_query + d_key + d_value, axis=1).astype(BF16)
    grad1 = grad2 + norm_back(stream1, r2, nt(d_triple2, axial_qkv[...]))
    g1_send[...] = grad1.astype(BF16).reshape(8, 16, C)
    g1_copies = exchange(g1_send, g1_recv, 3)

    hidden_out = nn(jnp.concatenate(hidden, axis=1), mlp_out[...])
    lo_send[...] = (stream2 + hidden_out).astype(BF16).reshape(8, 16, C)
    lo_copies = exchange(lo_send, lo_recv, 2)

    grad1_bf = arrived(g1_send, g1_recv, 3)
    back1 = nt(grad1_bf, win_out[...])
    scores_back, d_key, d_value = [], [], []
    for p in range(PAIRS):
        upstream = stacked(back1[:, lanes(p)])
        d_weights = nt(kv1[:, lanes(p, C)], upstream)
        weights = weights1[p].astype(F32)
        product = weights * d_weights
        delta = jnp.sum(product, axis=0, keepdims=True)
        d_scores = (product - weights * delta).astype(BF16)
        scores_back.append(d_scores)
        d_key.append(nn(d_scores, q1[p]).astype(BF16))
        d_value.append(nn(weights1[p], upstream).astype(BF16))
    d_kv = jnp.concatenate(d_key + d_value, axis=1)
    back_x = {-1: slice(0, 2), 0: slice(2, 4), 1: slice(4, 6)}
    back_y = {-1: slice(0, 1), 0: slice(1, 5), 1: slice(5, 6)}
    push = []
    for side in (1, -1, 0):
        rows = slice(192 * (side + 1), 192 * (side + 2))
        dn_block = nt(d_kv[rows], win_qkv[:, C : 3 * C]).reshape(2, 6, 16, C)
        dn_send[back_x[side]] = dn_block.astype(BF16)
        for index, (dx, dy) in enumerate(SIDES):
            if dx != side:
                continue
            dst = rim_big.at[index - 6] if dy == 0 else rim_small.at[index]
            copy = pltpu.make_async_remote_copy(
                src_ref=dn_send.at[back_x[dx], back_y[dy]],
                dst_ref=dst,
                send_sem=push_send.at[index],
                recv_sem=push_recv.at[index],
                device_id=at(dx, dy),
                device_id_type=MESH,
            )
            copy.start()
            push.append(copy)

    d_query = [
        (diagonal(nn(kt1[p], scores_back[p])) * 0.125).astype(BF16) for p in range(PAIRS)
    ]
    d_query = nt(to_xyz, jnp.concatenate(d_query, axis=0)).astype(BF16)
    d_normed = dn_block[:, 1:5].reshape(TOK, C) + nt(d_query, win_qkv[:, 0:C])
    grad1_xyz = nn(to_xyz, grad1_bf)
    out_ref[...] = nn(to_xyz, arrived(lo_send, lo_recv, 2)).astype(BF16)
    for copy in push:
        copy.wait_recv()
    d_normed = d_normed + (rim_big[0].astype(F32) + rim_big[1].astype(F32)).reshape(TOK, C)
    below = [i for i, (_, dy) in enumerate(SIDES) if dy == 1]
    above = [i for i, (_, dy) in enumerate(SIDES) if dy == -1]
    first = sum(rim_small[i].astype(F32) for i in below).reshape(2, 16, C)
    last = sum(rim_small[i].astype(F32) for i in above).reshape(2, 16, C)
    none = jnp.zeros((32, C), F32)
    edges = jnp.concatenate([first[0], none, last[0], first[1], none, last[1]], axis=0)
    field_f = rim[2:4, 1:5].reshape(TOK, C).astype(F32)
    grad_ref[...] = grad1_xyz + norm_back(field_f, inverse_rms(field_f), d_normed + edges)

    for copy in halo + cot_copies + s1_copies + lo_copies + g1_copies + push:
        copy.wait_send()


def shards(nx, ny, field, cotangent, *rest):
    block = (2, 4, 16, C)
    tiles = (8, 16, C)
    vmem = pltpu.VMEM
    dma = pltpu.SemaphoreType.DMA
    weights, pattern = rest[:6], rest[6]
    in_hbm = pl.BlockSpec(memory_space=pltpu.HBM)
    in_vmem = pl.BlockSpec(memory_space=pltpu.VMEM)
    layer_output, field_grad = pl.pallas_call(
        functools.partial(kernel, nx, ny),
        out_shape=(
            jax.ShapeDtypeStruct((TOK, C), BF16),
            jax.ShapeDtypeStruct((TOK, C), F32),
        ),
        in_specs=[in_hbm] * 9,
        out_specs=(in_vmem, in_vmem),
        scratch_shapes=[vmem(w.shape, BF16) for w in weights]
        + [pltpu.SMEM((3, 6), jnp.int32), vmem((6, 6, 16, C), BF16)]
        + [vmem(tiles, BF16)] * 9
        + [
            vmem((6, 6, 16, C), BF16),
            vmem((2,) + block, BF16),
            vmem((6, 2, 1, 16, C), BF16),
            vmem((PAIRS, KEYS, 256), BF16),
            vmem((KEYS, 2 * C), BF16),
            vmem((PAIRS, TOK, KEYS), BF16),
            vmem((KEYS, TOK), F32),
            vmem((PAIRS, 256, TOK), BF16),
            dma((9,)),
            dma((8,)),
            dma((8,)),
            dma((4, 8)),
            dma((4, 8)),
            dma((8,)),
            dma((8,)),
        ],
        compiler_params=pltpu.CompilerParams(
            collective_id=0, has_side_effects=True, vmem_limit_bytes=60 * 1024 * 1024
        ),
    )(field.reshape(block), cotangent.reshape(tiles), *weights, pattern.T)
    return layer_output.reshape(field.shape), field_grad.reshape(field.shape)


def solution(mesh):
    split = P("gx", "gy", None, None)
    return jax.shard_map(
        functools.partial(shards, mesh.shape["gx"], mesh.shape["gy"]),
        mesh=mesh,
        in_specs=(split, split) + (P(),) * 7,
        out_specs=(split, split),
        check_vma=False,
    )
```

```python
import functools

import jax
import jax.numpy as jnp
from jax import lax
from jax.experimental import pallas as pl
from jax.experimental.pallas import tpu as pltpu
from jax.sharding import PartitionSpec as P

F32 = jnp.float32
BF16 = jnp.bfloat16
C = 384
FF = 1536
PAIRS = 3
TOK = 128
KEYS = 576
OWN, AROUND, EARLY, EDGES = slice(0, 128), slice(128, 384), slice(0, 384), slice(384, 576)
EPSILON = 1e-06
MASKED = -1e30
MESH = pl.DeviceIdType.MESH

SIDES = [(1, 1), (-1, -1), (1, -1), (-1, 1), (0, 1), (0, -1), (1, 0), (-1, 0)]
PEERS = [2, 6, 1, 3, 5, 7, 0, 4]


def nn(a, b):
    return lax.dot_general(a, b, (((1,), (0,)), ((), ())), preferred_element_type=F32)


def nt(a, b):
    return lax.dot_general(a, b, (((1,), (1,)), ((), ())), preferred_element_type=F32)


def inverse_rms(v):
    return lax.rsqrt(jnp.sum(v * v, axis=-1, keepdims=True) * (1.0 / C) + EPSILON)


def norm_back(v, r, upstream):
    inner = jnp.sum(v * upstream, axis=-1, keepdims=True) * (1.0 / C)
    return r * upstream - v * (r * r * r * inner)


def iota(shape, dim):
    return lax.broadcasted_iota(jnp.int32, shape, dim)


def stacked(pair):
    first = iota(pair.shape, 1) < 64
    upper = jnp.where(first, pair, 0.0)
    return jnp.concatenate([upper, pair - upper], axis=0).astype(BF16)


def diagonal(both):
    return jnp.concatenate([both[:64, :128], both[64:, 128:]], axis=0)


def abreast(both):
    return jnp.concatenate([both[:TOK], both[TOK:]], axis=1)


def lanes(p, base=0):
    return slice(base + 128 * p, base + 128 * (p + 1))


def kernel(
    nx,
    ny,
    field,
    cot,
    win_qkv_h,
    win_out_h,
    axial_qkv_h,
    axial_out_h,
    mlp_in_h,
    mlp_out_h,
    pattern_h,
    out_ref,
    grad_ref,
    win_qkv,
    win_out,
    axial_qkv,
    axial_out,
    mlp_in,
    mlp_out,
    pattern,
    own,
    sides,
    edges,
    cot_own,
    cot_send,
    cot_recv,
    s1_send,
    s1_recv,
    lo_send,
    lo_recv,
    g1_send,
    g1_recv,
    dn_send,
    dn_recv,
    weights1,
    kv1,
    kt1,
    vt1,
    ot1,
    scores1,
    bias1,
    q1,
    local_sem,
    halo_send,
    halo_recv,
    a2a_send,
    a2a_recv,
    push_send,
    push_recv,
):
    gx = lax.axis_index("gx")
    gy = lax.axis_index("gy")

    partner = gx + 2 - 4 * ((gx >> 1) & 1)

    def step(index, by, size):
        moved = index + by
        if by > 0:
            return jnp.where(moved >= size, moved - size, moved)
        return jnp.where(moved < 0, moved + size, moved) if by else index

    def at(dx, dy):
        return (step(gx, dx, nx), step(gy, dy, ny))

    barrier = pltpu.get_barrier_semaphore()
    greeted = [at(dx, dy) for dx, dy in SIDES] + [(partner, step(gy, d, ny)) for d in PEERS]
    for device in greeted:
        pl.semaphore_signal(barrier, inc=1, device_id=device, device_id_type=MESH)

    local = []
    for index, (src, dst) in enumerate(
        [
            (field, own),
            (cot, cot_own),
            (win_qkv_h, win_qkv),
            (win_out_h, win_out),
            (axial_qkv_h, axial_qkv),
            (axial_out_h, axial_out),
            (mlp_in_h, mlp_in),
            (mlp_out_h, mlp_out),
            (pattern_h, pattern),
        ]
    ):
        copy = pltpu.make_async_copy(src, dst, local_sem.at[index])
        copy.start()
        local.append(copy)
    local[0].wait()
    pl.semaphore_wait(barrier, len(greeted))

    own_y = {0: slice(0, 4), 1: slice(3, 4), -1: slice(0, 1)}
    halo = []
    for index, (dx, dy) in enumerate(SIDES):
        copy = pltpu.make_async_remote_copy(
            src_ref=own.at[:, own_y[dy]],
            dst_ref=sides.at[index - 6] if dy == 0 else edges.at[index],
            send_sem=halo_send.at[index],
            recv_sem=halo_recv.at[index],
            device_id=at(dx, dy),
            device_id_type=MESH,
        )
        copy.start()
        halo.append(copy)

    def exchange(send, recv, group):
        copies = []
        for d in PEERS:
            peer = step(gy, d, ny)
            copy = pltpu.make_async_remote_copy(
                src_ref=send.at[peer],
                dst_ref=recv.at[gy],
                send_sem=a2a_send.at[group, d],
                recv_sem=a2a_recv.at[group, d],
                device_id=(partner, peer),
                device_id_type=MESH,
            )
            copy.start()
            copies.append(copy)
        return copies

    def arrived(send, recv, group):
        for d in PEERS:
            source = step(gy, -d, ny)
            pltpu.make_async_remote_copy(
                src_ref=send.at[source],
                dst_ref=recv.at[source],
                send_sem=a2a_send.at[group, d],
                recv_sem=a2a_recv.at[group, d],
                device_id=(partner, source),
                device_id_type=MESH,
            ).wait_recv()
        return recv[...].reshape(TOK, C)

    row, col = iota((TOK, TOK), 0), iota((TOK, TOK), 1)
    to_zxy = jnp.where(row == (col & 7) * 16 + (col >> 3), 1.0, 0.0).astype(BF16)
    to_xyz = jnp.where(col == (row & 7) * 16 + (row >> 3), 1.0, 0.0).astype(BF16)
    eye = jnp.where(row == col, 1.0, 0.0).astype(BF16)

    local[1].wait()
    cot_send[...] = nn(to_zxy, cot_own[...].reshape(TOK, C)).astype(BF16).reshape(8, 16, C)

    def near(rows, bits, x_base, y_base):
        key, query = iota((rows, TOK), 0), iota((rows, TOK), 1)
        gap_x = (key >> (3 + bits)) + x_base - ((query >> 3) & 1)
        gap_y = ((key >> 3) & ((1 << bits) - 1)) + y_base - (query & 7)
        gap_z = ((key & 7) - (query >> 4) + 2) & 7
        inside = (jnp.abs(gap_x) <= 2) & (jnp.abs(gap_y) <= 2) & (gap_z <= 4)
        return jnp.where(inside, 0.0, MASKED)

    bias1[OWN, :] = near(TOK, 3, 0, 0)
    for index, (dx, dy) in enumerate(SIDES):
        if dy == 0:
            start = 128 * (index - 5)
            bias1[start : start + 128, :] = near(128, 3, -2 * dx, 0)
        else:
            start = 384 + 32 * index
            bias1[start : start + 32, :] = near(32, 1, -2 * dx, -2 if dy == 1 else 8)

    def window_scores(part, tokens):
        values = tokens.astype(F32)
        normed = (values * inverse_rms(values)).astype(BF16)
        kv = nn(normed, win_qkv[:, C : 3 * C]).astype(BF16)
        kv1[part] = kv
        bias = jnp.concatenate([bias1[part, :], bias1[part, :]], axis=1)
        for p in range(PAIRS):
            scores1[p, part] = nt(kv[:, lanes(p)], q1[p]) + bias
            vt1[p, :, part] = nt(eye, kv[:, lanes(p, C)]).astype(BF16)
        return normed

    field_own = own[...].reshape(TOK, C)
    field_zxy = nn(to_zxy, field_own)
    normed1_zxy = (field_zxy * inverse_rms(field_zxy)).astype(BF16)
    local[2].wait()
    query1 = nn(normed1_zxy, win_qkv[:, 0:C]).astype(BF16).astype(F32) * 0.125
    for p in range(PAIRS):
        q1[p] = stacked(query1[:, lanes(p)])
    window_scores(OWN, field_own)
    for copy in halo[6:]:
        copy.wait_recv()
    window_scores(AROUND, sides[...].reshape(256, C))
    tops, sums, outs = [], [], []
    for p in range(PAIRS):
        scores = scores1[p, EARLY]
        tops.append(jnp.max(scores, axis=0, keepdims=True))
        e = jnp.exp(scores - tops[p])
        scores1[p, EARLY] = e
        sums.append(jnp.sum(e, axis=0, keepdims=True))
        outs.append(diagonal(nn(vt1[p, :, EARLY], e.astype(BF16))))
    for copy in halo[:6]:
        copy.wait_recv()
    cot_copies = exchange(cot_send, cot_recv, 0)
    window_scores(EDGES, edges[...].reshape(192, C))
    attended, early_scale = [], []
    for p in range(PAIRS):
        scores = scores1[p, EDGES]
        top = jnp.maximum(tops[p], jnp.max(scores, axis=0, keepdims=True))
        e = jnp.exp(scores - top)
        shrink = jnp.exp(tops[p] - top)
        scale = 1.0 / (shrink * sums[p] + jnp.sum(e, axis=0, keepdims=True))
        weights = (e * scale).astype(BF16)
        weights1[p, EDGES] = weights
        early_scale.append(shrink * scale)
        early = jnp.concatenate(
            [
                outs[p][:64] * early_scale[p][:, :TOK],
                outs[p][64:] * early_scale[p][:, TOK:],
            ],
            axis=0,
        )
        ot = early + diagonal(nn(vt1[p, :, EDGES], weights))
        ot1[p] = ot
        attended.append(nt(eye, ot.astype(BF16)))
    attended = jnp.concatenate(attended, axis=1).astype(BF16)
    local[3].wait()
    s1_send[...] = (field_zxy + nn(attended, win_out[...])).astype(BF16).reshape(8, 16, C)
    s1_copies = exchange(s1_send, s1_recv, 1)

    for p in range(PAIRS):
        weights1[p, EARLY] = (scores1[p, EARLY] * early_scale[p]).astype(BF16)
        kt1[p] = nt(eye, kv1[:, lanes(p)]).astype(BF16)
    for copy in local[4:]:
        copy.wait()
    off = ((col >> 4) - (row >> 4)) & 7
    same_line = ((row ^ col) & 8) == 0
    bias2 = []
    for head in range(2 * PAIRS):
        hit = off == 0
        for j in range(3):
            hit = hit | (off == pattern[j, head])
        bias2.append(jnp.where(hit & same_line, 0.0, MASKED))

    gradient_bf = arrived(cot_send, cot_recv, 0)
    gradient = gradient_bf.astype(F32)
    d_hidden = [
        nt(gradient_bf, mlp_out[512 * c : 512 * (c + 1), :]) for c in range(FF // 512)
    ]
    stream1 = arrived(s1_send, s1_recv, 1).astype(F32)
    r2 = inverse_rms(stream1)
    triple2 = nn((stream1 * r2).astype(BF16), axial_qkv[...]).astype(BF16)
    query2 = triple2[:, 0:C].astype(F32) * 0.125
    q2 = [stacked(query2[:, lanes(p)]) for p in range(PAIRS)]
    weights2 = []
    attended2 = []
    for p in range(PAIRS):
        pair_bias = jnp.concatenate([bias2[2 * p], bias2[2 * p + 1]], axis=0)
        scores = nt(q2[p], triple2[:, lanes(p, C)]) + pair_bias
        e = jnp.exp(scores - jnp.max(scores, axis=1, keepdims=True))
        weights = (e * (1.0 / jnp.sum(e, axis=1, keepdims=True))).astype(BF16)
        weights2.append(weights)
        values = stacked(triple2[:, lanes(p, 2 * C)].astype(F32))
        attended2.append(nn(abreast(weights), values))
    attended2 = jnp.concatenate(attended2, axis=1).astype(BF16)
    stream2 = (stream1 + nn(attended2, axial_out[...])).astype(BF16).astype(F32)

    r3 = inverse_rms(stream2)
    normed3 = (stream2 * r3).astype(BF16)
    hidden = []
    back = None
    for c in range(FF // 512):
        part = slice(512 * c, 512 * (c + 1))
        a = nn(normed3, mlp_in[:, part])
        square = a * a
        t = jnp.tanh(0.7978845608028654 * (a + 0.044715 * (a * square)))
        half = 0.5 * (1.0 + t)
        hidden.append((a * half).astype(BF16))
        slope = half + (0.5 * a) * (1.0 - t * t) * (
            0.7978845608028654 + (3 * 0.044715 * 0.7978845608028654) * square
        )
        term = nt((d_hidden[c] * slope).astype(BF16), mlp_in[:, part])
        back = term if back is None else back + term
    grad2 = gradient + norm_back(stream2, r3, back)

    back2 = nt(grad2.astype(BF16), axial_out[...])
    d_query, d_key, d_value = [], [], []
    for p in range(PAIRS):
        upstream = stacked(back2[:, lanes(p)])
        keys, values = triple2[:, lanes(p, C)], triple2[:, lanes(p, 2 * C)]
        weights = weights2[p].astype(F32)
        d_weights = nt(upstream, values)
        delta = jnp.sum(weights * d_weights, axis=1, keepdims=True)
        d_scores = (weights * (d_weights - delta)).astype(BF16)
        d_query.append(nn(abreast(d_scores), stacked(keys.astype(F32))) * 0.125)
        weights_t = nt(eye, weights2[p])
        d_weights = nt(values, upstream)
        delta = jnp.sum(weights_t * d_weights, axis=0, keepdims=True)
        d_scores = (weights_t * (d_weights - delta)).astype(BF16)
        d_key.append(nn(d_scores, q2[p]))
        d_value.append(nn(weights_t.astype(BF16), upstream))
    d_triple2 = jnp.concatenate(d_query + d_key + d_value, axis=1).astype(BF16)
    grad1 = grad2 + norm_back(stream1, r2, nt(d_triple2, axial_qkv[...]))
    g1_send[...] = grad1.astype(BF16).reshape(8, 16, C)
    g1_copies = exchange(g1_send, g1_recv, 3)

    hidden_out = nn(jnp.concatenate(hidden, axis=1), mlp_out[...])
    lo_send[...] = (stream2 + hidden_out).astype(BF16).reshape(8, 16, C)
    lo_copies = exchange(lo_send, lo_recv, 2)

    grad1_bf = arrived(g1_send, g1_recv, 3)
    back1 = nt(grad1_bf, win_out[...])
    back1_t = nt(win_out[...], grad1_bf).astype(BF16).astype(F32)
    upstream, delta = [], []
    for p in range(PAIRS):
        upstream.append(stacked(back1[:, lanes(p)]))
        product = ot1[p] * back1_t[lanes(p)]
        halves = [jnp.sum(product[h : h + 64], axis=0, keepdims=True) for h in (0, 64)]
        delta.append(jnp.concatenate(halves, axis=1))

    def window_back(part):
        d_scores, d_key, d_value = [], [], []
        for p in range(PAIRS):
            weights = weights1[p, part]
            d_weights = nt(kv1[part, lanes(p, C)], upstream[p])
            d_scores.append((weights.astype(F32) * (d_weights - delta[p])).astype(BF16))
            d_key.append(nn(d_scores[p], q1[p]).astype(BF16))
            d_value.append(nn(weights, upstream[p]).astype(BF16))
        d_kv = jnp.concatenate(d_key + d_value, axis=1)
        return d_scores, nt(d_kv, win_qkv[:, C : 3 * C])

    push = []

    def send_back(index):
        dx, dy = SIDES[index]
        if dy == 0:
            rows = slice(8 * (index - 6), 8 * (index - 5))
        else:
            rows = slice(16 + 2 * index, 18 + 2 * index)
        copy = pltpu.make_async_remote_copy(
            src_ref=dn_send.at[rows],
            dst_ref=dn_recv.at[rows],
            send_sem=push_send.at[index],
            recv_sem=push_recv.at[index],
            device_id=at(-dx, -dy),
            device_id_type=MESH,
        )
        copy.start()
        push.append(copy)

    scores_edges, dn = window_back(EDGES)
    dn_send[16:28] = dn.astype(BF16).reshape(12, 16, C)
    for index in range(6):
        send_back(index)
    scores_around, dn = window_back(AROUND)
    dn_send[0:16] = dn.astype(BF16).reshape(16, 16, C)
    for index in range(6, 8):
        send_back(index)

    scores_own, d_normed = window_back(OWN)
    d_query = []
    for p in range(PAIRS):
        both = nn(kt1[p, :, EDGES], scores_edges[p]) + nn(kt1[p, :, AROUND], scores_around[p])
        both = both + nn(kt1[p, :, OWN], scores_own[p])
        d_query.append((diagonal(both) * 0.125).astype(BF16))
    d_query = nt(to_xyz, jnp.concatenate(d_query, axis=0)).astype(BF16)
    d_normed = d_normed + nt(d_query, win_qkv[:, 0:C])
    grad1_xyz = nn(to_xyz, grad1_bf)
    out_ref[...] = nn(to_xyz, arrived(lo_send, lo_recv, 2)).astype(BF16)
    for copy in push:
        copy.wait_recv()
    d_normed = d_normed + (dn_recv[0:8].astype(F32) + dn_recv[8:16].astype(F32)).reshape(TOK, C)
    first, last = [
        sum(
            dn_recv[16 + 2 * i : 18 + 2 * i].astype(F32)
            for i, (_, dy) in enumerate(SIDES)
            if dy == way
        )
        for way in (-1, 1)
    ]
    none = jnp.zeros((32, C), F32)
    rims = jnp.concatenate([first[0], none, last[0], first[1], none, last[1]], axis=0)
    field_f = own[...].reshape(TOK, C).astype(F32)
    grad_ref[...] = grad1_xyz + norm_back(field_f, inverse_rms(field_f), d_normed + rims)

    for copy in halo + cot_copies + s1_copies + lo_copies + g1_copies + push:
        copy.wait_send()


def store(out_ref, grad_ref, out_hbm, grad_hbm, sem):
    copies = [
        pltpu.make_async_copy(grad_ref, grad_hbm, sem.at[0]),
        pltpu.make_async_copy(out_ref, out_hbm, sem.at[1]),
    ]
    for copy in copies:
        copy.start()
    for copy in copies:
        copy.wait()


def shards(nx, ny, field, cotangent, *rest):
    block = (2, 4, 16, C)
    tiles = (8, 16, C)
    vmem = pltpu.VMEM
    dma = pltpu.SemaphoreType.DMA
    weights, pattern = rest[:6], rest[6]
    in_hbm = pl.BlockSpec(memory_space=pltpu.HBM)
    in_vmem = pl.BlockSpec(memory_space=pltpu.VMEM)
    results = pl.pallas_call(
        functools.partial(kernel, nx, ny),
        out_shape=(pltpu.VMEM((TOK, C), BF16), pltpu.VMEM((TOK, C), F32)),
        in_specs=[in_hbm] * 9,
        out_specs=(in_vmem, in_vmem),
        scratch_shapes=[vmem(w.shape, BF16) for w in weights]
        + [pltpu.SMEM((3, 6), jnp.int32), vmem(block, BF16)]
        + [vmem((2,) + block, BF16), vmem((6, 2, 1, 16, C), BF16)]
        + [vmem(tiles, BF16)] * 9
        + [
            vmem((28, 16, C), BF16),
            vmem((28, 16, C), BF16),
            vmem((PAIRS, KEYS, 256), BF16),
            vmem((KEYS, 2 * C), BF16),
            vmem((PAIRS, TOK, KEYS), BF16),
            vmem((PAIRS, TOK, KEYS), BF16),
            vmem((PAIRS, TOK, TOK), F32),
            vmem((PAIRS, KEYS, 256), F32),
            vmem((KEYS, TOK), F32),
            vmem((PAIRS, 256, TOK), BF16),
            dma((9,)),
            dma((8,)),
            dma((8,)),
            dma((4, 8)),
            dma((4, 8)),
            dma((8,)),
            dma((8,)),
        ],
        compiler_params=pltpu.CompilerParams(
            collective_id=0, has_side_effects=True, vmem_limit_bytes=60 * 1024 * 1024
        ),
    )(field.reshape(block), cotangent.reshape(tiles), *weights, pattern.T)
    layer_output, field_grad = pl.pallas_call(
        store,
        out_shape=(
            jax.ShapeDtypeStruct((TOK, C), BF16),
            jax.ShapeDtypeStruct((TOK, C), F32),
        ),
        in_specs=[in_vmem] * 2,
        out_specs=(in_hbm, in_hbm),
        scratch_shapes=[dma((2,))],
        compiler_params=pltpu.CompilerParams(vmem_limit_bytes=4 * 1024 * 1024),
    )(*results)
    return layer_output.reshape(field.shape), field_grad.reshape(field.shape)


def solution(mesh):
    split = P("gx", "gy", None, None)
    return jax.shard_map(
        functools.partial(shards, mesh.shape["gx"], mesh.shape["gy"]),
        mesh=mesh,
        in_specs=(split, split) + (P(),) * 7,
        out_specs=(split, split),
        check_vma=False,
    )
```

```python
import functools

import jax
import jax.numpy as jnp
from jax import lax
from jax.experimental import pallas as pl
from jax.experimental.pallas import tpu as pltpu
from jax.sharding import PartitionSpec as P

F32 = jnp.float32
BF16 = jnp.bfloat16
C = 384
FF = 1536
PAIRS = 3
TOK = 128
KEYS = 576
OWN, AROUND, EARLY, EDGES = slice(0, 128), slice(128, 384), slice(0, 384), slice(384, 576)
EPSILON = 1e-06
MASKED = -1e30
MESH = pl.DeviceIdType.MESH

SIDES = [(1, 1), (-1, -1), (1, -1), (-1, 1), (0, 1), (0, -1), (1, 0), (-1, 0)]
PEERS = [2, 6, 1, 3, 5, 7, 0, 4]


def nn(a, b):
    return lax.dot_general(a, b, (((1,), (0,)), ((), ())), preferred_element_type=F32)


def nt(a, b):
    return lax.dot_general(a, b, (((1,), (1,)), ((), ())), preferred_element_type=F32)


def inverse_rms(v):
    return lax.rsqrt(jnp.sum(v * v, axis=-1, keepdims=True) * (1.0 / C) + EPSILON)


def norm_back(v, r, upstream):
    inner = jnp.sum(v * upstream, axis=-1, keepdims=True) * (1.0 / C)
    return r * upstream - v * (r * r * r * inner)


def iota(shape, dim):
    return lax.broadcasted_iota(jnp.int32, shape, dim)


def stacked(pair):
    first = iota(pair.shape, 1) < 64
    upper = jnp.where(first, pair, 0.0)
    return jnp.concatenate([upper, pair - upper], axis=0).astype(BF16)


def diagonal(both):
    return jnp.concatenate([both[:64, :128], both[64:, 128:]], axis=0)


def abreast(both):
    return jnp.concatenate([both[:TOK], both[TOK:]], axis=1)


def lanes(p, base=0):
    return slice(base + 128 * p, base + 128 * (p + 1))


def kernel(
    nx,
    ny,
    field,
    cot,
    win_qkv_h,
    win_out_h,
    axial_qkv_h,
    axial_out_h,
    mlp_in_h,
    mlp_out_h,
    pattern_h,
    out_ref,
    grad_ref,
    win_qkv,
    win_out,
    axial_qkv,
    axial_out,
    mlp_in,
    mlp_out,
    win_out_t,
    win_kv_t,
    axial_out_t,
    axial_qkv_t,
    mlp_in_t,
    pattern,
    own,
    sides,
    edges,
    cot_own,
    cot_send,
    cot_recv,
    s1_send,
    s1_recv,
    lo_send,
    lo_recv,
    g1_send,
    g1_recv,
    dn_send,
    dn_recv,
    weights1,
    kv1,
    kt1,
    vt1,
    ot1,
    scores1,
    bias1,
    q1,
    local_sem,
    halo_send,
    halo_recv,
    a2a_send,
    a2a_recv,
    push_send,
    push_recv,
):
    gx = lax.axis_index("gx")
    gy = lax.axis_index("gy")

    partner = gx + 2 - 4 * ((gx >> 1) & 1)

    def step(index, by, size):
        moved = index + by
        if by > 0:
            return jnp.where(moved >= size, moved - size, moved)
        return jnp.where(moved < 0, moved + size, moved) if by else index

    def at(dx, dy):
        return (step(gx, dx, nx), step(gy, dy, ny))

    barrier = pltpu.get_barrier_semaphore()
    greeted = [at(dx, dy) for dx, dy in SIDES] + [(partner, step(gy, d, ny)) for d in PEERS]
    for device in greeted:
        pl.semaphore_signal(barrier, inc=1, device_id=device, device_id_type=MESH)

    local = []
    for index, (src, dst) in enumerate(
        [
            (field, own),
            (cot, cot_own),
            (win_qkv_h, win_qkv),
            (win_out_h, win_out),
            (axial_qkv_h, axial_qkv),
            (axial_out_h, axial_out),
            (mlp_in_h, mlp_in),
            (mlp_out_h, mlp_out),
            (pattern_h, pattern),
        ]
    ):
        copy = pltpu.make_async_copy(src, dst, local_sem.at[index])
        copy.start()
        local.append(copy)
    local[0].wait()
    pl.semaphore_wait(barrier, len(greeted))

    own_y = {0: slice(0, 4), 1: slice(3, 4), -1: slice(0, 1)}
    halo = []
    for index, (dx, dy) in enumerate(SIDES):
        copy = pltpu.make_async_remote_copy(
            src_ref=own.at[:, own_y[dy]],
            dst_ref=sides.at[index - 6] if dy == 0 else edges.at[index],
            send_sem=halo_send.at[index],
            recv_sem=halo_recv.at[index],
            device_id=at(dx, dy),
            device_id_type=MESH,
        )
        copy.start()
        halo.append(copy)

    def exchange(send, recv, group):
        copies = []
        for d in PEERS:
            peer = step(gy, d, ny)
            copy = pltpu.make_async_remote_copy(
                src_ref=send.at[peer],
                dst_ref=recv.at[gy],
                send_sem=a2a_send.at[group, d],
                recv_sem=a2a_recv.at[group, d],
                device_id=(partner, peer),
                device_id_type=MESH,
            )
            copy.start()
            copies.append(copy)
        return copies

    def arrived(send, recv, group):
        for d in PEERS:
            source = step(gy, -d, ny)
            pltpu.make_async_remote_copy(
                src_ref=send.at[source],
                dst_ref=recv.at[source],
                send_sem=a2a_send.at[group, d],
                recv_sem=a2a_recv.at[group, d],
                device_id=(partner, source),
                device_id_type=MESH,
            ).wait_recv()
        return recv[...].reshape(TOK, C)

    row, col = iota((TOK, TOK), 0), iota((TOK, TOK), 1)
    to_zxy = jnp.where(row == (col & 7) * 16 + (col >> 3), 1.0, 0.0).astype(BF16)
    to_xyz = jnp.where(col == (row & 7) * 16 + (row >> 3), 1.0, 0.0).astype(BF16)
    eye = jnp.where(row == col, 1.0, 0.0).astype(BF16)

    local[1].wait()
    cot_send[...] = nn(to_zxy, cot_own[...].reshape(TOK, C)).astype(BF16).reshape(8, 16, C)

    def near(rows, bits, x_base, y_base):
        key, query = iota((rows, TOK), 0), iota((rows, TOK), 1)
        gap_x = (key >> (3 + bits)) + x_base - ((query >> 3) & 1)
        gap_y = ((key >> 3) & ((1 << bits) - 1)) + y_base - (query & 7)
        gap_z = ((key & 7) - (query >> 4) + 2) & 7
        inside = (jnp.abs(gap_x) <= 2) & (jnp.abs(gap_y) <= 2) & (gap_z <= 4)
        return jnp.where(inside, 0.0, MASKED)

    bias1[OWN, :] = near(TOK, 3, 0, 0)
    for index, (dx, dy) in enumerate(SIDES):
        if dy == 0:
            start = 128 * (index - 5)
            bias1[start : start + 128, :] = near(128, 3, -2 * dx, 0)
        else:
            start = 384 + 32 * index
            bias1[start : start + 32, :] = near(32, 1, -2 * dx, -2 if dy == 1 else 8)

    def window_scores(part, tokens):
        values = tokens.astype(F32)
        normed = (values * inverse_rms(values)).astype(BF16)
        kv = nn(normed, win_qkv[:, C : 3 * C]).astype(BF16)
        kv1[part] = kv
        bias = jnp.concatenate([bias1[part, :], bias1[part, :]], axis=1)
        for p in range(PAIRS):
            scores1[p, part] = nt(kv[:, lanes(p)], q1[p]) + bias
            vt1[p, :, part] = nt(eye, kv[:, lanes(p, C)]).astype(BF16)
        return normed

    field_own = own[...].reshape(TOK, C)
    field_zxy = nn(to_zxy, field_own)
    normed1_zxy = (field_zxy * inverse_rms(field_zxy)).astype(BF16)
    local[2].wait()
    query1 = nn(normed1_zxy, win_qkv[:, 0:C]).astype(BF16).astype(F32) * 0.125
    for p in range(PAIRS):
        q1[p] = stacked(query1[:, lanes(p)])
    window_scores(OWN, field_own)
    cot_copies = exchange(cot_send, cot_recv, 0)
    for copy in local[5:7]:
        copy.wait()
    axial_out_t[...] = axial_out[...].T
    mlp_in_t[...] = mlp_in[...].T
    for copy in halo[6:]:
        copy.wait_recv()
    window_scores(AROUND, sides[...].reshape(256, C))
    tops, sums, outs = [], [], []
    for p in range(PAIRS):
        scores = scores1[p, EARLY]
        tops.append(jnp.max(scores, axis=0, keepdims=True))
        e = jnp.exp(scores - tops[p])
        scores1[p, EARLY] = e
        sums.append(jnp.sum(e, axis=0, keepdims=True))
        outs.append(diagonal(nn(vt1[p, :, EARLY], e.astype(BF16))))
    for copy in halo[:6]:
        copy.wait_recv()
    window_scores(EDGES, edges[...].reshape(192, C))
    attended, early_scale = [], []
    for p in range(PAIRS):
        scores = scores1[p, EDGES]
        top = jnp.maximum(tops[p], jnp.max(scores, axis=0, keepdims=True))
        e = jnp.exp(scores - top)
        shrink = jnp.exp(tops[p] - top)
        scale = 1.0 / (shrink * sums[p] + jnp.sum(e, axis=0, keepdims=True))
        weights = (e * scale).astype(BF16)
        weights1[p, EDGES] = weights
        early_scale.append(shrink * scale)
        early = jnp.concatenate(
            [
                outs[p][:64] * early_scale[p][:, :TOK],
                outs[p][64:] * early_scale[p][:, TOK:],
            ],
            axis=0,
        )
        ot = early + diagonal(nn(vt1[p, :, EDGES], weights))
        ot1[p] = ot
        attended.append(ot.astype(BF16).T)
    attended = jnp.concatenate(attended, axis=1)
    local[3].wait()
    s1_send[...] = (field_zxy + nn(attended, win_out[...])).astype(BF16).reshape(8, 16, C)
    s1_copies = exchange(s1_send, s1_recv, 1)

    for p in range(PAIRS):
        weights1[p, EARLY] = (scores1[p, EARLY] * early_scale[p]).astype(BF16)
        kt1[p] = nt(eye, kv1[:, lanes(p)]).astype(BF16)
    for copy in (local[4], local[7], local[8]):
        copy.wait()
    axial_qkv_t[...] = axial_qkv[...].T
    off = ((col >> 4) - (row >> 4)) & 7
    same_line = ((row ^ col) & 8) == 0
    bias2 = []
    for head in range(2 * PAIRS):
        hit = off == 0
        for j in range(3):
            hit = hit | (off == pattern[j, head])
        bias2.append(jnp.where(hit & same_line, 0.0, MASKED))

    gradient_bf = arrived(cot_send, cot_recv, 0)
    gradient = gradient_bf.astype(F32)
    d_hidden = [
        nt(gradient_bf, mlp_out[512 * c : 512 * (c + 1), :]) for c in range(FF // 512)
    ]
    stream1 = arrived(s1_send, s1_recv, 1).astype(F32)
    r2 = inverse_rms(stream1)
    triple2 = nn((stream1 * r2).astype(BF16), axial_qkv[...]).astype(BF16)
    query2 = triple2[:, 0:C].astype(F32) * 0.125
    q2 = [stacked(query2[:, lanes(p)]) for p in range(PAIRS)]
    weights2 = []
    attended2 = []
    for p in range(PAIRS):
        pair_bias = jnp.concatenate([bias2[2 * p], bias2[2 * p + 1]], axis=0)
        scores = nt(q2[p], triple2[:, lanes(p, C)]) + pair_bias
        e = jnp.exp(scores - jnp.max(scores, axis=1, keepdims=True))
        weights = (e * (1.0 / jnp.sum(e, axis=1, keepdims=True))).astype(BF16)
        weights2.append(weights)
        values = stacked(triple2[:, lanes(p, 2 * C)].astype(F32))
        attended2.append(nn(abreast(weights), values))
    attended2 = jnp.concatenate(attended2, axis=1).astype(BF16)
    stream2 = (stream1 + nn(attended2, axial_out[...])).astype(BF16).astype(F32)

    r3 = inverse_rms(stream2)
    normed3 = (stream2 * r3).astype(BF16)
    hidden = []
    back = None
    for c in range(FF // 512):
        part = slice(512 * c, 512 * (c + 1))
        a = nn(normed3, mlp_in[:, part])
        square = a * a
        t = jnp.tanh(0.7978845608028654 * (a + 0.044715 * (a * square)))
        half = 0.5 * (1.0 + t)
        hidden.append((a * half).astype(BF16))
        slope = half + (0.5 * a) * (1.0 - t * t) * (
            0.7978845608028654 + (3 * 0.044715 * 0.7978845608028654) * square
        )
        term = nn((d_hidden[c] * slope).astype(BF16), mlp_in_t[part, :])
        back = term if back is None else back + term
    grad2 = gradient + norm_back(stream2, r3, back)

    back2 = nn(grad2.astype(BF16), axial_out_t[...])
    d_query, d_key, d_value = [], [], []
    for p in range(PAIRS):
        upstream = stacked(back2[:, lanes(p)])
        keys = stacked(triple2[:, lanes(p, C)].astype(F32))
        weights = weights2[p].astype(F32)
        d_weights = nt(upstream, triple2[:, lanes(p, 2 * C)])
        delta = jnp.sum(weights * d_weights, axis=1, keepdims=True)
        d_scores = (weights * (d_weights - delta)).astype(BF16)
        d_query.append(nn(abreast(d_scores), keys) * 0.125)
        d_key.append(nn(d_scores.T, q2[p]))
        d_value.append(nn(weights2[p].T, upstream))
    d_triple2 = jnp.concatenate(d_query + d_key + d_value, axis=1).astype(BF16)
    grad1 = grad2 + norm_back(stream1, r2, nn(d_triple2, axial_qkv_t[...]))
    g1_send[...] = grad1.astype(BF16).reshape(8, 16, C)
    g1_copies = exchange(g1_send, g1_recv, 3)

    hidden_out = nn(jnp.concatenate(hidden, axis=1), mlp_out[...])
    lo_send[...] = (stream2 + hidden_out).astype(BF16).reshape(8, 16, C)
    lo_copies = exchange(lo_send, lo_recv, 2)
    win_out_t[...] = win_out[...].T
    win_kv_t[...] = win_qkv[:, C : 3 * C].T

    grad1_bf = arrived(g1_send, g1_recv, 3)
    back1 = nn(grad1_bf, win_out_t[...])
    back1_t = nt(win_out[...], grad1_bf).astype(BF16).astype(F32)
    upstream, delta = [], []
    for p in range(PAIRS):
        upstream.append(stacked(back1[:, lanes(p)]))
        product = ot1[p] * back1_t[lanes(p)]
        halves = [jnp.sum(product[h : h + 64], axis=0, keepdims=True) for h in (0, 64)]
        delta.append(jnp.concatenate(halves, axis=1))

    def window_back(part):
        d_scores, d_key, d_value = [], [], []
        for p in range(PAIRS):
            weights = weights1[p, part]
            d_weights = nt(kv1[part, lanes(p, C)], upstream[p])
            d_scores.append((weights.astype(F32) * (d_weights - delta[p])).astype(BF16))
            d_key.append(nn(d_scores[p], q1[p]).astype(BF16))
            d_value.append(nn(weights, upstream[p]).astype(BF16))
        d_kv = jnp.concatenate(d_key + d_value, axis=1)
        return d_scores, nn(d_kv, win_kv_t[...])

    push = []

    def send_back(index):
        dx, dy = SIDES[index]
        if dy == 0:
            rows = slice(8 * (index - 6), 8 * (index - 5))
        else:
            rows = slice(16 + 2 * index, 18 + 2 * index)
        copy = pltpu.make_async_remote_copy(
            src_ref=dn_send.at[rows],
            dst_ref=dn_recv.at[rows],
            send_sem=push_send.at[index],
            recv_sem=push_recv.at[index],
            device_id=at(-dx, -dy),
            device_id_type=MESH,
        )
        copy.start()
        push.append(copy)

    scores_edges, dn = window_back(EDGES)
    dn_send[16:28] = dn.astype(BF16).reshape(12, 16, C)
    for index in range(6):
        send_back(index)
    scores_around, dn = window_back(AROUND)
    dn_send[0:16] = dn.astype(BF16).reshape(16, 16, C)
    for index in range(6, 8):
        send_back(index)

    scores_own, d_normed = window_back(OWN)
    d_query = []
    for p in range(PAIRS):
        both = nn(kt1[p, :, EDGES], scores_edges[p]) + nn(kt1[p, :, AROUND], scores_around[p])
        both = both + nn(kt1[p, :, OWN], scores_own[p])
        d_query.append((diagonal(both) * 0.125).astype(BF16))
    d_query = nt(to_xyz, jnp.concatenate(d_query, axis=0)).astype(BF16)
    d_normed = d_normed + nt(d_query, win_qkv[:, 0:C])
    grad1_xyz = nn(to_xyz, grad1_bf)
    out_ref[...] = nn(to_xyz, arrived(lo_send, lo_recv, 2)).astype(BF16)
    for copy in push:
        copy.wait_recv()
    d_normed = d_normed + (dn_recv[0:8].astype(F32) + dn_recv[8:16].astype(F32)).reshape(TOK, C)
    first, last = [
        sum(
            dn_recv[16 + 2 * i : 18 + 2 * i].astype(F32)
            for i, (_, dy) in enumerate(SIDES)
            if dy == way
        )
        for way in (-1, 1)
    ]
    none = jnp.zeros((32, C), F32)
    rims = jnp.concatenate([first[0], none, last[0], first[1], none, last[1]], axis=0)
    field_f = own[...].reshape(TOK, C).astype(F32)
    grad_ref[...] = grad1_xyz + norm_back(field_f, inverse_rms(field_f), d_normed + rims)

    for copy in halo + cot_copies + s1_copies + lo_copies + g1_copies + push:
        copy.wait_send()


def store(out_ref, grad_ref, out_hbm, grad_hbm, sem):
    copies = [
        pltpu.make_async_copy(grad_ref, grad_hbm, sem.at[0]),
        pltpu.make_async_copy(out_ref, out_hbm, sem.at[1]),
    ]
    for copy in copies:
        copy.start()
    for copy in copies:
        copy.wait()


def shards(nx, ny, field, cotangent, *rest):
    block = (2, 4, 16, C)
    tiles = (8, 16, C)
    vmem = pltpu.VMEM
    dma = pltpu.SemaphoreType.DMA
    weights, pattern = rest[:6], rest[6]
    in_hbm = pl.BlockSpec(memory_space=pltpu.HBM)
    in_vmem = pl.BlockSpec(memory_space=pltpu.VMEM)
    results = pl.pallas_call(
        functools.partial(kernel, nx, ny),
        out_shape=(pltpu.VMEM((TOK, C), BF16), pltpu.VMEM((TOK, C), F32)),
        in_specs=[in_hbm] * 9,
        out_specs=(in_vmem, in_vmem),
        scratch_shapes=[vmem(w.shape, BF16) for w in weights]
        + [vmem((n, C), BF16) for n in (C, 2 * C, C, 3 * C, FF)]
        + [pltpu.SMEM((3, 6), jnp.int32), vmem(block, BF16)]
        + [vmem((2,) + block, BF16), vmem((6, 2, 1, 16, C), BF16)]
        + [vmem(tiles, BF16)] * 9
        + [
            vmem((28, 16, C), BF16),
            vmem((28, 16, C), BF16),
            vmem((PAIRS, KEYS, 256), BF16),
            vmem((KEYS, 2 * C), BF16),
            vmem((PAIRS, TOK, KEYS), BF16),
            vmem((PAIRS, TOK, KEYS), BF16),
            vmem((PAIRS, TOK, TOK), F32),
            vmem((PAIRS, KEYS, 256), F32),
            vmem((KEYS, TOK), F32),
            vmem((PAIRS, 256, TOK), BF16),
            dma((9,)),
            dma((8,)),
            dma((8,)),
            dma((4, 8)),
            dma((4, 8)),
            dma((8,)),
            dma((8,)),
        ],
        compiler_params=pltpu.CompilerParams(
            collective_id=0, has_side_effects=True, vmem_limit_bytes=60 * 1024 * 1024
        ),
    )(field.reshape(block), cotangent.reshape(tiles), *weights, pattern.T)
    layer_output, field_grad = pl.pallas_call(
        store,
        out_shape=(
            jax.ShapeDtypeStruct((TOK, C), BF16),
            jax.ShapeDtypeStruct((TOK, C), F32),
        ),
        in_specs=[in_vmem] * 2,
        out_specs=(in_hbm, in_hbm),
        scratch_shapes=[dma((2,))],
        compiler_params=pltpu.CompilerParams(vmem_limit_bytes=4 * 1024 * 1024),
    )(*results)
    return layer_output.reshape(field.shape), field_grad.reshape(field.shape)


def solution(mesh):
    split = P("gx", "gy", None, None)
    return jax.shard_map(
        functools.partial(shards, mesh.shape["gx"], mesh.shape["gy"]),
        mesh=mesh,
        in_specs=(split, split) + (P(),) * 7,
        out_specs=(split, split),
        check_vma=False,
    )
```

```python
import functools

import jax
import jax.numpy as jnp
from jax import lax
from jax.experimental import pallas as pl
from jax.experimental.pallas import tpu as pltpu
from jax.sharding import PartitionSpec as P

F32 = jnp.float32
BF16 = jnp.bfloat16
C = 384
FF = 1536
CHUNK = 1536
PAIRS = 3
TOK = 128
KEYS = 576
OWN, AROUND, EARLY, EDGES = slice(0, 128), slice(128, 384), slice(0, 384), slice(384, 576)
EPSILON = 1e-06
MASKED = -1e30
MESH = pl.DeviceIdType.MESH

SIDES = [(1, 1), (-1, -1), (1, -1), (-1, 1), (0, 1), (0, -1), (1, 0), (-1, 0)]
PEERS = [2, 6, 1, 3, 5, 7, 0, 4]


def nn(a, b):
    return lax.dot_general(a, b, (((1,), (0,)), ((), ())), preferred_element_type=F32)


def nt(a, b):
    return lax.dot_general(a, b, (((1,), (1,)), ((), ())), preferred_element_type=F32)


def inverse_rms(v):
    return lax.rsqrt(jnp.sum(v * v, axis=-1, keepdims=True) * (1.0 / C) + EPSILON)


def norm_back(v, r, upstream):
    inner = jnp.sum(v * upstream, axis=-1, keepdims=True) * (1.0 / C)
    return r * upstream - v * (r * r * r * inner)


def iota(shape, dim):
    return lax.broadcasted_iota(jnp.int32, shape, dim)


def diagonal(both):
    return jnp.concatenate([both[:64, :128], both[64:, 128:]], axis=0)


def abreast(both):
    return jnp.concatenate([both[:TOK], both[TOK:]], axis=1)


def lanes(p, base=0):
    return slice(base + 128 * p, base + 128 * (p + 1))


def kernel(
    nx,
    ny,
    field,
    cot,
    win_qkv_h,
    win_out_h,
    axial_qkv_h,
    axial_out_h,
    mlp_in_h,
    mlp_out_h,
    pattern_h,
    out_ref,
    grad_ref,
    win_qkv,
    win_out,
    axial_qkv,
    axial_out,
    mlp_in,
    mlp_out,
    win_out_t,
    win_kv_t,
    axial_out_t,
    axial_qkv_t,
    mlp_in_t,
    pattern,
    own,
    sides,
    edges,
    cot_own,
    cot_send,
    cot_recv,
    s1_send,
    s1_recv,
    lo_send,
    lo_recv,
    g1_send,
    g1_recv,
    dn_send,
    dn_recv,
    weights1,
    kv1,
    kt1,
    vt1,
    ot1,
    scores1,
    bias1,
    q1,
    local_sem,
    halo_send,
    halo_recv,
    a2a_send,
    a2a_recv,
    push_send,
    push_recv,
):
    gx = lax.axis_index("gx")
    gy = lax.axis_index("gy")

    partner = gx + 2 - 4 * ((gx >> 1) & 1)

    def step(index, by, size):
        moved = index + by
        if by > 0:
            return jnp.where(moved >= size, moved - size, moved)
        return jnp.where(moved < 0, moved + size, moved) if by else index

    def at(dx, dy):
        return (step(gx, dx, nx), step(gy, dy, ny))

    barrier = pltpu.get_barrier_semaphore()
    greeted = [at(dx, dy) for dx, dy in SIDES] + [(partner, step(gy, d, ny)) for d in PEERS]
    for device in greeted:
        pl.semaphore_signal(barrier, inc=1, device_id=device, device_id_type=MESH)

    local = []
    for index, (src, dst) in enumerate(
        [
            (field, own),
            (cot, cot_own),
            (win_qkv_h, win_qkv),
            (win_out_h, win_out),
            (axial_qkv_h, axial_qkv),
            (axial_out_h, axial_out),
            (mlp_in_h, mlp_in),
            (mlp_out_h, mlp_out),
            (pattern_h, pattern),
        ]
    ):
        copy = pltpu.make_async_copy(src, dst, local_sem.at[index])
        copy.start()
        local.append(copy)
    local[0].wait()
    pl.semaphore_wait(barrier, len(greeted))

    own_y = {0: slice(0, 4), 1: slice(3, 4), -1: slice(0, 1)}
    halo = []
    for index, (dx, dy) in enumerate(SIDES):
        copy = pltpu.make_async_remote_copy(
            src_ref=own.at[:, own_y[dy]],
            dst_ref=sides.at[index - 6] if dy == 0 else edges.at[index],
            send_sem=halo_send.at[index],
            recv_sem=halo_recv.at[index],
            device_id=at(dx, dy),
            device_id_type=MESH,
        )
        copy.start()
        halo.append(copy)

    def exchange(send, recv, group):
        copies = []
        for d in PEERS:
            peer = step(gy, d, ny)
            copy = pltpu.make_async_remote_copy(
                src_ref=send.at[peer],
                dst_ref=recv.at[gy],
                send_sem=a2a_send.at[group, d],
                recv_sem=a2a_recv.at[group, d],
                device_id=(partner, peer),
                device_id_type=MESH,
            )
            copy.start()
            copies.append(copy)
        return copies

    def arrived(send, recv, group):
        for d in PEERS:
            source = step(gy, -d, ny)
            pltpu.make_async_remote_copy(
                src_ref=send.at[source],
                dst_ref=recv.at[source],
                send_sem=a2a_send.at[group, d],
                recv_sem=a2a_recv.at[group, d],
                device_id=(partner, source),
                device_id_type=MESH,
            ).wait_recv()
        return recv[...].reshape(TOK, C)

    row, col = iota((TOK, TOK), 0), iota((TOK, TOK), 1)
    to_zxy = jnp.where(row == (col & 7) * 16 + (col >> 3), 1.0, 0.0).astype(BF16)
    to_xyz = jnp.where(col == (row & 7) * 16 + (row >> 3), 1.0, 0.0).astype(BF16)
    eye = jnp.where(row == col, 1.0, 0.0).astype(BF16)
    head0 = jnp.where(col < 64, 1.0, 0.0).astype(BF16)
    head1 = jnp.where(col < 64, 0.0, 1.0).astype(BF16)

    def stacked(pair):
        return jnp.concatenate([pair * head0, pair * head1], axis=0)

    local[1].wait()
    cot_send[...] = nn(to_zxy, cot_own[...].reshape(TOK, C)).astype(BF16).reshape(8, 16, C)

    def near(rows, bits, x_base, y_base):
        key, query = iota((rows, TOK), 0), iota((rows, TOK), 1)
        gap_x = (key >> (3 + bits)) + x_base - ((query >> 3) & 1)
        gap_y = ((key >> 3) & ((1 << bits) - 1)) + y_base - (query & 7)
        gap_z = ((key & 7) - (query >> 4) + 2) & 7
        inside = (jnp.abs(gap_x) <= 2) & (jnp.abs(gap_y) <= 2) & (gap_z <= 4)
        return jnp.where(inside, 0.0, MASKED)

    bias1[OWN, :] = near(TOK, 3, 0, 0)
    for index, (dx, dy) in enumerate(SIDES):
        if dy == 0:
            start = 128 * (index - 5)
            bias1[start : start + 128, :] = near(128, 3, -2 * dx, 0)
        else:
            start = 384 + 32 * index
            bias1[start : start + 32, :] = near(32, 1, -2 * dx, -2 if dy == 1 else 8)

    def window_scores(part, tokens):
        values = tokens.astype(F32)
        normed = (values * inverse_rms(values)).astype(BF16)
        kv = nn(normed, win_qkv[:, C : 3 * C]).astype(BF16)
        kv1[part] = kv
        bias = jnp.concatenate([bias1[part, :], bias1[part, :]], axis=1)
        for p in range(PAIRS):
            scores1[p, part] = nt(kv[:, lanes(p)], q1[p]) + bias
            vt1[p, :, part] = nt(eye, kv[:, lanes(p, C)]).astype(BF16)
        return normed

    field_own = own[...].reshape(TOK, C)
    field_zxy = nn(to_zxy, field_own)
    normed1_zxy = (field_zxy * inverse_rms(field_zxy)).astype(BF16)
    local[2].wait()
    query1 = nn(normed1_zxy, win_qkv[:, 0:C]).astype(BF16) * 0.125
    for p in range(PAIRS):
        q1[p] = stacked(query1[:, lanes(p)])
    window_scores(OWN, field_own)
    cot_copies = exchange(cot_send, cot_recv, 0)
    for copy in local[5:7]:
        copy.wait()
    axial_out_t[...] = axial_out[...].T
    mlp_in_t[...] = mlp_in[...].T
    for copy in halo[6:]:
        copy.wait_recv()
    window_scores(AROUND, sides[...].reshape(256, C))
    tops, sums, outs = [], [], []
    for p in range(PAIRS):
        scores = scores1[p, EARLY]
        tops.append(jnp.max(scores, axis=0, keepdims=True))
        e = jnp.exp(scores - tops[p])
        scores1[p, EARLY] = e
        sums.append(jnp.sum(e, axis=0, keepdims=True))
        outs.append(diagonal(nn(vt1[p, :, EARLY], e.astype(BF16))))
    for copy in halo[:6]:
        copy.wait_recv()
    window_scores(EDGES, edges[...].reshape(192, C))
    attended, early_scale = [], []
    for p in range(PAIRS):
        scores = scores1[p, EDGES]
        top = jnp.maximum(tops[p], jnp.max(scores, axis=0, keepdims=True))
        e = jnp.exp(scores - top)
        shrink = jnp.exp(tops[p] - top)
        scale = 1.0 / (shrink * sums[p] + jnp.sum(e, axis=0, keepdims=True))
        weights = (e * scale).astype(BF16)
        weights1[p, EDGES] = weights
        early_scale.append(shrink * scale)
        early = jnp.concatenate(
            [
                outs[p][:64] * early_scale[p][:, :TOK],
                outs[p][64:] * early_scale[p][:, TOK:],
            ],
            axis=0,
        )
        ot = early + diagonal(nn(vt1[p, :, EDGES], weights))
        ot1[p] = ot
        attended.append(ot.astype(BF16).T)
    attended = jnp.concatenate(attended, axis=1)
    local[3].wait()
    s1_send[...] = (field_zxy + nn(attended, win_out[...])).astype(BF16).reshape(8, 16, C)
    s1_copies = exchange(s1_send, s1_recv, 1)

    for p in range(PAIRS):
        weights1[p, EARLY] = (scores1[p, EARLY] * early_scale[p]).astype(BF16)
        kt1[p] = nt(eye, kv1[:, lanes(p)]).astype(BF16)
    for copy in (local[4], local[7], local[8]):
        copy.wait()
    axial_qkv_t[...] = axial_qkv[...].T
    off = ((col >> 4) - (row >> 4)) & 7
    same_line = ((row ^ col) & 8) == 0
    bias2 = []
    for head in range(2 * PAIRS):
        hit = off == 0
        for j in range(3):
            hit = hit | (off == pattern[j, head])
        bias2.append(jnp.where(hit & same_line, 0.0, MASKED))

    gradient_bf = arrived(cot_send, cot_recv, 0)
    gradient = gradient_bf.astype(F32)
    d_hidden = [
        nt(gradient_bf, mlp_out[CHUNK * c : CHUNK * (c + 1), :]) for c in range(FF // CHUNK)
    ]
    stream1 = arrived(s1_send, s1_recv, 1).astype(F32)
    r2 = inverse_rms(stream1)
    triple2 = nn((stream1 * r2).astype(BF16), axial_qkv[...]).astype(BF16)
    query2 = triple2[:, 0:C] * 0.125
    q2 = [stacked(query2[:, lanes(p)]) for p in range(PAIRS)]
    weights2 = []
    attended2 = []
    for p in range(PAIRS):
        pair_bias = jnp.concatenate([bias2[2 * p], bias2[2 * p + 1]], axis=0)
        scores = nt(q2[p], triple2[:, lanes(p, C)]) + pair_bias
        e = jnp.exp(scores - jnp.max(scores, axis=1, keepdims=True))
        weights = (e * (1.0 / jnp.sum(e, axis=1, keepdims=True))).astype(BF16)
        weights2.append(weights)
        values = stacked(triple2[:, lanes(p, 2 * C)])
        attended2.append(nn(abreast(weights), values))
    attended2 = jnp.concatenate(attended2, axis=1).astype(BF16)
    stream2 = (stream1 + nn(attended2, axial_out[...])).astype(BF16).astype(F32)

    r3 = inverse_rms(stream2)
    normed3 = (stream2 * r3).astype(BF16)
    hidden = []
    back = None
    for c in range(FF // CHUNK):
        part = slice(CHUNK * c, CHUNK * (c + 1))
        a = nn(normed3, mlp_in[:, part])
        square = a * a
        t = jnp.tanh(0.7978845608028654 * (a + 0.044715 * (a * square)))
        half = 0.5 * (1.0 + t)
        hidden.append((a * half).astype(BF16))
        slope = half + (0.5 * a) * (1.0 - t * t) * (
            0.7978845608028654 + (3 * 0.044715 * 0.7978845608028654) * square
        )
        term = nn((d_hidden[c] * slope).astype(BF16), mlp_in_t[part, :])
        back = term if back is None else back + term
    grad2 = gradient + norm_back(stream2, r3, back)

    back2 = nn(grad2.astype(BF16), axial_out_t[...]).astype(BF16)
    d_query, d_key, d_value = [], [], []
    for p in range(PAIRS):
        upstream = stacked(back2[:, lanes(p)])
        keys = stacked(triple2[:, lanes(p, C)])
        weights = weights2[p].astype(F32)
        d_weights = nt(upstream, triple2[:, lanes(p, 2 * C)])
        delta = jnp.sum(weights * d_weights, axis=1, keepdims=True)
        d_scores = (weights * (d_weights - delta)).astype(BF16)
        d_query.append(nn(abreast(d_scores), keys) * 0.125)
        d_key.append(nn(d_scores.T, q2[p]))
        d_value.append(nn(weights2[p].T, upstream))
    d_triple2 = jnp.concatenate(d_query + d_key + d_value, axis=1).astype(BF16)
    grad1 = grad2 + norm_back(stream1, r2, nn(d_triple2, axial_qkv_t[...]))
    g1_send[...] = grad1.astype(BF16).reshape(8, 16, C)
    g1_copies = exchange(g1_send, g1_recv, 3)

    hidden_out = nn(jnp.concatenate(hidden, axis=1), mlp_out[...])
    lo_send[...] = (stream2 + hidden_out).astype(BF16).reshape(8, 16, C)
    lo_copies = exchange(lo_send, lo_recv, 2)
    win_out_t[...] = win_out[...].T
    win_kv_t[...] = win_qkv[:, C : 3 * C].T

    grad1_bf = arrived(g1_send, g1_recv, 3)
    back1 = nn(grad1_bf, win_out_t[...]).astype(BF16)
    back1_t = nt(win_out[...], grad1_bf).astype(BF16).astype(F32)
    upstream, delta = [], []
    for p in range(PAIRS):
        upstream.append(stacked(back1[:, lanes(p)]))
        product = ot1[p] * back1_t[lanes(p)]
        halves = [jnp.sum(product[h : h + 64], axis=0, keepdims=True) for h in (0, 64)]
        delta.append(jnp.concatenate(halves, axis=1))

    def window_back(part):
        d_scores, d_key, d_value = [], [], []
        for p in range(PAIRS):
            weights = weights1[p, part]
            d_weights = nt(kv1[part, lanes(p, C)], upstream[p])
            d_scores.append((weights.astype(F32) * (d_weights - delta[p])).astype(BF16))
            d_key.append(nn(d_scores[p], q1[p]).astype(BF16))
            d_value.append(nn(weights, upstream[p]).astype(BF16))
        d_kv = jnp.concatenate(d_key + d_value, axis=1)
        return d_scores, nn(d_kv, win_kv_t[...])

    push = []

    def send_back(index):
        dx, dy = SIDES[index]
        if dy == 0:
            rows = slice(8 * (index - 6), 8 * (index - 5))
        else:
            rows = slice(16 + 2 * index, 18 + 2 * index)
        copy = pltpu.make_async_remote_copy(
            src_ref=dn_send.at[rows],
            dst_ref=dn_recv.at[rows],
            send_sem=push_send.at[index],
            recv_sem=push_recv.at[index],
            device_id=at(-dx, -dy),
            device_id_type=MESH,
        )
        copy.start()
        push.append(copy)

    scores_edges, dn_edges = window_back(EDGES)
    scores_around, dn_around = window_back(AROUND)
    dn_send[16:28] = dn_edges.astype(BF16).reshape(12, 16, C)
    dn_send[0:16] = dn_around.astype(BF16).reshape(16, 16, C)
    for index in range(8):
        send_back(index)

    scores_own, d_normed = window_back(OWN)
    d_query = []
    for p in range(PAIRS):
        both = nn(kt1[p, :, EDGES], scores_edges[p]) + nn(kt1[p, :, AROUND], scores_around[p])
        both = both + nn(kt1[p, :, OWN], scores_own[p])
        d_query.append((diagonal(both) * 0.125).astype(BF16))
    d_query = nt(to_xyz, jnp.concatenate(d_query, axis=0)).astype(BF16)
    d_normed = d_normed + nt(d_query, win_qkv[:, 0:C])
    grad1_xyz = nn(to_xyz, grad1_bf)
    out_ref[...] = nn(to_xyz, arrived(lo_send, lo_recv, 2)).astype(BF16)
    for copy in push:
        copy.wait_recv()
    d_normed = d_normed + (dn_recv[0:8].astype(F32) + dn_recv[8:16].astype(F32)).reshape(TOK, C)
    first, last = [
        sum(
            dn_recv[16 + 2 * i : 18 + 2 * i].astype(F32)
            for i, (_, dy) in enumerate(SIDES)
            if dy == way
        )
        for way in (-1, 1)
    ]
    none = jnp.zeros((32, C), F32)
    rims = jnp.concatenate([first[0], none, last[0], first[1], none, last[1]], axis=0)
    field_f = own[...].reshape(TOK, C).astype(F32)
    grad_ref[...] = grad1_xyz + norm_back(field_f, inverse_rms(field_f), d_normed + rims)

    for copy in halo + cot_copies + s1_copies + lo_copies + g1_copies + push:
        copy.wait_send()


def store(out_ref, grad_ref, out_hbm, grad_hbm, sem):
    copies = [
        pltpu.make_async_copy(grad_ref, grad_hbm, sem.at[0]),
        pltpu.make_async_copy(out_ref, out_hbm, sem.at[1]),
    ]
    for copy in copies:
        copy.start()
    for copy in copies:
        copy.wait()


def shards(nx, ny, field, cotangent, *rest):
    block = (2, 4, 16, C)
    tiles = (8, 16, C)
    vmem = pltpu.VMEM
    dma = pltpu.SemaphoreType.DMA
    weights, pattern = rest[:6], rest[6]
    in_hbm = pl.BlockSpec(memory_space=pltpu.HBM)
    in_vmem = pl.BlockSpec(memory_space=pltpu.VMEM)
    results = pl.pallas_call(
        functools.partial(kernel, nx, ny),
        out_shape=(pltpu.VMEM((TOK, C), BF16), pltpu.VMEM((TOK, C), F32)),
        in_specs=[in_hbm] * 9,
        out_specs=(in_vmem, in_vmem),
        scratch_shapes=[vmem(w.shape, BF16) for w in weights]
        + [vmem((n, C), BF16) for n in (C, 2 * C, C, 3 * C, FF)]
        + [pltpu.SMEM((3, 6), jnp.int32), vmem(block, BF16)]
        + [vmem((2,) + block, BF16), vmem((6, 2, 1, 16, C), BF16)]
        + [vmem(tiles, BF16)] * 9
        + [
            vmem((28, 16, C), BF16),
            vmem((28, 16, C), BF16),
            vmem((PAIRS, KEYS, 256), BF16),
            vmem((KEYS, 2 * C), BF16),
            vmem((PAIRS, TOK, KEYS), BF16),
            vmem((PAIRS, TOK, KEYS), BF16),
            vmem((PAIRS, TOK, TOK), F32),
            vmem((PAIRS, KEYS, 256), F32),
            vmem((KEYS, TOK), F32),
            vmem((PAIRS, 256, TOK), BF16),
            dma((9,)),
            dma((8,)),
            dma((8,)),
            dma((4, 8)),
            dma((4, 8)),
            dma((8,)),
            dma((8,)),
        ],
        compiler_params=pltpu.CompilerParams(
            collective_id=0, has_side_effects=True, vmem_limit_bytes=60 * 1024 * 1024
        ),
    )(field.reshape(block), cotangent.reshape(tiles), *weights, pattern.T)
    layer_output, field_grad = pl.pallas_call(
        store,
        out_shape=(
            jax.ShapeDtypeStruct((TOK, C), BF16),
            jax.ShapeDtypeStruct((TOK, C), F32),
        ),
        in_specs=[in_vmem] * 2,
        out_specs=(in_hbm, in_hbm),
        scratch_shapes=[dma((2,))],
        compiler_params=pltpu.CompilerParams(vmem_limit_bytes=4 * 1024 * 1024),
    )(*results)
    return layer_output.reshape(field.shape), field_grad.reshape(field.shape)


def solution(mesh):
    split = P("gx", "gy", None, None)
    return jax.shard_map(
        functools.partial(shards, mesh.shape["gx"], mesh.shape["gy"]),
        mesh=mesh,
        in_specs=(split, split) + (P(),) * 7,
        out_specs=(split, split),
        check_vma=False,
    )
```

```python
import functools

import jax
import jax.numpy as jnp
from jax import lax
from jax.experimental import pallas as pl
from jax.experimental.pallas import tpu as pltpu
from jax.sharding import PartitionSpec as P

F32 = jnp.float32
BF16 = jnp.bfloat16
C = 384
FF = 1536
CHUNK = 1536
PAIRS = 3
TOK = 128
KEYS = 576
OWN, AROUND, EARLY, EDGES = slice(0, 128), slice(128, 384), slice(0, 384), slice(384, 576)
EPSILON = 1e-06
MASKED = -1e30
MESH = pl.DeviceIdType.MESH

SIDES = [(1, 1), (-1, -1), (1, -1), (-1, 1), (0, 1), (0, -1), (1, 0), (-1, 0)]
PEERS = [2, 6, 1, 3, 5, 7, 0, 4]


def nn(a, b):
    return lax.dot_general(a, b, (((1,), (0,)), ((), ())), preferred_element_type=F32)


def nt(a, b):
    return lax.dot_general(a, b, (((1,), (1,)), ((), ())), preferred_element_type=F32)


def inverse_rms(v):
    return lax.rsqrt(jnp.sum(v * v, axis=-1, keepdims=True) * (1.0 / C) + EPSILON)


def norm_back(v, r, upstream):
    inner = jnp.sum(v * upstream, axis=-1, keepdims=True) * (1.0 / C)
    return r * upstream - v * (r * r * r * inner)


def iota(shape, dim):
    return lax.broadcasted_iota(jnp.int32, shape, dim)


def diagonal(both):
    return jnp.concatenate([both[:64, :128], both[64:, 128:]], axis=0)


def abreast(both):
    return jnp.concatenate([both[:TOK], both[TOK:]], axis=1)


def lanes(p, base=0):
    return slice(base + 128 * p, base + 128 * (p + 1))


def kernel(
    nx,
    ny,
    field,
    cot,
    win_qkv_h,
    win_out_h,
    axial_qkv_h,
    axial_out_h,
    mlp_in_h,
    mlp_out_h,
    pattern_h,
    out_ref,
    grad_ref,
    win_qkv,
    win_out,
    axial_qkv,
    axial_out,
    mlp_in,
    mlp_out,
    win_out_t,
    win_kv_t,
    axial_out_t,
    axial_qkv_t,
    mlp_in_t,
    pattern,
    own,
    sides,
    edges,
    cot_own,
    cot_send,
    cot_recv,
    s1_send,
    s1_recv,
    lo_send,
    lo_recv,
    g1_send,
    g1_recv,
    dn_send,
    dn_recv,
    weights1,
    kv1,
    kt1,
    vt1,
    ot1,
    scores1,
    bias1,
    q1,
    local_sem,
    halo_send,
    halo_recv,
    a2a_send,
    a2a_recv,
    push_send,
    push_recv,
):
    gx = lax.axis_index("gx")
    gy = lax.axis_index("gy")

    partner = gx + 2 - 4 * ((gx >> 1) & 1)

    def step(index, by, size):
        moved = index + by
        if by > 0:
            return jnp.where(moved >= size, moved - size, moved)
        return jnp.where(moved < 0, moved + size, moved) if by else index

    def at(dx, dy):
        return (step(gx, dx, nx), step(gy, dy, ny))

    barrier = pltpu.get_barrier_semaphore()
    greeted = [at(dx, dy) for dx, dy in SIDES] + [(partner, step(gy, d, ny)) for d in PEERS]
    for device in greeted:
        pl.semaphore_signal(barrier, inc=1, device_id=device, device_id_type=MESH)

    local = [
        pltpu.make_async_copy(src, dst, local_sem.at[index])
        for index, (src, dst) in enumerate(
            [
                (field, own),
                (cot, cot_own),
                (win_qkv_h, win_qkv),
                (win_out_h, win_out),
                (axial_qkv_h, axial_qkv),
                (axial_out_h, axial_out),
                (mlp_in_h, mlp_in),
                (mlp_out_h, mlp_out),
                (pattern_h, pattern),
            ]
        )
    ]
    for copy in local[:2]:
        copy.start()
    local[0].wait()
    pl.semaphore_wait(barrier, len(greeted))

    own_y = {0: slice(0, 4), 1: slice(3, 4), -1: slice(0, 1)}
    halo = []
    for index, (dx, dy) in enumerate(SIDES):
        copy = pltpu.make_async_remote_copy(
            src_ref=own.at[:, own_y[dy]],
            dst_ref=sides.at[index - 6] if dy == 0 else edges.at[index],
            send_sem=halo_send.at[index],
            recv_sem=halo_recv.at[index],
            device_id=at(dx, dy),
            device_id_type=MESH,
        )
        copy.start()
        halo.append(copy)
    for copy in local[2:]:
        copy.start()

    def exchange(send, recv, group):
        copies = []
        for d in PEERS:
            peer = step(gy, d, ny)
            copy = pltpu.make_async_remote_copy(
                src_ref=send.at[peer],
                dst_ref=recv.at[gy],
                send_sem=a2a_send.at[group, d],
                recv_sem=a2a_recv.at[group, d],
                device_id=(partner, peer),
                device_id_type=MESH,
            )
            copy.start()
            copies.append(copy)
        return copies

    def arrived(send, recv, group):
        for d in PEERS:
            source = step(gy, -d, ny)
            pltpu.make_async_remote_copy(
                src_ref=send.at[source],
                dst_ref=recv.at[source],
                send_sem=a2a_send.at[group, d],
                recv_sem=a2a_recv.at[group, d],
                device_id=(partner, source),
                device_id_type=MESH,
            ).wait_recv()
        return recv[...].reshape(TOK, C)

    row, col = iota((TOK, TOK), 0), iota((TOK, TOK), 1)
    to_zxy = jnp.where(row == (col & 7) * 16 + (col >> 3), 1.0, 0.0).astype(BF16)
    to_xyz = jnp.where(col == (row & 7) * 16 + (row >> 3), 1.0, 0.0).astype(BF16)
    eye = jnp.where(row == col, 1.0, 0.0).astype(BF16)
    head0 = jnp.where(col < 64, 1.0, 0.0).astype(BF16)
    head1 = jnp.where(col < 64, 0.0, 1.0).astype(BF16)

    def stacked(pair):
        return jnp.concatenate([pair * head0, pair * head1], axis=0)

    local[1].wait()
    cot_send[...] = nn(to_zxy, cot_own[...].reshape(TOK, C)).astype(BF16).reshape(8, 16, C)

    def near(rows, bits, x_base, y_base):
        key, query = iota((rows, TOK), 0), iota((rows, TOK), 1)
        gap_x = (key >> (3 + bits)) + x_base - ((query >> 3) & 1)
        gap_y = ((key >> 3) & ((1 << bits) - 1)) + y_base - (query & 7)
        gap_z = ((key & 7) - (query >> 4) + 2) & 7
        inside = (jnp.abs(gap_x) <= 2) & (jnp.abs(gap_y) <= 2) & (gap_z <= 4)
        return jnp.where(inside, 0.0, MASKED)

    bias1[OWN, :] = near(TOK, 3, 0, 0)
    for index, (dx, dy) in enumerate(SIDES):
        if dy == 0:
            start = 128 * (index - 5)
            bias1[start : start + 128, :] = near(128, 3, -2 * dx, 0)
        else:
            start = 384 + 32 * index
            bias1[start : start + 32, :] = near(32, 1, -2 * dx, -2 if dy == 1 else 8)

    def window_scores(part, tokens):
        values = tokens.astype(F32)
        normed = (values * inverse_rms(values)).astype(BF16)
        kv = nn(normed, win_qkv[:, C : 3 * C]).astype(BF16)
        kv1[part] = kv
        bias = jnp.concatenate([bias1[part, :], bias1[part, :]], axis=1)
        for p in range(PAIRS):
            scores1[p, part] = nt(kv[:, lanes(p)], q1[p]) + bias
            vt1[p, :, part] = nt(eye, kv[:, lanes(p, C)]).astype(BF16)
        return normed

    field_own = own[...].reshape(TOK, C)
    field_zxy = nn(to_zxy, field_own)
    normed1_zxy = (field_zxy * inverse_rms(field_zxy)).astype(BF16)
    local[2].wait()
    query1 = nn(normed1_zxy, win_qkv[:, 0:C]).astype(BF16) * 0.125
    for p in range(PAIRS):
        q1[p] = stacked(query1[:, lanes(p)])
    window_scores(OWN, field_own)
    cot_copies = exchange(cot_send, cot_recv, 0)
    for copy in local[5:7]:
        copy.wait()
    axial_out_t[...] = axial_out[...].T
    mlp_in_t[...] = mlp_in[...].T
    for copy in halo[6:]:
        copy.wait_recv()
    window_scores(AROUND, sides[...].reshape(256, C))
    tops, sums, outs = [], [], []
    for p in range(PAIRS):
        scores = scores1[p, EARLY]
        tops.append(jnp.max(scores, axis=0, keepdims=True))
        e = jnp.exp(scores - tops[p])
        scores1[p, EARLY] = e
        sums.append(jnp.sum(e, axis=0, keepdims=True))
        outs.append(diagonal(nn(vt1[p, :, EARLY], e.astype(BF16))))
    for copy in halo[:6]:
        copy.wait_recv()
    window_scores(EDGES, edges[...].reshape(192, C))
    attended, early_scale = [], []
    for p in range(PAIRS):
        scores = scores1[p, EDGES]
        top = jnp.maximum(tops[p], jnp.max(scores, axis=0, keepdims=True))
        e = jnp.exp(scores - top)
        shrink = jnp.exp(tops[p] - top)
        scale = 1.0 / (shrink * sums[p] + jnp.sum(e, axis=0, keepdims=True))
        weights = (e * scale).astype(BF16)
        weights1[p, EDGES] = weights
        early_scale.append(shrink * scale)
        early = jnp.concatenate(
            [
                outs[p][:64] * early_scale[p][:, :TOK],
                outs[p][64:] * early_scale[p][:, TOK:],
            ],
            axis=0,
        )
        ot = early + diagonal(nn(vt1[p, :, EDGES], weights))
        ot1[p] = ot
        attended.append(ot.astype(BF16).T)
    attended = jnp.concatenate(attended, axis=1)
    local[3].wait()
    s1_send[...] = (field_zxy + nn(attended, win_out[...])).astype(BF16).reshape(8, 16, C)
    s1_copies = exchange(s1_send, s1_recv, 1)

    for p in range(PAIRS):
        weights1[p, EARLY] = (scores1[p, EARLY] * early_scale[p]).astype(BF16)
        kt1[p] = nt(eye, kv1[:, lanes(p)]).astype(BF16)
    for copy in (local[4], local[7], local[8]):
        copy.wait()
    axial_qkv_t[...] = axial_qkv[...].T
    off = ((col >> 4) - (row >> 4)) & 7
    same_line = ((row ^ col) & 8) == 0
    bias2 = []
    for head in range(2 * PAIRS):
        hit = off == 0
        for j in range(3):
            hit = hit | (off == pattern[j, head])
        bias2.append(jnp.where(hit & same_line, 0.0, MASKED))

    gradient_bf = arrived(cot_send, cot_recv, 0)
    gradient = gradient_bf.astype(F32)
    d_hidden = [
        nt(gradient_bf, mlp_out[CHUNK * c : CHUNK * (c + 1), :]) for c in range(FF // CHUNK)
    ]
    stream1 = arrived(s1_send, s1_recv, 1).astype(F32)
    r2 = inverse_rms(stream1)
    triple2 = nn((stream1 * r2).astype(BF16), axial_qkv[...]).astype(BF16)
    query2 = triple2[:, 0:C] * 0.125
    q2 = [stacked(query2[:, lanes(p)]) for p in range(PAIRS)]
    weights2 = []
    attended2 = []
    for p in range(PAIRS):
        pair_bias = jnp.concatenate([bias2[2 * p], bias2[2 * p + 1]], axis=0)
        scores = nt(q2[p], triple2[:, lanes(p, C)]) + pair_bias
        e = jnp.exp(scores - jnp.max(scores, axis=1, keepdims=True))
        weights = (e * (1.0 / jnp.sum(e, axis=1, keepdims=True))).astype(BF16)
        weights2.append(weights)
        values = stacked(triple2[:, lanes(p, 2 * C)])
        attended2.append(nn(abreast(weights), values))
    attended2 = jnp.concatenate(attended2, axis=1).astype(BF16)
    stream2 = (stream1 + nn(attended2, axial_out[...])).astype(BF16).astype(F32)

    r3 = inverse_rms(stream2)
    normed3 = (stream2 * r3).astype(BF16)
    hidden = []
    back = None
    for c in range(FF // CHUNK):
        part = slice(CHUNK * c, CHUNK * (c + 1))
        a = nn(normed3, mlp_in[:, part])
        square = a * a
        t = jnp.tanh(0.7978845608028654 * (a + 0.044715 * (a * square)))
        half = 0.5 * (1.0 + t)
        hidden.append((a * half).astype(BF16))
        slope = half + (0.5 * a) * (1.0 - t * t) * (
            0.7978845608028654 + (3 * 0.044715 * 0.7978845608028654) * square
        )
        term = nn((d_hidden[c] * slope).astype(BF16), mlp_in_t[part, :])
        back = term if back is None else back + term
    grad2 = gradient + norm_back(stream2, r3, back)

    back2 = nn(grad2.astype(BF16), axial_out_t[...]).astype(BF16)
    d_query, d_key, d_value = [], [], []
    for p in range(PAIRS):
        upstream = stacked(back2[:, lanes(p)])
        keys = stacked(triple2[:, lanes(p, C)])
        weights = weights2[p].astype(F32)
        d_weights = nt(upstream, triple2[:, lanes(p, 2 * C)])
        delta = jnp.sum(weights * d_weights, axis=1, keepdims=True)
        d_scores = (weights * (d_weights - delta)).astype(BF16)
        d_query.append(nn(abreast(d_scores), keys) * 0.125)
        d_key.append(nn(d_scores.T, q2[p]))
        d_value.append(nn(weights2[p].T, upstream))
    d_triple2 = jnp.concatenate(d_query + d_key + d_value, axis=1).astype(BF16)
    grad1 = grad2 + norm_back(stream1, r2, nn(d_triple2, axial_qkv_t[...]))
    g1_send[...] = grad1.astype(BF16).reshape(8, 16, C)
    g1_copies = exchange(g1_send, g1_recv, 3)

    hidden_out = nn(jnp.concatenate(hidden, axis=1), mlp_out[...])
    lo_send[...] = (stream2 + hidden_out).astype(BF16).reshape(8, 16, C)
    lo_copies = exchange(lo_send, lo_recv, 2)
    win_out_t[...] = win_out[...].T
    win_kv_t[...] = win_qkv[:, C : 3 * C].T

    grad1_bf = arrived(g1_send, g1_recv, 3)
    back1 = nn(grad1_bf, win_out_t[...]).astype(BF16)
    back1_t = nt(win_out[...], grad1_bf).astype(BF16).astype(F32)
    upstream, delta = [], []
    for p in range(PAIRS):
        upstream.append(stacked(back1[:, lanes(p)]))
        product = ot1[p] * back1_t[lanes(p)]
        halves = [jnp.sum(product[h : h + 64], axis=0, keepdims=True) for h in (0, 64)]
        delta.append(jnp.concatenate(halves, axis=1))

    def window_back(part):
        d_scores, d_key, d_value = [], [], []
        for p in range(PAIRS):
            weights = weights1[p, part]
            d_weights = nt(kv1[part, lanes(p, C)], upstream[p])
            d_scores.append((weights.astype(F32) * (d_weights - delta[p])).astype(BF16))
            d_key.append(nn(d_scores[p], q1[p]).astype(BF16))
            d_value.append(nn(weights, upstream[p]).astype(BF16))
        d_kv = jnp.concatenate(d_key + d_value, axis=1)
        return d_scores, nn(d_kv, win_kv_t[...])

    push = []

    def send_back(index):
        dx, dy = SIDES[index]
        if dy == 0:
            rows = slice(8 * (index - 6), 8 * (index - 5))
        else:
            rows = slice(16 + 2 * index, 18 + 2 * index)
        copy = pltpu.make_async_remote_copy(
            src_ref=dn_send.at[rows],
            dst_ref=dn_recv.at[rows],
            send_sem=push_send.at[index],
            recv_sem=push_recv.at[index],
            device_id=at(-dx, -dy),
            device_id_type=MESH,
        )
        copy.start()
        push.append(copy)

    scores_edges, dn = window_back(EDGES)
    dn_send[16:28] = dn.astype(BF16).reshape(12, 16, C)
    for index in range(6):
        send_back(index)
    scores_around, dn = window_back(AROUND)
    dn_send[0:16] = dn.astype(BF16).reshape(16, 16, C)
    for index in range(6, 8):
        send_back(index)

    scores_own, d_normed = window_back(OWN)
    d_query = []
    for p in range(PAIRS):
        both = nn(kt1[p, :, EDGES], scores_edges[p]) + nn(kt1[p, :, AROUND], scores_around[p])
        both = both + nn(kt1[p, :, OWN], scores_own[p])
        d_query.append((diagonal(both) * 0.125).astype(BF16))
    d_query = nt(to_xyz, jnp.concatenate(d_query, axis=0)).astype(BF16)
    d_normed = d_normed + nt(d_query, win_qkv[:, 0:C])
    grad1_xyz = nn(to_xyz, grad1_bf)
    out_ref[...] = nn(to_xyz, arrived(lo_send, lo_recv, 2)).astype(BF16)
    for copy in push:
        copy.wait_recv()
    d_normed = d_normed + (dn_recv[0:8].astype(F32) + dn_recv[8:16].astype(F32)).reshape(TOK, C)
    first, last = [
        sum(
            dn_recv[16 + 2 * i : 18 + 2 * i].astype(F32)
            for i, (_, dy) in enumerate(SIDES)
            if dy == way
        )
        for way in (-1, 1)
    ]
    none = jnp.zeros((32, C), F32)
    rims = jnp.concatenate([first[0], none, last[0], first[1], none, last[1]], axis=0)
    field_f = own[...].reshape(TOK, C).astype(F32)
    grad_ref[...] = grad1_xyz + norm_back(field_f, inverse_rms(field_f), d_normed + rims)

    for copy in halo + cot_copies + s1_copies + lo_copies + g1_copies + push:
        copy.wait_send()


def store(out_ref, grad_ref, out_hbm, grad_hbm, sem):
    copies = [
        pltpu.make_async_copy(grad_ref, grad_hbm, sem.at[0]),
        pltpu.make_async_copy(out_ref, out_hbm, sem.at[1]),
    ]
    for copy in copies:
        copy.start()
    for copy in copies:
        copy.wait()


def shards(nx, ny, field, cotangent, *rest):
    block = (2, 4, 16, C)
    tiles = (8, 16, C)
    vmem = pltpu.VMEM
    dma = pltpu.SemaphoreType.DMA
    weights, pattern = rest[:6], rest[6]
    in_hbm = pl.BlockSpec(memory_space=pltpu.HBM)
    in_vmem = pl.BlockSpec(memory_space=pltpu.VMEM)
    results = pl.pallas_call(
        functools.partial(kernel, nx, ny),
        out_shape=(pltpu.VMEM((TOK, C), BF16), pltpu.VMEM((TOK, C), F32)),
        in_specs=[in_hbm] * 9,
        out_specs=(in_vmem, in_vmem),
        scratch_shapes=[vmem(w.shape, BF16) for w in weights]
        + [vmem((n, C), BF16) for n in (C, 2 * C, C, 3 * C, FF)]
        + [pltpu.SMEM((3, 6), jnp.int32), vmem(block, BF16)]
        + [vmem((2,) + block, BF16), vmem((6, 2, 1, 16, C), BF16)]
        + [vmem(tiles, BF16)] * 9
        + [
            vmem((28, 16, C), BF16),
            vmem((28, 16, C), BF16),
            vmem((PAIRS, KEYS, 256), BF16),
            vmem((KEYS, 2 * C), BF16),
            vmem((PAIRS, TOK, KEYS), BF16),
            vmem((PAIRS, TOK, KEYS), BF16),
            vmem((PAIRS, TOK, TOK), F32),
            vmem((PAIRS, KEYS, 256), F32),
            vmem((KEYS, TOK), F32),
            vmem((PAIRS, 256, TOK), BF16),
            dma((9,)),
            dma((8,)),
            dma((8,)),
            dma((4, 8)),
            dma((4, 8)),
            dma((8,)),
            dma((8,)),
        ],
        compiler_params=pltpu.CompilerParams(
            collective_id=0, has_side_effects=True, vmem_limit_bytes=60 * 1024 * 1024
        ),
    )(field.reshape(block), cotangent.reshape(tiles), *weights, pattern.T)
    layer_output, field_grad = pl.pallas_call(
        store,
        out_shape=(
            jax.ShapeDtypeStruct((TOK, C), BF16),
            jax.ShapeDtypeStruct((TOK, C), F32),
        ),
        in_specs=[in_vmem] * 2,
        out_specs=(in_hbm, in_hbm),
        scratch_shapes=[dma((2,))],
        compiler_params=pltpu.CompilerParams(vmem_limit_bytes=4 * 1024 * 1024),
    )(*results)
    return layer_output.reshape(field.shape), field_grad.reshape(field.shape)


def solution(mesh):
    split = P("gx", "gy", None, None)
    return jax.shard_map(
        functools.partial(shards, mesh.shape["gx"], mesh.shape["gy"]),
        mesh=mesh,
        in_specs=(split, split) + (P(),) * 7,
        out_specs=(split, split),
        check_vma=False,
    )
```

```python
import functools

import jax
import jax.numpy as jnp
from jax import lax
from jax.experimental import pallas as pl
from jax.experimental.pallas import tpu as pltpu
from jax.sharding import PartitionSpec as P

F32 = jnp.float32
BF16 = jnp.bfloat16
C = 384
FF = 1536
CHUNK = 512
PAIRS = 3
TOK = 128
KEYS = 576
OWN, EDGES, AROUND, EARLY = slice(0, 128), slice(128, 320), slice(320, 576), slice(0, 320)
OWN_LANES, AROUND_LANES, EDGES_LANES = slice(0, 128), slice(128, 384), slice(384, 576)
EPSILON = 1e-06
MASKED = -1e30
MESH = pl.DeviceIdType.MESH

SIDES = [(1, 1), (-1, -1), (1, -1), (-1, 1), (0, 1), (0, -1), (1, 0), (-1, 0)]
PEERS = [2, 6, 1, 3, 5, 7, 0, 4]


def nn(a, b):
    return lax.dot_general(a, b, (((1,), (0,)), ((), ())), preferred_element_type=F32)


def nt(a, b):
    return lax.dot_general(a, b, (((1,), (1,)), ((), ())), preferred_element_type=F32)


def inverse_rms(v):
    return lax.rsqrt(jnp.sum(v * v, axis=-1, keepdims=True) * (1.0 / C) + EPSILON)


def norm_back(v, r, upstream):
    inner = jnp.sum(v * upstream, axis=-1, keepdims=True) * (1.0 / C)
    return r * upstream - v * (r * r * r * inner)


def iota(shape, dim):
    return lax.broadcasted_iota(jnp.int32, shape, dim)


def diagonal(both):
    return jnp.concatenate([both[:64, :128], both[64:, 128:]], axis=0)


def abreast(both):
    return jnp.concatenate([both[:TOK], both[TOK:]], axis=1)


def lanes(p, base=0):
    return slice(base + 128 * p, base + 128 * (p + 1))


def kernel(
    nx,
    ny,
    field,
    cot,
    win_qkv_h,
    win_out_h,
    axial_qkv_h,
    axial_out_h,
    mlp_in_h,
    mlp_out_h,
    pattern_h,
    out_ref,
    grad_ref,
    win_qkv,
    win_out,
    axial_qkv,
    axial_out,
    mlp_in,
    mlp_out,
    win_out_t,
    win_kv_t,
    axial_out_t,
    axial_qkv_t,
    mlp_in_t,
    pattern,
    own,
    sides,
    edges,
    cot_own,
    cot_send,
    cot_recv,
    s1_send,
    s1_recv,
    lo_send,
    lo_recv,
    g1_send,
    g1_recv,
    dn_send,
    dn_recv,
    weights1,
    kv1,
    kt1,
    vt1,
    ot1,
    scores1,
    bias1,
    q1,
    local_sem,
    halo_send,
    halo_recv,
    a2a_send,
    a2a_recv,
    push_send,
    push_recv,
):
    gx = lax.axis_index("gx")
    gy = lax.axis_index("gy")

    partner = gx + 2 - 4 * ((gx >> 1) & 1)

    def step(index, by, size):
        moved = index + by
        if by > 0:
            return jnp.where(moved >= size, moved - size, moved)
        return jnp.where(moved < 0, moved + size, moved) if by else index

    def at(dx, dy):
        return (step(gx, dx, nx), step(gy, dy, ny))

    barrier = pltpu.get_barrier_semaphore()
    greeted = [at(dx, dy) for dx, dy in SIDES] + [(partner, step(gy, d, ny)) for d in PEERS]
    for device in greeted:
        pl.semaphore_signal(barrier, inc=1, device_id=device, device_id_type=MESH)

    local = [
        pltpu.make_async_copy(src, dst, local_sem.at[index])
        for index, (src, dst) in enumerate(
            [
                (field, own),
                (cot, cot_own),
                (win_qkv_h, win_qkv),
                (win_out_h, win_out),
                (axial_qkv_h, axial_qkv),
                (axial_out_h, axial_out),
                (mlp_in_h, mlp_in),
                (mlp_out_h, mlp_out),
                (pattern_h, pattern),
            ]
        )
    ]
    for copy in local[:2]:
        copy.start()
    local[0].wait()
    pl.semaphore_wait(barrier, len(greeted))

    own_y = {0: slice(0, 4), 1: slice(3, 4), -1: slice(0, 1)}
    halo = []
    for index, (dx, dy) in enumerate(SIDES):
        copy = pltpu.make_async_remote_copy(
            src_ref=own.at[:, own_y[dy]],
            dst_ref=sides.at[index - 6] if dy == 0 else edges.at[index],
            send_sem=halo_send.at[index],
            recv_sem=halo_recv.at[index],
            device_id=at(dx, dy),
            device_id_type=MESH,
        )
        copy.start()
        halo.append(copy)
    for copy in local[2:]:
        copy.start()

    def exchange(send, recv, group):
        copies = []
        for d in PEERS:
            peer = step(gy, d, ny)
            copy = pltpu.make_async_remote_copy(
                src_ref=send.at[peer],
                dst_ref=recv.at[gy],
                send_sem=a2a_send.at[group, d],
                recv_sem=a2a_recv.at[group, d],
                device_id=(partner, peer),
                device_id_type=MESH,
            )
            copy.start()
            copies.append(copy)
        return copies

    def arrived(send, recv, group):
        for d in PEERS:
            source = step(gy, -d, ny)
            pltpu.make_async_remote_copy(
                src_ref=send.at[source],
                dst_ref=recv.at[source],
                send_sem=a2a_send.at[group, d],
                recv_sem=a2a_recv.at[group, d],
                device_id=(partner, source),
                device_id_type=MESH,
            ).wait_recv()
        return recv[...].reshape(TOK, C)

    row, col = iota((TOK, TOK), 0), iota((TOK, TOK), 1)
    to_zxy = jnp.where(row == (col & 7) * 16 + (col >> 3), 1.0, 0.0).astype(BF16)
    to_xyz = jnp.where(col == (row & 7) * 16 + (row >> 3), 1.0, 0.0).astype(BF16)
    eye = jnp.where(row == col, 1.0, 0.0).astype(BF16)
    head0 = jnp.where(col < 64, 1.0, 0.0).astype(BF16)
    head1 = jnp.where(col < 64, 0.0, 1.0).astype(BF16)

    def stacked(pair):
        return jnp.concatenate([pair * head0, pair * head1], axis=0)

    local[1].wait()
    cot_send[...] = nn(to_zxy, cot_own[...].reshape(TOK, C)).astype(BF16).reshape(8, 16, C)

    def near(rows, bits, x_base, y_base):
        key, query = iota((rows, TOK), 0), iota((rows, TOK), 1)
        gap_x = (key >> (3 + bits)) + x_base - ((query >> 3) & 1)
        gap_y = ((key >> 3) & ((1 << bits) - 1)) + y_base - (query & 7)
        gap_z = ((key & 7) - (query >> 4) + 2) & 7
        inside = (jnp.abs(gap_x) <= 2) & (jnp.abs(gap_y) <= 2) & (gap_z <= 4)
        return jnp.where(inside, 0.0, MASKED)

    bias1[OWN, :] = near(TOK, 3, 0, 0)
    for index, (dx, dy) in enumerate(SIDES):
        if dy == 0:
            start = 320 + 128 * (index - 6)
            bias1[start : start + 128, :] = near(128, 3, -2 * dx, 0)
        else:
            start = 128 + 32 * index
            bias1[start : start + 32, :] = near(32, 1, -2 * dx, -2 if dy == 1 else 8)

    def window_scores(part, part_lanes, tokens):
        values = tokens.astype(F32)
        normed = (values * inverse_rms(values)).astype(BF16)
        kv = nn(normed, win_qkv[:, C : 3 * C]).astype(BF16)
        kv1[part] = kv
        bias = jnp.concatenate([bias1[part, :], bias1[part, :]], axis=1)
        for p in range(PAIRS):
            scores1[p, part] = nt(kv[:, lanes(p)], q1[p]) + bias
            vt1[p, :, part_lanes] = nt(eye, kv[:, lanes(p, C)]).astype(BF16)

    field_own = own[...].reshape(TOK, C)
    field_zxy = nn(to_zxy, field_own)
    normed1_zxy = (field_zxy * inverse_rms(field_zxy)).astype(BF16)
    local[2].wait()
    query1 = nn(normed1_zxy, win_qkv[:, 0:C]).astype(BF16) * 0.125
    for p in range(PAIRS):
        q1[p] = stacked(query1[:, lanes(p)])
    window_scores(OWN, OWN_LANES, field_own)
    cot_copies = exchange(cot_send, cot_recv, 0)
    for copy in local[5:7]:
        copy.wait()
    axial_out_t[...] = axial_out[...].T
    mlp_in_t[...] = mlp_in[...].T
    for copy in halo[:6]:
        copy.wait_recv()
    window_scores(EDGES, EDGES_LANES, edges[...].reshape(192, C))
    tops, sums, outs = [], [], []
    for p in range(PAIRS):
        scores = scores1[p, EARLY]
        tops.append(jnp.max(scores, axis=0, keepdims=True))
        e = jnp.exp(scores - tops[p])
        scores1[p, EARLY] = e
        sums.append(jnp.sum(e, axis=0, keepdims=True))
        e = e.astype(BF16)
        out = nn(vt1[p, :, OWN_LANES], e[OWN]) + nn(vt1[p, :, EDGES_LANES], e[EDGES])
        outs.append(diagonal(out))
    for copy in halo[6:]:
        copy.wait_recv()
    window_scores(AROUND, AROUND_LANES, sides[...].reshape(256, C))
    attended, early_scale = [], []
    for p in range(PAIRS):
        scores = scores1[p, AROUND]
        top = jnp.maximum(tops[p], jnp.max(scores, axis=0, keepdims=True))
        e = jnp.exp(scores - top)
        shrink = jnp.exp(tops[p] - top)
        scale = 1.0 / (shrink * sums[p] + jnp.sum(e, axis=0, keepdims=True))
        weights = (e * scale).astype(BF16)
        weights1[p, AROUND] = weights
        early_scale.append(shrink * scale)
        early = jnp.concatenate(
            [
                outs[p][:64] * early_scale[p][:, :TOK],
                outs[p][64:] * early_scale[p][:, TOK:],
            ],
            axis=0,
        )
        ot = early + diagonal(nn(vt1[p, :, AROUND_LANES], weights))
        ot1[p] = ot
        attended.append(ot.astype(BF16).T)
    attended = jnp.concatenate(attended, axis=1)
    local[3].wait()
    s1_send[...] = (field_zxy + nn(attended, win_out[...])).astype(BF16).reshape(8, 16, C)
    s1_copies = exchange(s1_send, s1_recv, 1)

    for p in range(PAIRS):
        weights1[p, EARLY] = (scores1[p, EARLY] * early_scale[p]).astype(BF16)
        for part, part_lanes in (
            (OWN, OWN_LANES),
            (AROUND, AROUND_LANES),
            (EDGES, EDGES_LANES),
        ):
            kt1[p, :, part_lanes] = nt(eye, kv1[part, lanes(p)]).astype(BF16)
    for copy in (local[4], local[7], local[8]):
        copy.wait()
    axial_qkv_t[...] = axial_qkv[...].T
    off = ((col >> 4) - (row >> 4)) & 7
    same_line = ((row ^ col) & 8) == 0
    bias2 = []
    for head in range(2 * PAIRS):
        hit = off == 0
        for j in range(3):
            hit = hit | (off == pattern[j, head])
        bias2.append(jnp.where(hit & same_line, 0.0, MASKED))

    gradient_bf = arrived(cot_send, cot_recv, 0)
    gradient = gradient_bf.astype(F32)
    d_hidden = nt(gradient_bf, mlp_out[...])
    stream1 = arrived(s1_send, s1_recv, 1).astype(F32)
    r2 = inverse_rms(stream1)
    triple2 = nn((stream1 * r2).astype(BF16), axial_qkv[...]).astype(BF16)
    query2 = triple2[:, 0:C] * 0.125
    q2 = [stacked(query2[:, lanes(p)]) for p in range(PAIRS)]
    weights2 = []
    attended2 = []
    for p in range(PAIRS):
        pair_bias = jnp.concatenate([bias2[2 * p], bias2[2 * p + 1]], axis=0)
        scores = nt(q2[p], triple2[:, lanes(p, C)]) + pair_bias
        e = jnp.exp(scores - jnp.max(scores, axis=1, keepdims=True))
        weights = (e * (1.0 / jnp.sum(e, axis=1, keepdims=True))).astype(BF16)
        weights2.append(weights)
        values = stacked(triple2[:, lanes(p, 2 * C)])
        attended2.append(nn(abreast(weights), values))
    attended2 = jnp.concatenate(attended2, axis=1).astype(BF16)
    stream2 = (stream1 + nn(attended2, axial_out[...])).astype(BF16).astype(F32)

    r3 = inverse_rms(stream2)
    normed3 = (stream2 * r3).astype(BF16)
    hidden, d_inner = [], []
    for c in range(FF // CHUNK):
        part = slice(CHUNK * c, CHUNK * (c + 1))
        a = nn(normed3, mlp_in[:, part])
        square = a * a
        t = jnp.tanh(a * (0.7978845608028654 + (0.044715 * 0.7978845608028654) * square))
        half = 0.5 + 0.5 * t
        hidden.append((a * half).astype(BF16))
        steep = a * (2 * 0.7978845608028654 + (6 * 0.044715 * 0.7978845608028654) * square)
        slope = half + (half - half * half) * steep
        d_inner.append((d_hidden[:, part] * slope).astype(BF16))
    back = nn(jnp.concatenate(d_inner, axis=1), mlp_in_t[...])
    grad2 = gradient + norm_back(stream2, r3, back)

    back2 = nn(grad2.astype(BF16), axial_out_t[...]).astype(BF16)
    d_query, d_key, d_value = [], [], []
    for p in range(PAIRS):
        upstream = stacked(back2[:, lanes(p)])
        keys = stacked(triple2[:, lanes(p, C)])
        weights = weights2[p].astype(F32)
        d_weights = nt(upstream, triple2[:, lanes(p, 2 * C)])
        delta = jnp.sum(weights * d_weights, axis=1, keepdims=True)
        d_scores = (weights * (d_weights - delta)).astype(BF16)
        d_query.append(nn(abreast(d_scores), keys) * 0.125)
        d_key.append(nn(d_scores.T, q2[p]))
        d_value.append(nn(weights2[p].T, upstream))
    d_triple2 = jnp.concatenate(d_query + d_key + d_value, axis=1).astype(BF16)
    grad1 = grad2 + norm_back(stream1, r2, nn(d_triple2, axial_qkv_t[...]))
    g1_send[...] = grad1.astype(BF16).reshape(8, 16, C)
    g1_copies = exchange(g1_send, g1_recv, 3)

    hidden_out = nn(jnp.concatenate(hidden, axis=1), mlp_out[...])
    lo_send[...] = (stream2 + hidden_out).astype(BF16).reshape(8, 16, C)
    lo_copies = exchange(lo_send, lo_recv, 2)
    win_out_t[...] = win_out[...].T
    win_kv_t[0:C] = win_qkv[:, 2 * C : 3 * C].T
    win_kv_t[C : 2 * C] = win_qkv[:, C : 2 * C].T

    grad1_bf = arrived(g1_send, g1_recv, 3)
    back1 = nn(grad1_bf, win_out_t[...]).astype(BF16)
    back1_t = nt(win_out[...], grad1_bf).astype(BF16).astype(F32)
    upstream, delta = [], []
    for p in range(PAIRS):
        upstream.append(stacked(back1[:, lanes(p)]))
        product = ot1[p] * back1_t[lanes(p)]
        halves = [jnp.sum(product[h : h + 64], axis=0, keepdims=True) for h in (0, 64)]
        delta.append(jnp.concatenate(halves, axis=1))

    def window_back(part):
        d_scores, d_key, d_value = [], [], []
        for p in range(PAIRS):
            weights = weights1[p, part]
            d_weights = nt(kv1[part, lanes(p, C)], upstream[p])
            d_scores.append((weights.astype(F32) * (d_weights - delta[p])).astype(BF16))
            d_key.append(nn(d_scores[p], q1[p]).astype(BF16))
            d_value.append(nn(weights, upstream[p]).astype(BF16))
        d_kv = jnp.concatenate(d_value + d_key, axis=1)
        return d_scores, nn(d_kv, win_kv_t[...])

    push = []

    def send_back(index):
        dx, dy = SIDES[index]
        if dy == 0:
            rows = slice(8 * (index - 6), 8 * (index - 5))
        else:
            rows = slice(16 + 2 * index, 18 + 2 * index)
        copy = pltpu.make_async_remote_copy(
            src_ref=dn_send.at[rows],
            dst_ref=dn_recv.at[rows],
            send_sem=push_send.at[index],
            recv_sem=push_recv.at[index],
            device_id=at(-dx, -dy),
            device_id_type=MESH,
        )
        copy.start()
        push.append(copy)

    scores_edges, dn = window_back(EDGES)
    dn_send[16:28] = dn.astype(BF16).reshape(12, 16, C)
    for index in range(6):
        send_back(index)
    scores_around, dn = window_back(AROUND)
    dn_send[0:16] = dn.astype(BF16).reshape(16, 16, C)
    for index in range(6, 8):
        send_back(index)

    scores_own, d_normed = window_back(OWN)
    d_query = []
    for p in range(PAIRS):
        both = nn(kt1[p, :, EDGES_LANES], scores_edges[p])
        both = both + nn(kt1[p, :, AROUND_LANES], scores_around[p])
        both = both + nn(kt1[p, :, OWN_LANES], scores_own[p])
        d_query.append((diagonal(both) * 0.125).astype(BF16))
    d_query = nt(to_xyz, jnp.concatenate(d_query, axis=0)).astype(BF16)
    d_normed = d_normed + nt(d_query, win_qkv[:, 0:C])
    grad1_xyz = nn(to_xyz, grad1_bf)
    out_ref[...] = nn(to_xyz, arrived(lo_send, lo_recv, 2)).astype(BF16)
    for copy in push:
        copy.wait_recv()
    d_normed = d_normed + (dn_recv[0:8].astype(F32) + dn_recv[8:16].astype(F32)).reshape(TOK, C)
    first, last = [
        sum(
            dn_recv[16 + 2 * i : 18 + 2 * i].astype(F32)
            for i, (_, dy) in enumerate(SIDES)
            if dy == way
        )
        for way in (-1, 1)
    ]
    none = jnp.zeros((32, C), F32)
    rims = jnp.concatenate([first[0], none, last[0], first[1], none, last[1]], axis=0)
    field_f = own[...].reshape(TOK, C).astype(F32)
    grad_ref[...] = grad1_xyz + norm_back(field_f, inverse_rms(field_f), d_normed + rims)

    for copy in halo + cot_copies + s1_copies + lo_copies + g1_copies + push:
        copy.wait_send()


def store(out_ref, grad_ref, out_hbm, grad_hbm, sem):
    copies = [
        pltpu.make_async_copy(grad_ref, grad_hbm, sem.at[0]),
        pltpu.make_async_copy(out_ref, out_hbm, sem.at[1]),
    ]
    for copy in copies:
        copy.start()
    for copy in copies:
        copy.wait()


def shards(nx, ny, field, cotangent, *rest):
    block = (2, 4, 16, C)
    tiles = (8, 16, C)
    vmem = pltpu.VMEM
    dma = pltpu.SemaphoreType.DMA
    weights, pattern = rest[:6], rest[6]
    in_hbm = pl.BlockSpec(memory_space=pltpu.HBM)
    in_vmem = pl.BlockSpec(memory_space=pltpu.VMEM)
    results = pl.pallas_call(
        functools.partial(kernel, nx, ny),
        out_shape=(pltpu.VMEM((TOK, C), BF16), pltpu.VMEM((TOK, C), F32)),
        in_specs=[in_hbm] * 9,
        out_specs=(in_vmem, in_vmem),
        scratch_shapes=[vmem(w.shape, BF16) for w in weights]
        + [vmem((n, C), BF16) for n in (C, 2 * C, C, 3 * C, FF)]
        + [pltpu.SMEM((3, 6), jnp.int32), vmem(block, BF16)]
        + [vmem((2,) + block, BF16), vmem((6, 2, 1, 16, C), BF16)]
        + [vmem(tiles, BF16)] * 9
        + [
            vmem((28, 16, C), BF16),
            vmem((28, 16, C), BF16),
            vmem((PAIRS, KEYS, 256), BF16),
            vmem((KEYS, 2 * C), BF16),
            vmem((PAIRS, TOK, KEYS), BF16),
            vmem((PAIRS, TOK, KEYS), BF16),
            vmem((PAIRS, TOK, TOK), F32),
            vmem((PAIRS, KEYS, 256), F32),
            vmem((KEYS, TOK), F32),
            vmem((PAIRS, 256, TOK), BF16),
            dma((9,)),
            dma((8,)),
            dma((8,)),
            dma((4, 8)),
            dma((4, 8)),
            dma((8,)),
            dma((8,)),
        ],
        compiler_params=pltpu.CompilerParams(
            collective_id=0, has_side_effects=True, vmem_limit_bytes=60 * 1024 * 1024
        ),
    )(field.reshape(block), cotangent.reshape(tiles), *weights, pattern.T)
    layer_output, field_grad = pl.pallas_call(
        store,
        out_shape=(
            jax.ShapeDtypeStruct((TOK, C), BF16),
            jax.ShapeDtypeStruct((TOK, C), F32),
        ),
        in_specs=[in_vmem] * 2,
        out_specs=(in_hbm, in_hbm),
        scratch_shapes=[dma((2,))],
        compiler_params=pltpu.CompilerParams(vmem_limit_bytes=4 * 1024 * 1024),
    )(*results)
    return layer_output.reshape(field.shape), field_grad.reshape(field.shape)


def solution(mesh):
    split = P("gx", "gy", None, None)
    return jax.shard_map(
        functools.partial(shards, mesh.shape["gx"], mesh.shape["gy"]),
        mesh=mesh,
        in_specs=(split, split) + (P(),) * 7,
        out_specs=(split, split),
        check_vma=False,
    )
```

```python
import functools

import jax
import jax.numpy as jnp
from jax import lax
from jax.experimental import pallas as pl
from jax.experimental.pallas import tpu as pltpu
from jax.sharding import PartitionSpec as P

F32 = jnp.float32
BF16 = jnp.bfloat16
C = 384
FF = 1536
CHUNK = 512
PAIRS = 3
TOK = 128
KEYS = 576
OWN, AROUND, EARLY, EDGES = slice(0, 128), slice(128, 384), slice(0, 384), slice(384, 576)
EPSILON = 1e-06
MASKED = -1e30
MESH = pl.DeviceIdType.MESH

SIDES = [(1, 1), (-1, -1), (1, -1), (-1, 1), (0, 1), (0, -1), (1, 0), (-1, 0)]
PEERS = [2, 6, 1, 3, 5, 7, 0, 4]


def nn(a, b):
    return lax.dot_general(a, b, (((1,), (0,)), ((), ())), preferred_element_type=F32)


def nt(a, b):
    return lax.dot_general(a, b, (((1,), (1,)), ((), ())), preferred_element_type=F32)


def inverse_rms(v):
    return lax.rsqrt(jnp.sum(v * v, axis=-1, keepdims=True) * (1.0 / C) + EPSILON)


def norm_back(v, r, upstream):
    inner = jnp.sum(v * upstream, axis=-1, keepdims=True) * (1.0 / C)
    return r * upstream - v * (r * r * r * inner)


def iota(shape, dim):
    return lax.broadcasted_iota(jnp.int32, shape, dim)


def diagonal(both):
    return jnp.concatenate([both[:64, :128], both[64:, 128:]], axis=0)


def abreast(both):
    return jnp.concatenate([both[:TOK], both[TOK:]], axis=1)


def lanes(p, base=0):
    return slice(base + 128 * p, base + 128 * (p + 1))


def kernel(
    nx,
    ny,
    field,
    cot,
    win_qkv_h,
    win_out_h,
    axial_qkv_h,
    axial_out_h,
    mlp_in_h,
    mlp_out_h,
    pattern_h,
    out_ref,
    grad_ref,
    win_qkv,
    win_out,
    axial_qkv,
    axial_out,
    mlp_in,
    mlp_out,
    win_out_t,
    win_kv_t,
    axial_out_t,
    axial_qkv_t,
    mlp_in_t,
    pattern,
    own,
    sides,
    edges,
    cot_own,
    cot_send,
    cot_recv,
    s1_send,
    s1_recv,
    lo_send,
    lo_recv,
    g1_send,
    g1_recv,
    dn_send,
    dn_recv,
    weights1,
    kv1,
    kt1,
    vt1,
    ot1,
    scores1,
    bias1,
    q1,
    local_sem,
    halo_send,
    halo_recv,
    a2a_send,
    a2a_recv,
    push_send,
    push_recv,
):
    gx = lax.axis_index("gx")
    gy = lax.axis_index("gy")

    partner = gx + 2 - 4 * ((gx >> 1) & 1)

    def step(index, by, size):
        moved = index + by
        if by > 0:
            return jnp.where(moved >= size, moved - size, moved)
        return jnp.where(moved < 0, moved + size, moved) if by else index

    def at(dx, dy):
        return (step(gx, dx, nx), step(gy, dy, ny))

    barrier = pltpu.get_barrier_semaphore()
    greeted = [at(dx, dy) for dx, dy in SIDES] + [(partner, step(gy, d, ny)) for d in PEERS]
    for device in greeted:
        pl.semaphore_signal(barrier, inc=1, device_id=device, device_id_type=MESH)

    local = [
        pltpu.make_async_copy(src, dst, local_sem.at[index])
        for index, (src, dst) in enumerate(
            [
                (field, own),
                (cot, cot_own),
                (win_qkv_h, win_qkv),
                (win_out_h, win_out),
                (axial_qkv_h, axial_qkv),
                (axial_out_h, axial_out),
                (mlp_in_h, mlp_in),
                (mlp_out_h, mlp_out),
                (pattern_h, pattern),
            ]
        )
    ]
    for copy in local[:2]:
        copy.start()
    local[0].wait()
    pl.semaphore_wait(barrier, len(greeted))

    own_y = {0: slice(0, 4), 1: slice(3, 4), -1: slice(0, 1)}
    halo = []
    for index, (dx, dy) in enumerate(SIDES):
        copy = pltpu.make_async_remote_copy(
            src_ref=own.at[:, own_y[dy]],
            dst_ref=sides.at[index - 6] if dy == 0 else edges.at[index],
            send_sem=halo_send.at[index],
            recv_sem=halo_recv.at[index],
            device_id=at(dx, dy),
            device_id_type=MESH,
        )
        halo.append(copy)
    for copy in halo[:6]:
        copy.start()
    for copy in local[2:]:
        copy.start()

    def exchange(send, recv, group):
        copies = []
        for d in PEERS:
            peer = step(gy, d, ny)
            copy = pltpu.make_async_remote_copy(
                src_ref=send.at[peer],
                dst_ref=recv.at[gy],
                send_sem=a2a_send.at[group, d],
                recv_sem=a2a_recv.at[group, d],
                device_id=(partner, peer),
                device_id_type=MESH,
            )
            copy.start()
            copies.append(copy)
        return copies

    def arrived(send, recv, group):
        for d in PEERS:
            source = step(gy, -d, ny)
            pltpu.make_async_remote_copy(
                src_ref=send.at[source],
                dst_ref=recv.at[source],
                send_sem=a2a_send.at[group, d],
                recv_sem=a2a_recv.at[group, d],
                device_id=(partner, source),
                device_id_type=MESH,
            ).wait_recv()
        return recv[...].reshape(TOK, C)

    row, col = iota((TOK, TOK), 0), iota((TOK, TOK), 1)
    to_zxy = jnp.where(row == (col & 7) * 16 + (col >> 3), 1.0, 0.0).astype(BF16)
    to_xyz = jnp.where(col == (row & 7) * 16 + (row >> 3), 1.0, 0.0).astype(BF16)
    eye = jnp.where(row == col, 1.0, 0.0).astype(BF16)
    head0 = jnp.where(col < 64, 1.0, 0.0).astype(BF16)
    head1 = jnp.where(col < 64, 0.0, 1.0).astype(BF16)

    def stacked(pair):
        return jnp.concatenate([pair * head0, pair * head1], axis=0)

    local[1].wait()
    cot_send[...] = nn(to_zxy, cot_own[...].reshape(TOK, C)).astype(BF16).reshape(8, 16, C)

    def near(rows, bits, x_base, y_base):
        key, query = iota((rows, TOK), 0), iota((rows, TOK), 1)
        gap_x = (key >> (3 + bits)) + x_base - ((query >> 3) & 1)
        gap_y = ((key >> 3) & ((1 << bits) - 1)) + y_base - (query & 7)
        gap_z = ((key & 7) - (query >> 4) + 2) & 7
        inside = (jnp.abs(gap_x) <= 2) & (jnp.abs(gap_y) <= 2) & (gap_z <= 4)
        return jnp.where(inside, 0.0, MASKED)

    bias1[OWN, :] = near(TOK, 3, 0, 0)
    for index, (dx, dy) in enumerate(SIDES):
        if dy == 0:
            start = 128 * (index - 5)
            bias1[start : start + 128, :] = near(128, 3, -2 * dx, 0)
        else:
            start = 384 + 32 * index
            bias1[start : start + 32, :] = near(32, 1, -2 * dx, -2 if dy == 1 else 8)

    for copy in halo[6:]:
        copy.start()

    def window_scores(part, tokens):
        values = tokens.astype(F32)
        normed = (values * inverse_rms(values)).astype(BF16)
        kv = nn(normed, win_qkv[:, C : 3 * C]).astype(BF16)
        kv1[part] = kv
        bias = jnp.concatenate([bias1[part, :], bias1[part, :]], axis=1)
        for p in range(PAIRS):
            scores1[p, part] = nt(kv[:, lanes(p)], q1[p]) + bias
            vt1[p, :, part] = nt(eye, kv[:, lanes(p, C)]).astype(BF16)
        return normed

    field_own = own[...].reshape(TOK, C)
    field_zxy = nn(to_zxy, field_own)
    normed1_zxy = (field_zxy * inverse_rms(field_zxy)).astype(BF16)
    local[2].wait()
    query1 = nn(normed1_zxy, win_qkv[:, 0:C]).astype(BF16) * 0.125
    for p in range(PAIRS):
        q1[p] = stacked(query1[:, lanes(p)])
    window_scores(OWN, field_own)
    for copy in local[5:7]:
        copy.wait()
    axial_out_t[...] = axial_out[...].T
    mlp_in_t[...] = mlp_in[...].T
    for copy in halo[6:]:
        copy.wait_recv()
    window_scores(AROUND, sides[...].reshape(256, C))
    tops, sums, outs = [], [], []
    for p in range(PAIRS):
        scores = scores1[p, EARLY]
        tops.append(jnp.max(scores, axis=0, keepdims=True))
        e = jnp.exp(scores - tops[p])
        scores1[p, EARLY] = e
        sums.append(jnp.sum(e, axis=0, keepdims=True))
        outs.append(diagonal(nn(vt1[p, :, EARLY], e.astype(BF16))))
    for copy in halo[:6]:
        copy.wait_recv()
    cot_copies = exchange(cot_send, cot_recv, 0)
    window_scores(EDGES, edges[...].reshape(192, C))
    attended, early_scale = [], []
    for p in range(PAIRS):
        scores = scores1[p, EDGES]
        top = jnp.maximum(tops[p], jnp.max(scores, axis=0, keepdims=True))
        e = jnp.exp(scores - top)
        shrink = jnp.exp(tops[p] - top)
        scale = 1.0 / (shrink * sums[p] + jnp.sum(e, axis=0, keepdims=True))
        weights = (e * scale).astype(BF16)
        weights1[p, EDGES] = weights
        early_scale.append(shrink * scale)
        early = jnp.concatenate(
            [
                outs[p][:64] * early_scale[p][:, :TOK],
                outs[p][64:] * early_scale[p][:, TOK:],
            ],
            axis=0,
        )
        ot = early + diagonal(nn(vt1[p, :, EDGES], weights))
        ot1[p] = ot
        attended.append(ot.astype(BF16).T)
    attended = jnp.concatenate(attended, axis=1)
    local[3].wait()
    s1_send[...] = (field_zxy + nn(attended, win_out[...])).astype(BF16).reshape(8, 16, C)
    s1_copies = exchange(s1_send, s1_recv, 1)

    for p in range(PAIRS):
        weights1[p, EARLY] = (scores1[p, EARLY] * early_scale[p]).astype(BF16)
        kt1[p] = nt(eye, kv1[:, lanes(p)]).astype(BF16)
    for copy in (local[4], local[7], local[8]):
        copy.wait()
    axial_qkv_t[...] = axial_qkv[...].T
    off = ((col >> 4) - (row >> 4)) & 7
    same_line = ((row ^ col) & 8) == 0
    bias2 = []
    for head in range(2 * PAIRS):
        hit = off == 0
        for j in range(3):
            hit = hit | (off == pattern[j, head])
        bias2.append(jnp.where(hit & same_line, 0.0, MASKED))

    gradient_bf = arrived(cot_send, cot_recv, 0)
    gradient = gradient_bf.astype(F32)
    d_hidden = nt(gradient_bf, mlp_out[...])
    stream1 = arrived(s1_send, s1_recv, 1).astype(F32)
    r2 = inverse_rms(stream1)
    triple2 = nn((stream1 * r2).astype(BF16), axial_qkv[...]).astype(BF16)
    query2 = triple2[:, 0:C] * 0.125
    q2 = [stacked(query2[:, lanes(p)]) for p in range(PAIRS)]
    weights2 = []
    attended2 = []
    for p in range(PAIRS):
        pair_bias = jnp.concatenate([bias2[2 * p], bias2[2 * p + 1]], axis=0)
        scores = nt(q2[p], triple2[:, lanes(p, C)]) + pair_bias
        e = jnp.exp(scores - jnp.max(scores, axis=1, keepdims=True))
        weights = (e * (1.0 / jnp.sum(e, axis=1, keepdims=True))).astype(BF16)
        weights2.append(weights)
        values = stacked(triple2[:, lanes(p, 2 * C)])
        attended2.append(nn(abreast(weights), values))
    attended2 = jnp.concatenate(attended2, axis=1).astype(BF16)
    stream2 = (stream1 + nn(attended2, axial_out[...])).astype(BF16).astype(F32)

    r3 = inverse_rms(stream2)
    normed3 = (stream2 * r3).astype(BF16)
    hidden, d_inner = [], []
    for c in range(FF // CHUNK):
        part = slice(CHUNK * c, CHUNK * (c + 1))
        a = nn(normed3, mlp_in[:, part])
        square = a * a
        t = jnp.tanh(a * (0.7978845608028654 + (0.044715 * 0.7978845608028654) * square))
        half = 0.5 + 0.5 * t
        hidden.append((a * half).astype(BF16))
        steep = a * (2 * 0.7978845608028654 + (6 * 0.044715 * 0.7978845608028654) * square)
        slope = half + (half - half * half) * steep
        d_inner.append((d_hidden[:, part] * slope).astype(BF16))
    back = nn(jnp.concatenate(d_inner, axis=1), mlp_in_t[...])
    grad2 = gradient + norm_back(stream2, r3, back)

    back2 = nn(grad2.astype(BF16), axial_out_t[...]).astype(BF16)
    d_query, d_key, d_value = [], [], []
    for p in range(PAIRS):
        upstream = stacked(back2[:, lanes(p)])
        keys = stacked(triple2[:, lanes(p, C)])
        weights = weights2[p].astype(F32)
        d_weights = nt(upstream, triple2[:, lanes(p, 2 * C)])
        delta = jnp.sum(weights * d_weights, axis=1, keepdims=True)
        d_scores = (weights * (d_weights - delta)).astype(BF16)
        d_query.append(nn(abreast(d_scores), keys) * 0.125)
        d_key.append(nn(d_scores.T, q2[p]))
        d_value.append(nn(weights2[p].T, upstream))
    d_triple2 = jnp.concatenate(d_query + d_key + d_value, axis=1).astype(BF16)
    grad1 = grad2 + norm_back(stream1, r2, nn(d_triple2, axial_qkv_t[...]))
    g1_send[...] = grad1.astype(BF16).reshape(8, 16, C)
    g1_copies = exchange(g1_send, g1_recv, 3)

    hidden_out = nn(jnp.concatenate(hidden, axis=1), mlp_out[...])
    lo_send[...] = (stream2 + hidden_out).astype(BF16).reshape(8, 16, C)
    win_out_t[...] = win_out[...].T
    win_kv_t[0:C] = win_qkv[:, 2 * C : 3 * C].T
    win_kv_t[C : 2 * C] = win_qkv[:, C : 2 * C].T

    grad1_bf = arrived(g1_send, g1_recv, 3)
    lo_copies = exchange(lo_send, lo_recv, 2)
    back1 = nn(grad1_bf, win_out_t[...]).astype(BF16)
    back1_t = nt(win_out[...], grad1_bf).astype(BF16).astype(F32)
    upstream, delta = [], []
    for p in range(PAIRS):
        upstream.append(stacked(back1[:, lanes(p)]))
        product = ot1[p] * back1_t[lanes(p)]
        halves = [jnp.sum(product[h : h + 64], axis=0, keepdims=True) for h in (0, 64)]
        delta.append(jnp.concatenate(halves, axis=1))

    def window_back(part):
        d_scores, d_key, d_value = [], [], []
        for p in range(PAIRS):
            weights = weights1[p, part]
            d_weights = nt(kv1[part, lanes(p, C)], upstream[p])
            d_scores.append((weights.astype(F32) * (d_weights - delta[p])).astype(BF16))
            d_key.append(nn(d_scores[p], q1[p]).astype(BF16))
            d_value.append(nn(weights, upstream[p]).astype(BF16))
        d_kv = jnp.concatenate(d_value + d_key, axis=1)
        return d_scores, nn(d_kv, win_kv_t[...])

    push = []

    def send_back(index):
        dx, dy = SIDES[index]
        if dy == 0:
            rows = slice(8 * (index - 6), 8 * (index - 5))
        else:
            rows = slice(16 + 2 * index, 18 + 2 * index)
        copy = pltpu.make_async_remote_copy(
            src_ref=dn_send.at[rows],
            dst_ref=dn_recv.at[rows],
            send_sem=push_send.at[index],
            recv_sem=push_recv.at[index],
            device_id=at(-dx, -dy),
            device_id_type=MESH,
        )
        copy.start()
        push.append(copy)

    scores_edges, dn = window_back(EDGES)
    dn_send[16:28] = dn.astype(BF16).reshape(12, 16, C)
    for index in range(6):
        send_back(index)
    scores_around, dn = window_back(AROUND)
    dn_send[0:16] = dn.astype(BF16).reshape(16, 16, C)
    for index in range(6, 8):
        send_back(index)

    scores_own, d_normed = window_back(OWN)
    d_query = []
    for p in range(PAIRS):
        both = nn(kt1[p, :, EDGES], scores_edges[p]) + nn(kt1[p, :, AROUND], scores_around[p])
        both = both + nn(kt1[p, :, OWN], scores_own[p])
        d_query.append((diagonal(both) * 0.125).astype(BF16))
    d_query = nt(to_xyz, jnp.concatenate(d_query, axis=0)).astype(BF16)
    d_normed = d_normed + nt(d_query, win_qkv[:, 0:C])
    grad1_xyz = nn(to_xyz, grad1_bf)
    out_ref[...] = nn(to_xyz, arrived(lo_send, lo_recv, 2)).astype(BF16)
    for copy in push:
        copy.wait_recv()
    d_normed = d_normed + (dn_recv[0:8].astype(F32) + dn_recv[8:16].astype(F32)).reshape(TOK, C)
    first, last = [
        sum(
            dn_recv[16 + 2 * i : 18 + 2 * i].astype(F32)
            for i, (_, dy) in enumerate(SIDES)
            if dy == way
        )
        for way in (-1, 1)
    ]
    none = jnp.zeros((32, C), F32)
    rims = jnp.concatenate([first[0], none, last[0], first[1], none, last[1]], axis=0)
    field_f = own[...].reshape(TOK, C).astype(F32)
    grad_ref[...] = grad1_xyz + norm_back(field_f, inverse_rms(field_f), d_normed + rims)

    for copy in halo + cot_copies + s1_copies + lo_copies + g1_copies + push:
        copy.wait_send()


def store(out_ref, grad_ref, out_hbm, grad_hbm, sem):
    copies = [
        pltpu.make_async_copy(grad_ref, grad_hbm, sem.at[0]),
        pltpu.make_async_copy(out_ref, out_hbm, sem.at[1]),
    ]
    for copy in copies:
        copy.start()
    for copy in copies:
        copy.wait()


def shards(nx, ny, field, cotangent, *rest):
    block = (2, 4, 16, C)
    tiles = (8, 16, C)
    vmem = pltpu.VMEM
    dma = pltpu.SemaphoreType.DMA
    weights, pattern = rest[:6], rest[6]
    in_hbm = pl.BlockSpec(memory_space=pltpu.HBM)
    in_vmem = pl.BlockSpec(memory_space=pltpu.VMEM)
    results = pl.pallas_call(
        functools.partial(kernel, nx, ny),
        out_shape=(pltpu.VMEM((TOK, C), BF16), pltpu.VMEM((TOK, C), F32)),
        in_specs=[in_hbm] * 9,
        out_specs=(in_vmem, in_vmem),
        scratch_shapes=[vmem(w.shape, BF16) for w in weights]
        + [vmem((n, C), BF16) for n in (C, 2 * C, C, 3 * C, FF)]
        + [pltpu.SMEM((3, 6), jnp.int32), vmem(block, BF16)]
        + [vmem((2,) + block, BF16), vmem((6, 2, 1, 16, C), BF16)]
        + [vmem(tiles, BF16)] * 9
        + [
            vmem((28, 16, C), BF16),
            vmem((28, 16, C), BF16),
            vmem((PAIRS, KEYS, 256), BF16),
            vmem((KEYS, 2 * C), BF16),
            vmem((PAIRS, TOK, KEYS), BF16),
            vmem((PAIRS, TOK, KEYS), BF16),
            vmem((PAIRS, TOK, TOK), F32),
            vmem((PAIRS, KEYS, 256), F32),
            vmem((KEYS, TOK), F32),
            vmem((PAIRS, 256, TOK), BF16),
            dma((9,)),
            dma((8,)),
            dma((8,)),
            dma((4, 8)),
            dma((4, 8)),
            dma((8,)),
            dma((8,)),
        ],
        compiler_params=pltpu.CompilerParams(
            collective_id=0, has_side_effects=True, vmem_limit_bytes=60 * 1024 * 1024
        ),
    )(field.reshape(block), cotangent.reshape(tiles), *weights, pattern.T)
    layer_output, field_grad = pl.pallas_call(
        store,
        out_shape=(
            jax.ShapeDtypeStruct((TOK, C), BF16),
            jax.ShapeDtypeStruct((TOK, C), F32),
        ),
        in_specs=[in_vmem] * 2,
        out_specs=(in_hbm, in_hbm),
        scratch_shapes=[dma((2,))],
        compiler_params=pltpu.CompilerParams(vmem_limit_bytes=4 * 1024 * 1024),
    )(*results)
    return layer_output.reshape(field.shape), field_grad.reshape(field.shape)


def solution(mesh):
    split = P("gx", "gy", None, None)
    return jax.shard_map(
        functools.partial(shards, mesh.shape["gx"], mesh.shape["gy"]),
        mesh=mesh,
        in_specs=(split, split) + (P(),) * 7,
        out_specs=(split, split),
        check_vma=False,
    )
```

```python
import functools

import jax
import jax.numpy as jnp
from jax import lax
from jax.experimental import pallas as pl
from jax.experimental.pallas import tpu as pltpu
from jax.sharding import PartitionSpec as P

F32 = jnp.float32
BF16 = jnp.bfloat16
C = 384
FF = 1536
CHUNK = 512
PAIRS = 3
TOK = 128
KEYS = 576
OWN, AROUND, EARLY, EDGES = slice(0, 128), slice(128, 384), slice(0, 384), slice(384, 576)
EPSILON = 1e-06
MASKED = -1e30
MESH = pl.DeviceIdType.MESH

SIDES = [(1, 1), (-1, -1), (1, -1), (-1, 1), (0, 1), (0, -1), (1, 0), (-1, 0)]
PEERS = [2, 6, 1, 3, 5, 7, 0, 4]


def nn(a, b):
    return lax.dot_general(a, b, (((1,), (0,)), ((), ())), preferred_element_type=F32)


def nt(a, b):
    return lax.dot_general(a, b, (((1,), (1,)), ((), ())), preferred_element_type=F32)


def inverse_rms(v):
    return lax.rsqrt(jnp.sum(v * v, axis=-1, keepdims=True) * (1.0 / C) + EPSILON)


def norm_back(v, r, upstream):
    inner = jnp.sum(v * upstream, axis=-1, keepdims=True) * (1.0 / C)
    return r * upstream - v * (r * r * r * inner)


def iota(shape, dim):
    return lax.broadcasted_iota(jnp.int32, shape, dim)


def diagonal(both):
    return jnp.concatenate([both[:64, :128], both[64:, 128:]], axis=0)


def abreast(both):
    return jnp.concatenate([both[:TOK], both[TOK:]], axis=1)


def lanes(p, base=0):
    return slice(base + 128 * p, base + 128 * (p + 1))


def kernel(
    nx,
    ny,
    field,
    cot,
    win_qkv_h,
    win_out_h,
    axial_qkv_h,
    axial_out_h,
    mlp_in_h,
    mlp_out_h,
    pattern_h,
    out_ref,
    grad_ref,
    win_qkv,
    win_out,
    axial_qkv,
    axial_out,
    mlp_in,
    mlp_out,
    win_out_t,
    win_kv_t,
    axial_out_t,
    axial_qkv_t,
    mlp_in_t,
    pattern,
    own,
    sides,
    edges,
    cot_own,
    cot_send,
    cot_recv,
    s1_send,
    s1_recv,
    lo_send,
    lo_recv,
    g1_send,
    g1_recv,
    dn_send,
    dn_recv,
    weights1,
    kv1,
    kt1,
    vt1,
    ot1,
    scores1,
    bias1,
    q1,
    local_sem,
    halo_send,
    halo_recv,
    a2a_send,
    a2a_recv,
    push_send,
    push_recv,
):
    gx = lax.axis_index("gx")
    gy = lax.axis_index("gy")

    partner = gx + 2 - 4 * ((gx >> 1) & 1)

    def step(index, by, size):
        moved = index + by
        if by > 0:
            return jnp.where(moved >= size, moved - size, moved)
        return jnp.where(moved < 0, moved + size, moved) if by else index

    def at(dx, dy):
        return (step(gx, dx, nx), step(gy, dy, ny))

    barrier = pltpu.get_barrier_semaphore()
    greeted = [at(dx, dy) for dx, dy in SIDES] + [(partner, step(gy, d, ny)) for d in PEERS]
    for device in greeted:
        pl.semaphore_signal(barrier, inc=1, device_id=device, device_id_type=MESH)

    local = [
        pltpu.make_async_copy(src, dst, local_sem.at[index])
        for index, (src, dst) in enumerate(
            [
                (field, own),
                (cot, cot_own),
                (win_qkv_h, win_qkv),
                (win_out_h, win_out),
                (axial_qkv_h, axial_qkv),
                (axial_out_h, axial_out),
                (mlp_in_h, mlp_in),
                (mlp_out_h, mlp_out),
                (pattern_h, pattern),
            ]
        )
    ]
    for copy in local[:2]:
        copy.start()
    local[0].wait()
    pl.semaphore_wait(barrier, len(greeted))

    own_y = {0: slice(0, 4), 1: slice(3, 4), -1: slice(0, 1)}
    halo = []
    for index, (dx, dy) in enumerate(SIDES):
        copy = pltpu.make_async_remote_copy(
            src_ref=own.at[:, own_y[dy]],
            dst_ref=sides.at[index - 6] if dy == 0 else edges.at[index],
            send_sem=halo_send.at[index],
            recv_sem=halo_recv.at[index],
            device_id=at(dx, dy),
            device_id_type=MESH,
        )
        copy.start()
        halo.append(copy)
    for copy in local[2:]:
        copy.start()

    def exchange(send, recv, group):
        copies = []
        for d in PEERS:
            peer = step(gy, d, ny)
            copy = pltpu.make_async_remote_copy(
                src_ref=send.at[peer],
                dst_ref=recv.at[gy],
                send_sem=a2a_send.at[group, d],
                recv_sem=a2a_recv.at[group, d],
                device_id=(partner, peer),
                device_id_type=MESH,
            )
            copy.start()
            copies.append(copy)
        return copies

    def arrived(send, recv, group):
        for d in PEERS:
            source = step(gy, -d, ny)
            pltpu.make_async_remote_copy(
                src_ref=send.at[source],
                dst_ref=recv.at[source],
                send_sem=a2a_send.at[group, d],
                recv_sem=a2a_recv.at[group, d],
                device_id=(partner, source),
                device_id_type=MESH,
            ).wait_recv()
        return recv[...].reshape(TOK, C)

    row, col = iota((TOK, TOK), 0), iota((TOK, TOK), 1)
    to_zxy = jnp.where(row == (col & 7) * 16 + (col >> 3), 1.0, 0.0).astype(BF16)
    to_xyz = jnp.where(col == (row & 7) * 16 + (row >> 3), 1.0, 0.0).astype(BF16)
    eye = jnp.where(row == col, 1.0, 0.0).astype(BF16)
    head0 = jnp.where(col < 64, 1.0, 0.0).astype(BF16)
    head1 = jnp.where(col < 64, 0.0, 1.0).astype(BF16)

    def stacked(pair):
        return jnp.concatenate([pair * head0, pair * head1], axis=0)

    local[1].wait()
    cot_send[...] = nn(to_zxy, cot_own[...].reshape(TOK, C)).astype(BF16).reshape(8, 16, C)

    def near(rows, bits, x_base, y_base):
        key, query = iota((rows, TOK), 0), iota((rows, TOK), 1)
        gap_x = (key >> (3 + bits)) + x_base - ((query >> 3) & 1)
        gap_y = ((key >> 3) & ((1 << bits) - 1)) + y_base - (query & 7)
        gap_z = ((key & 7) - (query >> 4) + 2) & 7
        inside = (jnp.abs(gap_x) <= 2) & (jnp.abs(gap_y) <= 2) & (gap_z <= 4)
        return jnp.where(inside, 0.0, MASKED)

    bias1[OWN, :] = near(TOK, 3, 0, 0)
    for index, (dx, dy) in enumerate(SIDES):
        if dy == 0:
            start = 128 * (index - 5)
            bias1[start : start + 128, :] = near(128, 3, -2 * dx, 0)
        else:
            start = 384 + 32 * index
            bias1[start : start + 32, :] = near(32, 1, -2 * dx, -2 if dy == 1 else 8)

    def window_scores(part, tokens):
        values = tokens.astype(F32)
        normed = (values * inverse_rms(values)).astype(BF16)
        kv = nn(normed, win_qkv[:, C : 3 * C]).astype(BF16)
        kv1[part] = kv
        bias = jnp.concatenate([bias1[part, :], bias1[part, :]], axis=1)
        for p in range(PAIRS):
            scores1[p, part] = nt(kv[:, lanes(p)], q1[p]) + bias
            vt1[p, :, part] = nt(eye, kv[:, lanes(p, C)]).astype(BF16)
        return normed

    field_own = own[...].reshape(TOK, C)
    field_zxy = nn(to_zxy, field_own)
    normed1_zxy = (field_zxy * inverse_rms(field_zxy)).astype(BF16)
    local[2].wait()
    query1 = nn(normed1_zxy, win_qkv[:, 0:C]).astype(BF16) * 0.125
    for p in range(PAIRS):
        q1[p] = stacked(query1[:, lanes(p)])
    window_scores(OWN, field_own)
    for copy in local[5:7]:
        copy.wait()
    axial_out_t[...] = axial_out[...].T
    mlp_in_t[...] = mlp_in[...].T
    for copy in halo[6:]:
        copy.wait_recv()
    window_scores(AROUND, sides[...].reshape(256, C))
    tops, sums, outs = [], [], []
    for p in range(PAIRS):
        scores = scores1[p, EARLY]
        tops.append(jnp.max(scores, axis=0, keepdims=True))
        e = jnp.exp(scores - tops[p])
        scores1[p, EARLY] = e
        sums.append(jnp.sum(e, axis=0, keepdims=True))
        outs.append(diagonal(nn(vt1[p, :, EARLY], e.astype(BF16))))
    for copy in halo[:6]:
        copy.wait_recv()
    cot_copies = exchange(cot_send, cot_recv, 0)
    window_scores(EDGES, edges[...].reshape(192, C))
    attended, early_scale = [], []
    for p in range(PAIRS):
        scores = scores1[p, EDGES]
        top = jnp.maximum(tops[p], jnp.max(scores, axis=0, keepdims=True))
        e = jnp.exp(scores - top)
        shrink = jnp.exp(tops[p] - top)
        scale = 1.0 / (shrink * sums[p] + jnp.sum(e, axis=0, keepdims=True))
        weights = (e * scale).astype(BF16)
        weights1[p, EDGES] = weights
        early_scale.append(shrink * scale)
        early = jnp.concatenate(
            [
                outs[p][:64] * early_scale[p][:, :TOK],
                outs[p][64:] * early_scale[p][:, TOK:],
            ],
            axis=0,
        )
        ot = early + diagonal(nn(vt1[p, :, EDGES], weights))
        ot1[p] = ot
        attended.append(ot.astype(BF16).T)
    attended = jnp.concatenate(attended, axis=1)
    local[3].wait()
    s1_send[...] = (field_zxy + nn(attended, win_out[...])).astype(BF16).reshape(8, 16, C)
    s1_copies = exchange(s1_send, s1_recv, 1)

    for p in range(PAIRS):
        weights1[p, EARLY] = (scores1[p, EARLY] * early_scale[p]).astype(BF16)
        kt1[p] = nt(eye, kv1[:, lanes(p)]).astype(BF16)
    for copy in (local[4], local[7], local[8]):
        copy.wait()
    axial_qkv_t[...] = axial_qkv[...].T
    off = ((col >> 4) - (row >> 4)) & 7
    same_line = ((row ^ col) & 8) == 0
    bias2 = []
    for head in range(2 * PAIRS):
        hit = off == 0
        for j in range(3):
            hit = hit | (off == pattern[j, head])
        bias2.append(jnp.where(hit & same_line, 0.0, MASKED))

    gradient_bf = arrived(cot_send, cot_recv, 0)
    gradient = gradient_bf.astype(F32)
    d_hidden = nt(gradient_bf, mlp_out[...])
    stream1 = arrived(s1_send, s1_recv, 1).astype(F32)
    r2 = inverse_rms(stream1)
    triple2 = nn((stream1 * r2).astype(BF16), axial_qkv[...]).astype(BF16)
    query2 = triple2[:, 0:C] * 0.125
    q2 = [stacked(query2[:, lanes(p)]) for p in range(PAIRS)]
    weights2 = []
    attended2 = []
    for p in range(PAIRS):
        pair_bias = jnp.concatenate([bias2[2 * p], bias2[2 * p + 1]], axis=0)
        scores = nt(q2[p], triple2[:, lanes(p, C)]) + pair_bias
        e = jnp.exp(scores - jnp.max(scores, axis=1, keepdims=True))
        weights = (e * (1.0 / jnp.sum(e, axis=1, keepdims=True))).astype(BF16)
        weights2.append(weights)
        values = stacked(triple2[:, lanes(p, 2 * C)])
        attended2.append(nn(abreast(weights), values))
    attended2 = jnp.concatenate(attended2, axis=1).astype(BF16)
    stream2 = (stream1 + nn(attended2, axial_out[...])).astype(BF16).astype(F32)

    r3 = inverse_rms(stream2)
    normed3 = (stream2 * r3).astype(BF16)
    hidden, d_inner = [], []
    for c in range(FF // CHUNK):
        part = slice(CHUNK * c, CHUNK * (c + 1))
        a = nn(normed3, mlp_in[:, part])
        square = a * a
        t = jnp.tanh(a * (0.7978845608028654 + (0.044715 * 0.7978845608028654) * square))
        half = 0.5 + 0.5 * t
        hidden.append((a * half).astype(BF16))
        steep = a * (2 * 0.7978845608028654 + (6 * 0.044715 * 0.7978845608028654) * square)
        slope = half + (half - half * half) * steep
        d_inner.append((d_hidden[:, part] * slope).astype(BF16))
    back = nn(jnp.concatenate(d_inner, axis=1), mlp_in_t[...])
    grad2 = gradient + norm_back(stream2, r3, back)

    back2 = nn(grad2.astype(BF16), axial_out_t[...]).astype(BF16)
    d_query, d_key, d_value = [], [], []
    for p in range(PAIRS):
        upstream = stacked(back2[:, lanes(p)])
        keys = stacked(triple2[:, lanes(p, C)])
        weights = weights2[p].astype(F32)
        d_weights = nt(upstream, triple2[:, lanes(p, 2 * C)])
        delta = jnp.sum(weights * d_weights, axis=1, keepdims=True)
        d_scores = (weights * (d_weights - delta)).astype(BF16)
        d_query.append(nn(abreast(d_scores), keys) * 0.125)
        d_key.append(nn(d_scores.T, q2[p]))
        d_value.append(nn(weights2[p].T, upstream))
    d_triple2 = jnp.concatenate(d_query + d_key + d_value, axis=1).astype(BF16)
    grad1 = grad2 + norm_back(stream1, r2, nn(d_triple2, axial_qkv_t[...]))
    g1_send[...] = grad1.astype(BF16).reshape(8, 16, C)
    g1_copies = exchange(g1_send, g1_recv, 3)

    hidden_out = nn(jnp.concatenate(hidden, axis=1), mlp_out[...])
    lo_send[...] = (stream2 + hidden_out).astype(BF16).reshape(8, 16, C)
    win_out_t[...] = win_out[...].T
    win_kv_t[0:C] = win_qkv[:, 2 * C : 3 * C].T
    win_kv_t[C : 2 * C] = win_qkv[:, C : 2 * C].T

    grad1_bf = arrived(g1_send, g1_recv, 3)
    lo_copies = exchange(lo_send, lo_recv, 2)
    back1 = nn(grad1_bf, win_out_t[...]).astype(BF16)
    back1_t = nt(win_out[...], grad1_bf).astype(BF16).astype(F32)
    upstream, delta = [], []
    for p in range(PAIRS):
        upstream.append(stacked(back1[:, lanes(p)]))
        product = ot1[p] * back1_t[lanes(p)]
        halves = [jnp.sum(product[h : h + 64], axis=0, keepdims=True) for h in (0, 64)]
        delta.append(jnp.concatenate(halves, axis=1))

    def window_back(part):
        d_scores, d_key, d_value = [], [], []
        for p in range(PAIRS):
            weights = weights1[p, part]
            d_weights = nt(kv1[part, lanes(p, C)], upstream[p])
            d_scores.append((weights.astype(F32) * (d_weights - delta[p])).astype(BF16))
            d_key.append(nn(d_scores[p], q1[p]).astype(BF16))
            d_value.append(nn(weights, upstream[p]).astype(BF16))
        d_kv = jnp.concatenate(d_value + d_key, axis=1)
        return d_scores, nn(d_kv, win_kv_t[...])

    push = []

    def send_back(index):
        dx, dy = SIDES[index]
        if dy == 0:
            rows = slice(8 * (index - 6), 8 * (index - 5))
        else:
            rows = slice(16 + 2 * index, 18 + 2 * index)
        copy = pltpu.make_async_remote_copy(
            src_ref=dn_send.at[rows],
            dst_ref=dn_recv.at[rows],
            send_sem=push_send.at[index],
            recv_sem=push_recv.at[index],
            device_id=at(-dx, -dy),
            device_id_type=MESH,
        )
        copy.start()
        push.append(copy)

    scores_edges, dn = window_back(EDGES)
    dn_send[16:28] = dn.astype(BF16).reshape(12, 16, C)
    for index in range(6):
        send_back(index)
    scores_around, dn = window_back(AROUND)
    dn_send[0:16] = dn.astype(BF16).reshape(16, 16, C)
    for index in range(6, 8):
        send_back(index)

    scores_own, d_normed = window_back(OWN)
    d_query = []
    for p in range(PAIRS):
        both = nn(kt1[p, :, EDGES], scores_edges[p]) + nn(kt1[p, :, AROUND], scores_around[p])
        both = both + nn(kt1[p, :, OWN], scores_own[p])
        d_query.append((diagonal(both) * 0.125).astype(BF16))
    d_query = nt(to_xyz, jnp.concatenate(d_query, axis=0)).astype(BF16)
    d_normed = d_normed + nt(d_query, win_qkv[:, 0:C])
    grad1_xyz = nn(to_xyz, grad1_bf)
    out_ref[...] = nn(to_xyz, arrived(lo_send, lo_recv, 2)).astype(BF16)
    for copy in push:
        copy.wait_recv()
    d_normed = d_normed + (dn_recv[0:8].astype(F32) + dn_recv[8:16].astype(F32)).reshape(TOK, C)
    first, last = [
        sum(
            dn_recv[16 + 2 * i : 18 + 2 * i].astype(F32)
            for i, (_, dy) in enumerate(SIDES)
            if dy == way
        )
        for way in (-1, 1)
    ]
    none = jnp.zeros((32, C), F32)
    rims = jnp.concatenate([first[0], none, last[0], first[1], none, last[1]], axis=0)
    field_f = own[...].reshape(TOK, C).astype(F32)
    grad_ref[...] = grad1_xyz + norm_back(field_f, inverse_rms(field_f), d_normed + rims)

    for copy in halo + cot_copies + s1_copies + lo_copies + g1_copies + push:
        copy.wait_send()


def store(out_ref, grad_ref, out_hbm, grad_hbm, sem):
    copies = [
        pltpu.make_async_copy(grad_ref, grad_hbm, sem.at[0]),
        pltpu.make_async_copy(out_ref, out_hbm, sem.at[1]),
    ]
    for copy in copies:
        copy.start()
    for copy in copies:
        copy.wait()


def shards(nx, ny, field, cotangent, *rest):
    block = (2, 4, 16, C)
    tiles = (8, 16, C)
    vmem = pltpu.VMEM
    dma = pltpu.SemaphoreType.DMA
    weights, pattern = rest[:6], rest[6]
    in_hbm = pl.BlockSpec(memory_space=pltpu.HBM)
    in_vmem = pl.BlockSpec(memory_space=pltpu.VMEM)
    results = pl.pallas_call(
        functools.partial(kernel, nx, ny),
        out_shape=(pltpu.VMEM((TOK, C), BF16), pltpu.VMEM((TOK, C), F32)),
        in_specs=[in_hbm] * 9,
        out_specs=(in_vmem, in_vmem),
        scratch_shapes=[vmem(w.shape, BF16) for w in weights]
        + [vmem((n, C), BF16) for n in (C, 2 * C, C, 3 * C, FF)]
        + [pltpu.SMEM((3, 6), jnp.int32), vmem(block, BF16)]
        + [vmem((2,) + block, BF16), vmem((6, 2, 1, 16, C), BF16)]
        + [vmem(tiles, BF16)] * 9
        + [
            vmem((28, 16, C), BF16),
            vmem((28, 16, C), BF16),
            vmem((PAIRS, KEYS, 256), BF16),
            vmem((KEYS, 2 * C), BF16),
            vmem((PAIRS, TOK, KEYS), BF16),
            vmem((PAIRS, TOK, KEYS), BF16),
            vmem((PAIRS, TOK, TOK), F32),
            vmem((PAIRS, KEYS, 256), F32),
            vmem((KEYS, TOK), F32),
            vmem((PAIRS, 256, TOK), BF16),
            dma((9,)),
            dma((8,)),
            dma((8,)),
            dma((4, 8)),
            dma((4, 8)),
            dma((8,)),
            dma((8,)),
        ],
        compiler_params=pltpu.CompilerParams(
            collective_id=0, has_side_effects=True, vmem_limit_bytes=60 * 1024 * 1024
        ),
    )(field.reshape(block), cotangent.reshape(tiles), *weights, pattern.T)
    layer_output, field_grad = pl.pallas_call(
        store,
        out_shape=(
            jax.ShapeDtypeStruct((TOK, C), BF16),
            jax.ShapeDtypeStruct((TOK, C), F32),
        ),
        in_specs=[in_vmem] * 2,
        out_specs=(in_hbm, in_hbm),
        scratch_shapes=[dma((2,))],
        compiler_params=pltpu.CompilerParams(vmem_limit_bytes=4 * 1024 * 1024),
    )(*results)
    return layer_output.reshape(field.shape), field_grad.reshape(field.shape)


def solution(mesh):
    split = P("gx", "gy", None, None)
    return jax.shard_map(
        functools.partial(shards, mesh.shape["gx"], mesh.shape["gy"]),
        mesh=mesh,
        in_specs=(split, split) + (P(),) * 7,
        out_specs=(split, split),
        check_vma=False,
    )
```

```python
import functools

import jax
import jax.numpy as jnp
from jax import lax
from jax.experimental import pallas as pl
from jax.experimental.pallas import tpu as pltpu
from jax.sharding import PartitionSpec as P

F32 = jnp.float32
BF16 = jnp.bfloat16
C = 384
FF = 1536
CHUNK = 512
PAIRS = 3
TOK = 128
KEYS = 576
OWN, AROUND, EARLY, EDGES = slice(0, 128), slice(128, 384), slice(0, 384), slice(384, 576)
EPSILON = 1e-06
MASKED = -1e30
MESH = pl.DeviceIdType.MESH

SIDES = [(1, 1), (-1, -1), (1, -1), (-1, 1), (0, 1), (0, -1), (1, 0), (-1, 0)]
PEERS = [2, 6, 1, 3, 5, 7, 0, 4]


def nn(a, b):
    return lax.dot_general(a, b, (((1,), (0,)), ((), ())), preferred_element_type=F32)


def nt(a, b):
    return lax.dot_general(a, b, (((1,), (1,)), ((), ())), preferred_element_type=F32)


def inverse_rms(v):
    return lax.rsqrt(jnp.sum(v * v, axis=-1, keepdims=True) * (1.0 / C) + EPSILON)


def norm_back(v, r, upstream):
    inner = jnp.sum(v * upstream, axis=-1, keepdims=True) * (1.0 / C)
    return r * upstream - v * (r * r * r * inner)


def iota(shape, dim):
    return lax.broadcasted_iota(jnp.int32, shape, dim)


def diagonal(both):
    return jnp.concatenate([both[:64, :128], both[64:, 128:]], axis=0)


def abreast(both):
    return jnp.concatenate([both[:TOK], both[TOK:]], axis=1)


def lanes(p, base=0):
    return slice(base + 128 * p, base + 128 * (p + 1))


def kernel(
    nx,
    ny,
    field,
    cot,
    win_qkv_h,
    win_out_h,
    axial_qkv_h,
    axial_out_h,
    mlp_in_h,
    mlp_out_h,
    pattern_h,
    out_ref,
    grad_ref,
    win_qkv,
    win_out,
    axial_qkv,
    axial_out,
    mlp_in,
    mlp_out,
    win_out_t,
    win_kv_t,
    axial_out_t,
    axial_qkv_t,
    mlp_in_t,
    pattern,
    own,
    sides,
    edges,
    cot_own,
    cot_send,
    cot_recv,
    s1_send,
    s1_recv,
    lo_send,
    lo_recv,
    g1_send,
    g1_recv,
    dn_send,
    dn_recv,
    weights1,
    kv1,
    kt1,
    vt1,
    ot1,
    scores1,
    bias1,
    q1,
    local_sem,
    halo_send,
    halo_recv,
    a2a_send,
    a2a_recv,
    push_send,
    push_recv,
):
    gx = lax.axis_index("gx")
    gy = lax.axis_index("gy")

    partner = gx + 2 - 4 * ((gx >> 1) & 1)

    def step(index, by, size):
        moved = index + by
        if by > 0:
            return jnp.where(moved >= size, moved - size, moved)
        return jnp.where(moved < 0, moved + size, moved) if by else index

    def at(dx, dy):
        return (step(gx, dx, nx), step(gy, dy, ny))

    barrier = pltpu.get_barrier_semaphore()
    greeted = [at(dx, dy) for dx, dy in SIDES] + [(partner, step(gy, d, ny)) for d in PEERS]
    for device in greeted:
        pl.semaphore_signal(barrier, inc=1, device_id=device, device_id_type=MESH)

    local = [
        pltpu.make_async_copy(src, dst, local_sem.at[index])
        for index, (src, dst) in enumerate(
            [
                (field, own),
                (cot, cot_own),
                (win_qkv_h, win_qkv),
                (win_out_h, win_out),
                (axial_qkv_h, axial_qkv),
                (axial_out_h, axial_out),
                (mlp_in_h, mlp_in),
                (mlp_out_h, mlp_out),
                (pattern_h, pattern),
            ]
        )
    ]
    for copy in local[:2]:
        copy.start()
    local[0].wait()
    pl.semaphore_wait(barrier, len(greeted))

    own_y = {0: slice(0, 4), 1: slice(3, 4), -1: slice(0, 1)}
    halo = []
    for index, (dx, dy) in enumerate(SIDES):
        copy = pltpu.make_async_remote_copy(
            src_ref=own.at[:, own_y[dy]],
            dst_ref=sides.at[index - 6] if dy == 0 else edges.at[index],
            send_sem=halo_send.at[index],
            recv_sem=halo_recv.at[index],
            device_id=at(dx, dy),
            device_id_type=MESH,
        )
        copy.start()
        halo.append(copy)
    for copy in local[2:]:
        copy.start()

    def exchange(send, recv, group):
        copies = []
        for d in PEERS:
            peer = step(gy, d, ny)
            copy = pltpu.make_async_remote_copy(
                src_ref=send.at[peer],
                dst_ref=recv.at[gy],
                send_sem=a2a_send.at[group, d],
                recv_sem=a2a_recv.at[group, d],
                device_id=(partner, peer),
                device_id_type=MESH,
            )
            copy.start()
            copies.append(copy)
        return copies

    def arrived(send, recv, group):
        for d in PEERS:
            source = step(gy, -d, ny)
            pltpu.make_async_remote_copy(
                src_ref=send.at[source],
                dst_ref=recv.at[source],
                send_sem=a2a_send.at[group, d],
                recv_sem=a2a_recv.at[group, d],
                device_id=(partner, source),
                device_id_type=MESH,
            ).wait_recv()
        return recv[...].reshape(TOK, C)

    row, col = iota((TOK, TOK), 0), iota((TOK, TOK), 1)
    to_zxy = jnp.where(row == (col & 7) * 16 + (col >> 3), 1.0, 0.0).astype(BF16)
    to_xyz = jnp.where(col == (row & 7) * 16 + (row >> 3), 1.0, 0.0).astype(BF16)
    eye = jnp.where(row == col, 1.0, 0.0).astype(BF16)
    head0 = jnp.where(col < 64, 1.0, 0.0).astype(BF16)
    head1 = jnp.where(col < 64, 0.0, 1.0).astype(BF16)

    def stacked(pair):
        return jnp.concatenate([pair * head0, pair * head1], axis=0)

    local[1].wait()
    cot_send[...] = nn(to_zxy, cot_own[...].reshape(TOK, C)).astype(BF16).reshape(8, 16, C)

    def near(rows, bits, x_base, y_base):
        key, query = iota((rows, TOK), 0), iota((rows, TOK), 1)
        gap_x = (key >> (3 + bits)) + x_base - ((query >> 3) & 1)
        gap_y = ((key >> 3) & ((1 << bits) - 1)) + y_base - (query & 7)
        gap_z = ((key & 7) - (query >> 4) + 2) & 7
        inside = (jnp.abs(gap_x) <= 2) & (jnp.abs(gap_y) <= 2) & (gap_z <= 4)
        return jnp.where(inside, 0.0, MASKED)

    bias1[OWN, :] = near(TOK, 3, 0, 0)
    for index, (dx, dy) in enumerate(SIDES):
        if dy == 0:
            start = 128 * (index - 5)
            bias1[start : start + 128, :] = near(128, 3, -2 * dx, 0)
        else:
            start = 384 + 32 * index
            bias1[start : start + 32, :] = near(32, 1, -2 * dx, -2 if dy == 1 else 8)

    def window_scores(part, tokens):
        values = tokens.astype(F32)
        normed = (values * inverse_rms(values)).astype(BF16)
        kv = nn(normed, win_qkv[:, C : 3 * C]).astype(BF16)
        kv1[part] = kv
        bias = jnp.concatenate([bias1[part, :], bias1[part, :]], axis=1)
        for p in range(PAIRS):
            scores1[p, part] = nt(kv[:, lanes(p)], q1[p]) + bias
            vt1[p, :, part] = nt(eye, kv[:, lanes(p, C)]).astype(BF16)
        return normed

    field_own = own[...].reshape(TOK, C)
    field_zxy = nn(to_zxy, field_own)
    normed1_zxy = (field_zxy * inverse_rms(field_zxy)).astype(BF16)
    local[2].wait()
    query1 = nn(normed1_zxy, win_qkv[:, 0:C]).astype(BF16) * 0.125
    for p in range(PAIRS):
        q1[p] = stacked(query1[:, lanes(p)])
    window_scores(OWN, field_own)
    for copy in local[5:7]:
        copy.wait()
    axial_out_t[...] = axial_out[...].T
    mlp_in_t[...] = mlp_in[...].T
    for copy in halo[6:]:
        copy.wait_recv()
    window_scores(AROUND, sides[...].reshape(256, C))
    tops, sums, outs = [], [], []
    for p in range(PAIRS):
        scores = scores1[p, EARLY]
        tops.append(jnp.max(scores, axis=0, keepdims=True))
        e = jnp.exp(scores - tops[p])
        scores1[p, EARLY] = e
        sums.append(jnp.sum(e, axis=0, keepdims=True))
        outs.append(diagonal(nn(vt1[p, :, EARLY], e.astype(BF16))))
    for copy in halo[:6]:
        copy.wait_recv()
    cot_copies = exchange(cot_send, cot_recv, 0)
    window_scores(EDGES, edges[...].reshape(192, C))
    attended, early_scale = [], []
    for p in range(PAIRS):
        scores = scores1[p, EDGES]
        top = jnp.maximum(tops[p], jnp.max(scores, axis=0, keepdims=True))
        e = jnp.exp(scores - top)
        shrink = jnp.exp(tops[p] - top)
        scale = 1.0 / (shrink * sums[p] + jnp.sum(e, axis=0, keepdims=True))
        weights = (e * scale).astype(BF16)
        weights1[p, EDGES] = weights
        early_scale.append(shrink * scale)
        early = jnp.concatenate(
            [
                outs[p][:64] * early_scale[p][:, :TOK],
                outs[p][64:] * early_scale[p][:, TOK:],
            ],
            axis=0,
        )
        ot = early + diagonal(nn(vt1[p, :, EDGES], weights))
        ot1[p] = ot
        attended.append(ot.astype(BF16).T)
    attended = jnp.concatenate(attended, axis=1)
    local[3].wait()
    s1_send[...] = (field_zxy + nn(attended, win_out[...])).astype(BF16).reshape(8, 16, C)
    s1_copies = exchange(s1_send, s1_recv, 1)

    for p in range(PAIRS):
        weights1[p, EARLY] = (scores1[p, EARLY] * early_scale[p]).astype(BF16)
        kt1[p] = nt(eye, kv1[:, lanes(p)]).astype(BF16)
    for copy in (local[4], local[7], local[8]):
        copy.wait()
    axial_qkv_t[...] = axial_qkv[...].T
    off = ((col >> 4) - (row >> 4)) & 7
    same_line = ((row ^ col) & 8) == 0
    bias2 = []
    for head in range(2 * PAIRS):
        hit = off == 0
        for j in range(3):
            hit = hit | (off == pattern[j, head])
        bias2.append(jnp.where(hit & same_line, 0.0, MASKED))

    gradient_bf = arrived(cot_send, cot_recv, 0)
    gradient = gradient_bf.astype(F32)
    d_hidden = nt(gradient_bf, mlp_out[...])
    stream1 = arrived(s1_send, s1_recv, 1).astype(F32)
    r2 = inverse_rms(stream1)
    triple2 = nn((stream1 * r2).astype(BF16), axial_qkv[...]).astype(BF16)
    query2 = triple2[:, 0:C] * 0.125
    q2 = [stacked(query2[:, lanes(p)]) for p in range(PAIRS)]
    weights2 = []
    attended2 = []
    for p in range(PAIRS):
        pair_bias = jnp.concatenate([bias2[2 * p], bias2[2 * p + 1]], axis=0)
        scores = nt(q2[p], triple2[:, lanes(p, C)]) + pair_bias
        e = jnp.exp(scores - jnp.max(scores, axis=1, keepdims=True))
        weights = (e * (1.0 / jnp.sum(e, axis=1, keepdims=True))).astype(BF16)
        weights2.append(weights)
        values = stacked(triple2[:, lanes(p, 2 * C)])
        attended2.append(nn(abreast(weights), values))
    attended2 = jnp.concatenate(attended2, axis=1).astype(BF16)
    stream2 = (stream1 + nn(attended2, axial_out[...])).astype(BF16).astype(F32)

    r3 = inverse_rms(stream2)
    normed3 = (stream2 * r3).astype(BF16)
    hidden, d_inner = [], []
    for c in range(FF // CHUNK):
        part = slice(CHUNK * c, CHUNK * (c + 1))
        a = nn(normed3, mlp_in[:, part])
        square = a * a
        t = jnp.tanh(a * (0.7978845608028654 + (0.044715 * 0.7978845608028654) * square))
        half = 0.5 + 0.5 * t
        hidden.append((a * half).astype(BF16))
        steep = a * (2 * 0.7978845608028654 + (6 * 0.044715 * 0.7978845608028654) * square)
        slope = half + (half - half * half) * steep
        d_inner.append((d_hidden[:, part] * slope).astype(BF16))
    back = nn(jnp.concatenate(d_inner, axis=1), mlp_in_t[...])
    grad2 = gradient + norm_back(stream2, r3, back)

    back2 = nn(grad2.astype(BF16), axial_out_t[...]).astype(BF16)
    d_query, d_key, d_value = [], [], []
    for p in range(PAIRS):
        upstream = stacked(back2[:, lanes(p)])
        keys = stacked(triple2[:, lanes(p, C)])
        weights = weights2[p].astype(F32)
        d_weights = nt(upstream, triple2[:, lanes(p, 2 * C)])
        delta = jnp.sum(weights * d_weights, axis=1, keepdims=True)
        d_scores = (weights * (d_weights - delta)).astype(BF16)
        d_query.append(nn(abreast(d_scores), keys) * 0.125)
        d_key.append(nn(d_scores.T, q2[p]))
        d_value.append(nn(weights2[p].T, upstream))
    d_triple2 = jnp.concatenate(d_query + d_key + d_value, axis=1).astype(BF16)
    grad1 = grad2 + norm_back(stream1, r2, nn(d_triple2, axial_qkv_t[...]))
    g1_send[...] = grad1.astype(BF16).reshape(8, 16, C)
    g1_copies = exchange(g1_send, g1_recv, 3)

    hidden_out = nn(jnp.concatenate(hidden, axis=1), mlp_out[...])
    lo_send[...] = (stream2 + hidden_out).astype(BF16).reshape(8, 16, C)
    lo_copies = exchange(lo_send, lo_recv, 2)
    win_out_t[...] = win_out[...].T
    win_kv_t[0:C] = win_qkv[:, 2 * C : 3 * C].T
    win_kv_t[C : 2 * C] = win_qkv[:, C : 2 * C].T

    grad1_bf = arrived(g1_send, g1_recv, 3)
    back1 = nn(grad1_bf, win_out_t[...]).astype(BF16)
    back1_t = nt(win_out[...], grad1_bf).astype(BF16).astype(F32)
    upstream, delta = [], []
    for p in range(PAIRS):
        upstream.append(stacked(back1[:, lanes(p)]))
        product = ot1[p] * back1_t[lanes(p)]
        halves = [jnp.sum(product[h : h + 64], axis=0, keepdims=True) for h in (0, 64)]
        delta.append(jnp.concatenate(halves, axis=1))

    def window_back(part):
        d_scores, d_key, d_value = [], [], []
        for p in range(PAIRS):
            weights = weights1[p, part]
            d_weights = nt(kv1[part, lanes(p, C)], upstream[p])
            d_scores.append((weights.astype(F32) * (d_weights - delta[p])).astype(BF16))
            d_key.append(nn(d_scores[p], q1[p]).astype(BF16))
            d_value.append(nn(weights, upstream[p]).astype(BF16))
        d_kv = jnp.concatenate(d_value + d_key, axis=1)
        return d_scores, nn(d_kv, win_kv_t[...])

    push = []

    def send_back(index):
        dx, dy = SIDES[index]
        if dy == 0:
            rows = slice(8 * (index - 6), 8 * (index - 5))
        else:
            rows = slice(16 + 2 * index, 18 + 2 * index)
        copy = pltpu.make_async_remote_copy(
            src_ref=dn_send.at[rows],
            dst_ref=dn_recv.at[rows],
            send_sem=push_send.at[index],
            recv_sem=push_recv.at[index],
            device_id=at(-dx, -dy),
            device_id_type=MESH,
        )
        copy.start()
        push.append(copy)

    scores_edges, dn = window_back(EDGES)
    dn_send[16:28] = dn.astype(BF16).reshape(12, 16, C)
    for index in range(6):
        send_back(index)
    scores_around, dn = window_back(AROUND)
    dn_send[0:16] = dn.astype(BF16).reshape(16, 16, C)
    for index in range(6, 8):
        send_back(index)

    scores_own, d_normed = window_back(OWN)
    d_query = []
    for p in range(PAIRS):
        both = nn(kt1[p, :, EDGES], scores_edges[p]) + nn(kt1[p, :, AROUND], scores_around[p])
        both = both + nn(kt1[p, :, OWN], scores_own[p])
        d_query.append((diagonal(both) * 0.125).astype(BF16))
    d_query = nt(to_xyz, jnp.concatenate(d_query, axis=0)).astype(BF16)
    d_normed = d_normed + nt(d_query, win_qkv[:, 0:C])
    grad1_xyz = nn(to_xyz, grad1_bf)
    out_ref[...] = nn(to_xyz, arrived(lo_send, lo_recv, 2)).astype(BF16)
    for copy in push:
        copy.wait_recv()
    d_normed = d_normed + (dn_recv[0:8].astype(F32) + dn_recv[8:16].astype(F32)).reshape(TOK, C)
    first, last = [
        sum(
            dn_recv[16 + 2 * i : 18 + 2 * i].astype(F32)
            for i, (_, dy) in enumerate(SIDES)
            if dy == way
        )
        for way in (-1, 1)
    ]
    none = jnp.zeros((32, C), F32)
    rims = jnp.concatenate([first[0], none, last[0], first[1], none, last[1]], axis=0)
    field_f = own[...].reshape(TOK, C).astype(F32)
    grad_ref[...] = grad1_xyz + norm_back(field_f, inverse_rms(field_f), d_normed + rims)

    for copy in halo + cot_copies + s1_copies + lo_copies + g1_copies + push:
        copy.wait_send()


def store(out_ref, grad_ref, out_hbm, grad_hbm, sem):
    copies = [
        pltpu.make_async_copy(grad_ref, grad_hbm, sem.at[0]),
        pltpu.make_async_copy(out_ref, out_hbm, sem.at[1]),
    ]
    for copy in copies:
        copy.start()
    for copy in copies:
        copy.wait()


def shards(nx, ny, field, cotangent, *rest):
    block = (2, 4, 16, C)
    tiles = (8, 16, C)
    vmem = pltpu.VMEM
    dma = pltpu.SemaphoreType.DMA
    weights, pattern = rest[:6], rest[6]
    in_hbm = pl.BlockSpec(memory_space=pltpu.HBM)
    in_vmem = pl.BlockSpec(memory_space=pltpu.VMEM)
    results = pl.pallas_call(
        functools.partial(kernel, nx, ny),
        out_shape=(pltpu.VMEM((TOK, C), BF16), pltpu.VMEM((TOK, C), F32)),
        in_specs=[in_hbm] * 9,
        out_specs=(in_vmem, in_vmem),
        scratch_shapes=[vmem(w.shape, BF16) for w in weights]
        + [vmem((n, C), BF16) for n in (C, 2 * C, C, 3 * C, FF)]
        + [pltpu.SMEM((3, 6), jnp.int32), vmem(block, BF16)]
        + [vmem((2,) + block, BF16), vmem((6, 2, 1, 16, C), BF16)]
        + [vmem(tiles, BF16)] * 9
        + [
            vmem((28, 16, C), BF16),
            vmem((28, 16, C), BF16),
            vmem((PAIRS, KEYS, 256), BF16),
            vmem((KEYS, 2 * C), BF16),
            vmem((PAIRS, TOK, KEYS), BF16),
            vmem((PAIRS, TOK, KEYS), BF16),
            vmem((PAIRS, TOK, TOK), F32),
            vmem((PAIRS, KEYS, 256), F32),
            vmem((KEYS, TOK), F32),
            vmem((PAIRS, 256, TOK), BF16),
            dma((9,)),
            dma((8,)),
            dma((8,)),
            dma((4, 8)),
            dma((4, 8)),
            dma((8,)),
            dma((8,)),
        ],
        compiler_params=pltpu.CompilerParams(
            collective_id=0, has_side_effects=True, vmem_limit_bytes=60 * 1024 * 1024
        ),
    )(field.reshape(block), cotangent.reshape(tiles), *weights, pattern.T)
    layer_output, field_grad = pl.pallas_call(
        store,
        out_shape=(
            jax.ShapeDtypeStruct((TOK, C), BF16),
            jax.ShapeDtypeStruct((TOK, C), F32),
        ),
        in_specs=[in_vmem] * 2,
        out_specs=(in_hbm, in_hbm),
        scratch_shapes=[dma((2,))],
        compiler_params=pltpu.CompilerParams(vmem_limit_bytes=4 * 1024 * 1024),
    )(*results)
    return layer_output.reshape(field.shape), field_grad.reshape(field.shape)


def solution(mesh):
    split = P("gx", "gy", None, None)
    return jax.shard_map(
        functools.partial(shards, mesh.shape["gx"], mesh.shape["gy"]),
        mesh=mesh,
        in_specs=(split, split) + (P(),) * 7,
        out_specs=(split, split),
        check_vma=False,
    )
```

```python
import functools

import jax
import jax.numpy as jnp
from jax import lax
from jax.experimental import pallas as pl
from jax.experimental.pallas import tpu as pltpu
from jax.sharding import PartitionSpec as P

F32 = jnp.float32
BF16 = jnp.bfloat16
C = 384
FF = 1536
CHUNK = 512
PAIRS = 3
TOK = 128
KEYS = 576
OWN, AROUND, EARLY, EDGES = slice(0, 128), slice(128, 384), slice(0, 384), slice(384, 576)
EPSILON = 1e-06
MASKED = -1e30
MESH = pl.DeviceIdType.MESH

SIDES = [(1, 1), (-1, -1), (1, -1), (-1, 1), (0, 1), (0, -1), (1, 0), (-1, 0)]
PEERS = [2, 6, 1, 3, 5, 7, 0, 4]


def nn(a, b):
    return lax.dot_general(a, b, (((1,), (0,)), ((), ())), preferred_element_type=F32)


def nt(a, b):
    return lax.dot_general(a, b, (((1,), (1,)), ((), ())), preferred_element_type=F32)


def inverse_rms(v):
    return lax.rsqrt(jnp.sum(v * v, axis=-1, keepdims=True) * (1.0 / C) + EPSILON)


def norm_back(v, r, upstream):
    inner = jnp.sum(v * upstream, axis=-1, keepdims=True) * (1.0 / C)
    return r * upstream - v * (r * r * r * inner)


def iota(shape, dim):
    return lax.broadcasted_iota(jnp.int32, shape, dim)


def diagonal(both):
    return jnp.concatenate([both[:64, :128], both[64:, 128:]], axis=0)


def abreast(both):
    return jnp.concatenate([both[:TOK], both[TOK:]], axis=1)


def lanes(p, base=0):
    return slice(base + 128 * p, base + 128 * (p + 1))


def kernel(
    nx,
    ny,
    field,
    cot,
    win_qkv_h,
    win_out_h,
    axial_qkv_h,
    axial_out_h,
    mlp_in_h,
    mlp_out_h,
    pattern_h,
    out_ref,
    grad_ref,
    win_qkv,
    win_out,
    axial_qkv,
    axial_out,
    mlp_in,
    mlp_out,
    win_out_t,
    win_kv_t,
    axial_out_t,
    axial_qkv_t,
    mlp_in_t,
    pattern,
    own,
    sides,
    edges,
    cot_own,
    cot_send,
    cot_recv,
    s1_send,
    s1_recv,
    lo_send,
    lo_recv,
    g1_send,
    g1_recv,
    dn_send,
    dn_recv,
    weights1,
    kv1,
    kt1,
    vt1,
    ot1,
    scores1,
    edge_values,
    bias1,
    q1,
    local_sem,
    halo_send,
    halo_recv,
    a2a_send,
    a2a_recv,
    push_send,
    push_recv,
):
    gx = lax.axis_index("gx")
    gy = lax.axis_index("gy")

    partner = gx + 2 - 4 * ((gx >> 1) & 1)

    def step(index, by, size):
        moved = index + by
        if by > 0:
            return jnp.where(moved >= size, moved - size, moved)
        return jnp.where(moved < 0, moved + size, moved) if by else index

    def at(dx, dy):
        return (step(gx, dx, nx), step(gy, dy, ny))

    barrier = pltpu.get_barrier_semaphore()
    greeted = [at(dx, dy) for dx, dy in SIDES] + [(partner, step(gy, d, ny)) for d in PEERS]
    for device in greeted:
        pl.semaphore_signal(barrier, inc=1, device_id=device, device_id_type=MESH)

    local = [
        pltpu.make_async_copy(src, dst, local_sem.at[index])
        for index, (src, dst) in enumerate(
            [
                (field, own),
                (cot, cot_own),
                (win_qkv_h, win_qkv),
                (win_out_h, win_out),
                (axial_qkv_h, axial_qkv),
                (axial_out_h, axial_out),
                (mlp_in_h, mlp_in),
                (mlp_out_h, mlp_out),
                (pattern_h, pattern),
            ]
        )
    ]
    for copy in local[:2]:
        copy.start()
    local[0].wait()
    pl.semaphore_wait(barrier, len(greeted))

    own_y = {0: slice(0, 4), 1: slice(3, 4), -1: slice(0, 1)}
    halo = []
    for index, (dx, dy) in enumerate(SIDES):
        copy = pltpu.make_async_remote_copy(
            src_ref=own.at[:, own_y[dy]],
            dst_ref=sides.at[index - 6] if dy == 0 else edges.at[index],
            send_sem=halo_send.at[index],
            recv_sem=halo_recv.at[index],
            device_id=at(dx, dy),
            device_id_type=MESH,
        )
        copy.start()
        halo.append(copy)
    for copy in local[2:]:
        copy.start()

    def exchange(send, recv, group):
        copies = []
        for d in PEERS:
            peer = step(gy, d, ny)
            copy = pltpu.make_async_remote_copy(
                src_ref=send.at[peer],
                dst_ref=recv.at[gy],
                send_sem=a2a_send.at[group, d],
                recv_sem=a2a_recv.at[group, d],
                device_id=(partner, peer),
                device_id_type=MESH,
            )
            copy.start()
            copies.append(copy)
        return copies

    def arrived(send, recv, group):
        for d in PEERS:
            source = step(gy, -d, ny)
            pltpu.make_async_remote_copy(
                src_ref=send.at[source],
                dst_ref=recv.at[source],
                send_sem=a2a_send.at[group, d],
                recv_sem=a2a_recv.at[group, d],
                device_id=(partner, source),
                device_id_type=MESH,
            ).wait_recv()
        return recv[...].reshape(TOK, C)

    row, col = iota((TOK, TOK), 0), iota((TOK, TOK), 1)
    to_zxy = jnp.where(row == (col & 7) * 16 + (col >> 3), 1.0, 0.0).astype(BF16)
    to_xyz = jnp.where(col == (row & 7) * 16 + (row >> 3), 1.0, 0.0).astype(BF16)
    eye = jnp.where(row == col, 1.0, 0.0).astype(BF16)
    head0 = jnp.where(col < 64, 1.0, 0.0).astype(BF16)
    head1 = jnp.where(col < 64, 0.0, 1.0).astype(BF16)

    def stacked(pair):
        return jnp.concatenate([pair * head0, pair * head1], axis=0)

    local[1].wait()
    cot_send[...] = nn(to_zxy, cot_own[...].reshape(TOK, C)).astype(BF16).reshape(8, 16, C)

    def near(rows, bits, x_base, y_base):
        key, query = iota((rows, TOK), 0), iota((rows, TOK), 1)
        gap_x = (key >> (3 + bits)) + x_base - ((query >> 3) & 1)
        gap_y = ((key >> 3) & ((1 << bits) - 1)) + y_base - (query & 7)
        gap_z = ((key & 7) - (query >> 4) + 2) & 7
        inside = (jnp.abs(gap_x) <= 2) & (jnp.abs(gap_y) <= 2) & (gap_z <= 4)
        return jnp.where(inside, 0.0, MASKED)

    bias1[OWN, :] = near(TOK, 3, 0, 0)
    for index, (dx, dy) in enumerate(SIDES):
        if dy == 0:
            start = 128 * (index - 5)
            bias1[start : start + 128, :] = near(128, 3, -2 * dx, 0)
        else:
            start = 384 + 32 * index
            bias1[start : start + 32, :] = near(32, 1, -2 * dx, -2 if dy == 1 else 8)

    def window_scores(part, tokens):
        values = tokens.astype(F32)
        normed = (values * inverse_rms(values)).astype(BF16)
        kv = nn(normed, win_qkv[:, C : 3 * C]).astype(BF16)
        kv1[part] = kv
        bias = jnp.concatenate([bias1[part, :], bias1[part, :]], axis=1)
        for p in range(PAIRS):
            scores1[p, part] = nt(kv[:, lanes(p)], q1[p]) + bias
            vt1[p, :, part] = nt(eye, kv[:, lanes(p, C)]).astype(BF16)
        return normed

    field_own = own[...].reshape(TOK, C)
    field_zxy = nn(to_zxy, field_own)
    normed1_zxy = (field_zxy * inverse_rms(field_zxy)).astype(BF16)
    local[2].wait()
    query1 = nn(normed1_zxy, win_qkv[:, 0:C]).astype(BF16) * 0.125
    for p in range(PAIRS):
        q1[p] = stacked(query1[:, lanes(p)])
    window_scores(OWN, field_own)
    for copy in local[5:7]:
        copy.wait()
    axial_out_t[...] = axial_out[...].T
    mlp_in_t[...] = mlp_in[...].T
    for copy in halo[6:]:
        copy.wait_recv()
    window_scores(AROUND, sides[...].reshape(256, C))
    tops, sums, outs = [], [], []
    for p in range(PAIRS):
        scores = scores1[p, EARLY]
        tops.append(jnp.max(scores, axis=0, keepdims=True))
        e = jnp.exp(scores - tops[p])
        scores1[p, EARLY] = e
        sums.append(jnp.sum(e, axis=0, keepdims=True))
        outs.append(diagonal(nn(vt1[p, :, EARLY], e.astype(BF16))))
    for copy in halo[:6]:
        copy.wait_recv()
    cot_copies = exchange(cot_send, cot_recv, 0)
    window_scores(EDGES, edges[...].reshape(192, C))
    attended, early_scale = [], []
    for p in range(PAIRS):
        scores = scores1[p, EDGES]
        top = jnp.maximum(tops[p], jnp.max(scores, axis=0, keepdims=True))
        e = jnp.exp(scores - top)
        shrink = jnp.exp(tops[p] - top)
        scale = 1.0 / (shrink * sums[p] + jnp.sum(e, axis=0, keepdims=True))
        weights = (e * scale).astype(BF16)
        weights1[p, EDGES] = weights
        early_scale.append(shrink * scale)
        early = jnp.concatenate(
            [
                outs[p][:64] * early_scale[p][:, :TOK],
                outs[p][64:] * early_scale[p][:, TOK:],
            ],
            axis=0,
        )
        ot = early + diagonal(nn(vt1[p, :, EDGES], weights))
        ot1[p] = ot
        attended.append(ot.astype(BF16).T)
    attended = jnp.concatenate(attended, axis=1)
    local[3].wait()
    s1_send[...] = (field_zxy + nn(attended, win_out[...])).astype(BF16).reshape(8, 16, C)
    s1_copies = exchange(s1_send, s1_recv, 1)

    for p in range(PAIRS):
        weights1[p, EARLY] = (scores1[p, EARLY] * early_scale[p]).astype(BF16)
        kt1[p] = nt(eye, kv1[:, lanes(p)]).astype(BF16)
    for copy in (local[4], local[7], local[8]):
        copy.wait()
    axial_qkv_t[...] = axial_qkv[...].T
    off = ((col >> 4) - (row >> 4)) & 7
    same_line = ((row ^ col) & 8) == 0
    bias2 = []
    for head in range(2 * PAIRS):
        hit = off == 0
        for j in range(3):
            hit = hit | (off == pattern[j, head])
        bias2.append(jnp.where(hit & same_line, 0.0, MASKED))

    gradient_bf = arrived(cot_send, cot_recv, 0)
    gradient = gradient_bf.astype(F32)
    d_hidden = nt(gradient_bf, mlp_out[...])
    stream1 = arrived(s1_send, s1_recv, 1).astype(F32)
    r2 = inverse_rms(stream1)
    triple2 = nn((stream1 * r2).astype(BF16), axial_qkv[...]).astype(BF16)
    query2 = triple2[:, 0:C] * 0.125
    q2 = [stacked(query2[:, lanes(p)]) for p in range(PAIRS)]
    weights2 = []
    attended2 = []
    for p in range(PAIRS):
        pair_bias = jnp.concatenate([bias2[2 * p], bias2[2 * p + 1]], axis=0)
        scores = nt(q2[p], triple2[:, lanes(p, C)]) + pair_bias
        e = jnp.exp(scores - jnp.max(scores, axis=1, keepdims=True))
        weights = (e * (1.0 / jnp.sum(e, axis=1, keepdims=True))).astype(BF16)
        weights2.append(weights)
        values = stacked(triple2[:, lanes(p, 2 * C)])
        attended2.append(nn(abreast(weights), values))
    attended2 = jnp.concatenate(attended2, axis=1).astype(BF16)
    stream2 = (stream1 + nn(attended2, axial_out[...])).astype(BF16).astype(F32)

    r3 = inverse_rms(stream2)
    normed3 = (stream2 * r3).astype(BF16)
    hidden, d_inner = [], []
    for c in range(FF // CHUNK):
        part = slice(CHUNK * c, CHUNK * (c + 1))
        a = nn(normed3, mlp_in[:, part])
        square = a * a
        t = jnp.tanh(a * (0.7978845608028654 + (0.044715 * 0.7978845608028654) * square))
        half = 0.5 + 0.5 * t
        hidden.append((a * half).astype(BF16))
        steep = a * (2 * 0.7978845608028654 + (6 * 0.044715 * 0.7978845608028654) * square)
        slope = half + (half - half * half) * steep
        d_inner.append((d_hidden[:, part] * slope).astype(BF16))
    back = nn(jnp.concatenate(d_inner, axis=1), mlp_in_t[...])
    grad2 = gradient + norm_back(stream2, r3, back)

    back2 = nn(grad2.astype(BF16), axial_out_t[...]).astype(BF16)
    d_query, d_key, d_value = [], [], []
    for p in range(PAIRS):
        upstream = stacked(back2[:, lanes(p)])
        keys = stacked(triple2[:, lanes(p, C)])
        weights = weights2[p].astype(F32)
        d_weights = nt(upstream, triple2[:, lanes(p, 2 * C)])
        delta = jnp.sum(weights * d_weights, axis=1, keepdims=True)
        d_scores = (weights * (d_weights - delta)).astype(BF16)
        d_query.append(nn(abreast(d_scores), keys) * 0.125)
        d_key.append(nn(d_scores.T, q2[p]))
        d_value.append(nn(weights2[p].T, upstream))
    d_triple2 = jnp.concatenate(d_query + d_key + d_value, axis=1).astype(BF16)
    grad1 = grad2 + norm_back(stream1, r2, nn(d_triple2, axial_qkv_t[...]))
    g1_send[...] = grad1.astype(BF16).reshape(8, 16, C)
    g1_copies = exchange(g1_send, g1_recv, 3)

    hidden_out = nn(jnp.concatenate(hidden, axis=1), mlp_out[...])
    lo_send[...] = (stream2 + hidden_out).astype(BF16).reshape(8, 16, C)
    lo_copies = exchange(lo_send, lo_recv, 2)
    feature = iota((TOK, C), 0)
    upper = jnp.where(feature < 64, 1.0, 0.0).astype(BF16)
    lower = jnp.where(feature < 64, 0.0, 1.0).astype(BF16)
    for p in range(PAIRS):
        rows = win_out[lanes(p), :]
        values = kv1[EDGES, lanes(p, C)]
        edge_values[2 * p] = nn(values, rows * upper).astype(BF16)
        edge_values[2 * p + 1] = nn(values, rows * lower).astype(BF16)
    win_out_t[...] = win_out[...].T
    win_kv_t[0:C] = win_qkv[:, 2 * C : 3 * C].T
    win_kv_t[C : 2 * C] = win_qkv[:, C : 2 * C].T

    grad1_bf = arrived(g1_send, g1_recv, 3)
    back1 = nn(grad1_bf, win_out_t[...]).astype(BF16)
    back1_t = nt(win_out[...], grad1_bf).astype(BF16).astype(F32)
    upstream, delta = [], []
    for p in range(PAIRS):
        upstream.append(stacked(back1[:, lanes(p)]))
        product = ot1[p] * back1_t[lanes(p)]
        halves = [jnp.sum(product[h : h + 64], axis=0, keepdims=True) for h in (0, 64)]
        delta.append(jnp.concatenate(halves, axis=1))

    def window_back(part):
        d_scores, d_key, d_value = [], [], []
        for p in range(PAIRS):
            weights = weights1[p, part]
            if part == EDGES:
                halves = [nt(edge_values[2 * p + h], grad1_bf) for h in range(2)]
                d_weights = jnp.concatenate(halves, axis=1)
            else:
                d_weights = nt(kv1[part, lanes(p, C)], upstream[p])
            d_scores.append((weights.astype(F32) * (d_weights - delta[p])).astype(BF16))
            d_key.append(nn(d_scores[p], q1[p]).astype(BF16))
            d_value.append(nn(weights, upstream[p]).astype(BF16))
        d_kv = jnp.concatenate(d_value + d_key, axis=1)
        return d_scores, nn(d_kv, win_kv_t[...])

    push = []

    def send_back(index):
        dx, dy = SIDES[index]
        if dy == 0:
            rows = slice(8 * (index - 6), 8 * (index - 5))
        else:
            rows = slice(16 + 2 * index, 18 + 2 * index)
        copy = pltpu.make_async_remote_copy(
            src_ref=dn_send.at[rows],
            dst_ref=dn_recv.at[rows],
            send_sem=push_send.at[index],
            recv_sem=push_recv.at[index],
            device_id=at(-dx, -dy),
            device_id_type=MESH,
        )
        copy.start()
        push.append(copy)

    scores_edges, dn = window_back(EDGES)
    dn_send[16:28] = dn.astype(BF16).reshape(12, 16, C)
    for index in range(6):
        send_back(index)
    scores_around, dn = window_back(AROUND)
    dn_send[0:16] = dn.astype(BF16).reshape(16, 16, C)
    for index in range(6, 8):
        send_back(index)

    scores_own, d_normed = window_back(OWN)
    d_query = []
    for p in range(PAIRS):
        both = nn(kt1[p, :, EDGES], scores_edges[p]) + nn(kt1[p, :, AROUND], scores_around[p])
        both = both + nn(kt1[p, :, OWN], scores_own[p])
        d_query.append((diagonal(both) * 0.125).astype(BF16))
    d_query = nt(to_xyz, jnp.concatenate(d_query, axis=0)).astype(BF16)
    d_normed = d_normed + nt(d_query, win_qkv[:, 0:C])
    grad1_xyz = nn(to_xyz, grad1_bf)
    out_ref[...] = nn(to_xyz, arrived(lo_send, lo_recv, 2)).astype(BF16)
    for copy in push:
        copy.wait_recv()
    d_normed = d_normed + (dn_recv[0:8].astype(F32) + dn_recv[8:16].astype(F32)).reshape(TOK, C)
    first, last = [
        sum(
            dn_recv[16 + 2 * i : 18 + 2 * i].astype(F32)
            for i, (_, dy) in enumerate(SIDES)
            if dy == way
        )
        for way in (-1, 1)
    ]
    none = jnp.zeros((32, C), F32)
    rims = jnp.concatenate([first[0], none, last[0], first[1], none, last[1]], axis=0)
    field_f = own[...].reshape(TOK, C).astype(F32)
    grad_ref[...] = grad1_xyz + norm_back(field_f, inverse_rms(field_f), d_normed + rims)

    for copy in halo + cot_copies + s1_copies + lo_copies + g1_copies + push:
        copy.wait_send()


def store(out_ref, grad_ref, out_hbm, grad_hbm, sem):
    copies = [
        pltpu.make_async_copy(grad_ref, grad_hbm, sem.at[0]),
        pltpu.make_async_copy(out_ref, out_hbm, sem.at[1]),
    ]
    for copy in copies:
        copy.start()
    for copy in copies:
        copy.wait()


def shards(nx, ny, field, cotangent, *rest):
    block = (2, 4, 16, C)
    tiles = (8, 16, C)
    vmem = pltpu.VMEM
    dma = pltpu.SemaphoreType.DMA
    weights, pattern = rest[:6], rest[6]
    in_hbm = pl.BlockSpec(memory_space=pltpu.HBM)
    in_vmem = pl.BlockSpec(memory_space=pltpu.VMEM)
    results = pl.pallas_call(
        functools.partial(kernel, nx, ny),
        out_shape=(pltpu.VMEM((TOK, C), BF16), pltpu.VMEM((TOK, C), F32)),
        in_specs=[in_hbm] * 9,
        out_specs=(in_vmem, in_vmem),
        scratch_shapes=[vmem(w.shape, BF16) for w in weights]
        + [vmem((n, C), BF16) for n in (C, 2 * C, C, 3 * C, FF)]
        + [pltpu.SMEM((3, 6), jnp.int32), vmem(block, BF16)]
        + [vmem((2,) + block, BF16), vmem((6, 2, 1, 16, C), BF16)]
        + [vmem(tiles, BF16)] * 9
        + [
            vmem((28, 16, C), BF16),
            vmem((28, 16, C), BF16),
            vmem((PAIRS, KEYS, 256), BF16),
            vmem((KEYS, 2 * C), BF16),
            vmem((PAIRS, TOK, KEYS), BF16),
            vmem((PAIRS, TOK, KEYS), BF16),
            vmem((PAIRS, TOK, TOK), F32),
            vmem((PAIRS, KEYS, 256), F32),
            vmem((2 * PAIRS, 192, C), BF16),
            vmem((KEYS, TOK), F32),
            vmem((PAIRS, 256, TOK), BF16),
            dma((9,)),
            dma((8,)),
            dma((8,)),
            dma((4, 8)),
            dma((4, 8)),
            dma((8,)),
            dma((8,)),
        ],
        compiler_params=pltpu.CompilerParams(
            collective_id=0, has_side_effects=True, vmem_limit_bytes=60 * 1024 * 1024
        ),
    )(field.reshape(block), cotangent.reshape(tiles), *weights, pattern.T)
    layer_output, field_grad = pl.pallas_call(
        store,
        out_shape=(
            jax.ShapeDtypeStruct((TOK, C), BF16),
            jax.ShapeDtypeStruct((TOK, C), F32),
        ),
        in_specs=[in_vmem] * 2,
        out_specs=(in_hbm, in_hbm),
        scratch_shapes=[dma((2,))],
        compiler_params=pltpu.CompilerParams(vmem_limit_bytes=4 * 1024 * 1024),
    )(*results)
    return layer_output.reshape(field.shape), field_grad.reshape(field.shape)


def solution(mesh):
    split = P("gx", "gy", None, None)
    return jax.shard_map(
        functools.partial(shards, mesh.shape["gx"], mesh.shape["gy"]),
        mesh=mesh,
        in_specs=(split, split) + (P(),) * 7,
        out_specs=(split, split),
        check_vma=False,
    )
```

```python
import functools

import jax
import jax.numpy as jnp
from jax import lax
from jax.experimental import pallas as pl
from jax.experimental.pallas import tpu as pltpu
from jax.sharding import PartitionSpec as P

F32 = jnp.float32
BF16 = jnp.bfloat16
C = 384
FF = 1536
CHUNK = 512
PAIRS = 3
TOK = 128
KEYS = 576
OWN, AROUND, EARLY, EDGES = slice(0, 128), slice(128, 384), slice(0, 384), slice(384, 576)
EPSILON = 1e-06
MASKED = -1e30
MESH = pl.DeviceIdType.MESH

SIDES = [(1, 1), (-1, -1), (1, -1), (-1, 1), (0, 1), (0, -1), (1, 0), (-1, 0)]
PEERS = [2, 6, 1, 3, 5, 7, 0, 4]


def nn(a, b):
    return lax.dot_general(a, b, (((1,), (0,)), ((), ())), preferred_element_type=F32)


def nt(a, b):
    return lax.dot_general(a, b, (((1,), (1,)), ((), ())), preferred_element_type=F32)


def inverse_rms(v):
    return lax.rsqrt(jnp.sum(v * v, axis=-1, keepdims=True) * (1.0 / C) + EPSILON)


def norm_back(v, r, upstream):
    inner = jnp.sum(v * upstream, axis=-1, keepdims=True) * (1.0 / C)
    return r * upstream - v * (r * r * r * inner)


def iota(shape, dim):
    return lax.broadcasted_iota(jnp.int32, shape, dim)


def diagonal(both):
    return jnp.concatenate([both[:64, :128], both[64:, 128:]], axis=0)


def abreast(both):
    return jnp.concatenate([both[:TOK], both[TOK:]], axis=1)


def lanes(p, base=0):
    return slice(base + 128 * p, base + 128 * (p + 1))


def kernel(
    nx,
    ny,
    field,
    cot,
    win_qkv_h,
    win_out_h,
    axial_qkv_h,
    axial_out_h,
    mlp_in_h,
    mlp_out_h,
    pattern_h,
    out_ref,
    grad_ref,
    win_qkv,
    win_out,
    axial_qkv,
    axial_out,
    mlp_in,
    mlp_out,
    win_out_t,
    win_kv_t,
    axial_out_t,
    axial_qkv_t,
    mlp_in_t,
    pattern,
    own,
    sides,
    edges,
    cot_own,
    cot_send,
    cot_recv,
    s1_send,
    s1_recv,
    lo_send,
    lo_recv,
    g1_send,
    g1_recv,
    dn_send,
    dn_recv,
    weights1,
    kv1,
    kt1,
    vt1,
    ot1,
    scores1,
    bias1,
    q1,
    local_sem,
    halo_send,
    halo_recv,
    a2a_send,
    a2a_recv,
    push_send,
    push_recv,
):
    gx = lax.axis_index("gx")
    gy = lax.axis_index("gy")

    partner = gx + 2 - 4 * ((gx >> 1) & 1)

    def step(index, by, size):
        moved = index + by
        if by > 0:
            return jnp.where(moved >= size, moved - size, moved)
        return jnp.where(moved < 0, moved + size, moved) if by else index

    def at(dx, dy):
        return (step(gx, dx, nx), step(gy, dy, ny))

    barrier = pltpu.get_barrier_semaphore()
    greeted = [at(dx, dy) for dx, dy in SIDES] + [(partner, step(gy, d, ny)) for d in PEERS]
    for device in greeted:
        pl.semaphore_signal(barrier, inc=1, device_id=device, device_id_type=MESH)

    local = [
        pltpu.make_async_copy(src, dst, local_sem.at[index])
        for index, (src, dst) in enumerate(
            [
                (field, own),
                (cot, cot_own),
                (win_qkv_h, win_qkv),
                (win_out_h, win_out),
                (axial_qkv_h, axial_qkv),
                (axial_out_h, axial_out),
                (mlp_in_h, mlp_in),
                (mlp_out_h, mlp_out),
                (pattern_h, pattern),
            ]
        )
    ]
    for copy in local[:2]:
        copy.start()
    local[0].wait()
    pl.semaphore_wait(barrier, len(greeted))

    own_y = {0: slice(0, 4), 1: slice(3, 4), -1: slice(0, 1)}
    halo = []
    for index, (dx, dy) in enumerate(SIDES):
        copy = pltpu.make_async_remote_copy(
            src_ref=own.at[:, own_y[dy]],
            dst_ref=sides.at[index - 6] if dy == 0 else edges.at[index],
            send_sem=halo_send.at[index],
            recv_sem=halo_recv.at[index],
            device_id=at(dx, dy),
            device_id_type=MESH,
        )
        copy.start()
        halo.append(copy)
    for copy in local[2:]:
        copy.start()

    def exchange(send, recv, group):
        copies = []
        for d in PEERS:
            peer = step(gy, d, ny)
            copy = pltpu.make_async_remote_copy(
                src_ref=send.at[peer],
                dst_ref=recv.at[gy],
                send_sem=a2a_send.at[group, d],
                recv_sem=a2a_recv.at[group, d],
                device_id=(partner, peer),
                device_id_type=MESH,
            )
            copy.start()
            copies.append(copy)
        return copies

    def arrived(send, recv, group):
        for d in PEERS:
            source = step(gy, -d, ny)
            pltpu.make_async_remote_copy(
                src_ref=send.at[source],
                dst_ref=recv.at[source],
                send_sem=a2a_send.at[group, d],
                recv_sem=a2a_recv.at[group, d],
                device_id=(partner, source),
                device_id_type=MESH,
            ).wait_recv()
        return recv[...].reshape(TOK, C)

    row, col = iota((TOK, TOK), 0), iota((TOK, TOK), 1)
    to_zxy = jnp.where(row == (col & 7) * 16 + (col >> 3), 1.0, 0.0).astype(BF16)
    to_xyz = jnp.where(col == (row & 7) * 16 + (row >> 3), 1.0, 0.0).astype(BF16)
    eye = jnp.where(row == col, 1.0, 0.0).astype(BF16)
    head0 = jnp.where(col < 64, 1.0, 0.0).astype(BF16)
    head1 = jnp.where(col < 64, 0.0, 1.0).astype(BF16)

    def stacked(pair):
        return jnp.concatenate([pair * head0, pair * head1], axis=0)

    local[1].wait()
    cot_send[...] = nn(to_zxy, cot_own[...].reshape(TOK, C)).astype(BF16).reshape(8, 16, C)

    def near(rows, bits, x_base, y_base):
        key, query = iota((rows, TOK), 0), iota((rows, TOK), 1)
        gap_x = (key >> (3 + bits)) + x_base - ((query >> 3) & 1)
        gap_y = ((key >> 3) & ((1 << bits) - 1)) + y_base - (query & 7)
        gap_z = ((key & 7) - (query >> 4) + 2) & 7
        inside = (jnp.abs(gap_x) <= 2) & (jnp.abs(gap_y) <= 2) & (gap_z <= 4)
        return jnp.where(inside, 0.0, MASKED)

    bias1[OWN, :] = near(TOK, 3, 0, 0)
    for index, (dx, dy) in enumerate(SIDES):
        if dy == 0:
            start = 128 * (index - 5)
            bias1[start : start + 128, :] = near(128, 3, -2 * dx, 0)
        else:
            start = 384 + 32 * index
            bias1[start : start + 32, :] = near(32, 1, -2 * dx, -2 if dy == 1 else 8)

    def window_scores(part, tokens):
        values = tokens.astype(F32)
        normed = (values * inverse_rms(values)).astype(BF16)
        kv = nn(normed, win_qkv[:, C : 3 * C]).astype(BF16)
        kv1[part] = kv
        bias = jnp.concatenate([bias1[part, :], bias1[part, :]], axis=1)
        for p in range(PAIRS):
            scores1[p, part] = nt(kv[:, lanes(p)], q1[p]) + bias
            vt1[p, :, part] = nt(eye, kv[:, lanes(p, C)]).astype(BF16)
        return normed

    field_own = own[...].reshape(TOK, C)
    field_zxy = nn(to_zxy, field_own)
    normed1_zxy = (field_zxy * inverse_rms(field_zxy)).astype(BF16)
    local[2].wait()
    query1 = nn(normed1_zxy, win_qkv[:, 0:C]).astype(BF16) * 0.125
    for p in range(PAIRS):
        q1[p] = stacked(query1[:, lanes(p)])
    window_scores(OWN, field_own)
    for copy in local[5:7]:
        copy.wait()
    axial_out_t[...] = axial_out[...].T
    mlp_in_t[...] = mlp_in[...].T
    for copy in halo[6:]:
        copy.wait_recv()
    window_scores(AROUND, sides[...].reshape(256, C))
    tops, sums, outs = [], [], []
    for p in range(PAIRS):
        scores = scores1[p, EARLY]
        tops.append(jnp.max(scores, axis=0, keepdims=True))
        e = jnp.exp(scores - tops[p])
        scores1[p, EARLY] = e
        sums.append(jnp.sum(e, axis=0, keepdims=True))
        outs.append(diagonal(nn(vt1[p, :, EARLY], e.astype(BF16))))
    for copy in halo[:6]:
        copy.wait_recv()
    window_scores(EDGES, edges[...].reshape(192, C))
    cot_copies = exchange(cot_send, cot_recv, 0)
    attended, early_scale = [], []
    for p in range(PAIRS):
        scores = scores1[p, EDGES]
        top = jnp.maximum(tops[p], jnp.max(scores, axis=0, keepdims=True))
        e = jnp.exp(scores - top)
        shrink = jnp.exp(tops[p] - top)
        scale = 1.0 / (shrink * sums[p] + jnp.sum(e, axis=0, keepdims=True))
        weights = (e * scale).astype(BF16)
        weights1[p, EDGES] = weights
        early_scale.append(shrink * scale)
        early = jnp.concatenate(
            [
                outs[p][:64] * early_scale[p][:, :TOK],
                outs[p][64:] * early_scale[p][:, TOK:],
            ],
            axis=0,
        )
        ot = early + diagonal(nn(vt1[p, :, EDGES], weights))
        ot1[p] = ot
        attended.append(ot.astype(BF16).T)
    attended = jnp.concatenate(attended, axis=1)
    local[3].wait()
    s1_send[...] = (field_zxy + nn(attended, win_out[...])).astype(BF16).reshape(8, 16, C)
    s1_copies = exchange(s1_send, s1_recv, 1)

    for p in range(PAIRS):
        weights1[p, EARLY] = (scores1[p, EARLY] * early_scale[p]).astype(BF16)
        kt1[p] = nt(eye, kv1[:, lanes(p)]).astype(BF16)
    for copy in (local[4], local[7], local[8]):
        copy.wait()
    axial_qkv_t[...] = axial_qkv[...].T
    off = ((col >> 4) - (row >> 4)) & 7
    same_line = ((row ^ col) & 8) == 0
    bias2 = []
    for head in range(2 * PAIRS):
        hit = off == 0
        for j in range(3):
            hit = hit | (off == pattern[j, head])
        bias2.append(jnp.where(hit & same_line, 0.0, MASKED))

    gradient_bf = arrived(cot_send, cot_recv, 0)
    gradient = gradient_bf.astype(F32)
    d_hidden = nt(gradient_bf, mlp_out[...])
    stream1 = arrived(s1_send, s1_recv, 1).astype(F32)
    r2 = inverse_rms(stream1)
    triple2 = nn((stream1 * r2).astype(BF16), axial_qkv[...]).astype(BF16)
    query2 = triple2[:, 0:C] * 0.125
    q2 = [stacked(query2[:, lanes(p)]) for p in range(PAIRS)]
    weights2 = []
    attended2 = []
    for p in range(PAIRS):
        pair_bias = jnp.concatenate([bias2[2 * p], bias2[2 * p + 1]], axis=0)
        scores = nt(q2[p], triple2[:, lanes(p, C)]) + pair_bias
        e = jnp.exp(scores - jnp.max(scores, axis=1, keepdims=True))
        weights = (e * (1.0 / jnp.sum(e, axis=1, keepdims=True))).astype(BF16)
        weights2.append(weights)
        values = stacked(triple2[:, lanes(p, 2 * C)])
        attended2.append(nn(abreast(weights), values))
    attended2 = jnp.concatenate(attended2, axis=1).astype(BF16)
    stream2 = (stream1 + nn(attended2, axial_out[...])).astype(BF16).astype(F32)

    r3 = inverse_rms(stream2)
    normed3 = (stream2 * r3).astype(BF16)
    hidden, d_inner = [], []
    for c in range(FF // CHUNK):
        part = slice(CHUNK * c, CHUNK * (c + 1))
        a = nn(normed3, mlp_in[:, part])
        square = a * a
        t = jnp.tanh(a * (0.7978845608028654 + (0.044715 * 0.7978845608028654) * square))
        half = 0.5 + 0.5 * t
        hidden.append((a * half).astype(BF16))
        steep = a * (2 * 0.7978845608028654 + (6 * 0.044715 * 0.7978845608028654) * square)
        slope = half + (half - half * half) * steep
        d_inner.append((d_hidden[:, part] * slope).astype(BF16))
    back = nn(jnp.concatenate(d_inner, axis=1), mlp_in_t[...])
    grad2 = gradient + norm_back(stream2, r3, back)

    back2 = nn(grad2.astype(BF16), axial_out_t[...]).astype(BF16)
    d_query, d_key, d_value = [], [], []
    for p in range(PAIRS):
        upstream = stacked(back2[:, lanes(p)])
        keys = stacked(triple2[:, lanes(p, C)])
        weights = weights2[p].astype(F32)
        d_weights = nt(upstream, triple2[:, lanes(p, 2 * C)])
        delta = jnp.sum(weights * d_weights, axis=1, keepdims=True)
        d_scores = (weights * (d_weights - delta)).astype(BF16)
        d_query.append(nn(abreast(d_scores), keys) * 0.125)
        d_key.append(nn(d_scores.T, q2[p]))
        d_value.append(nn(weights2[p].T, upstream))
    d_triple2 = jnp.concatenate(d_query + d_key + d_value, axis=1).astype(BF16)
    grad1 = grad2 + norm_back(stream1, r2, nn(d_triple2, axial_qkv_t[...]))
    g1_send[...] = grad1.astype(BF16).reshape(8, 16, C)
    g1_copies = exchange(g1_send, g1_recv, 3)

    hidden_out = nn(jnp.concatenate(hidden, axis=1), mlp_out[...])
    lo_send[...] = (stream2 + hidden_out).astype(BF16).reshape(8, 16, C)
    lo_copies = exchange(lo_send, lo_recv, 2)
    win_out_t[...] = win_out[...].T
    win_kv_t[0:C] = win_qkv[:, 2 * C : 3 * C].T
    win_kv_t[C : 2 * C] = win_qkv[:, C : 2 * C].T

    grad1_bf = arrived(g1_send, g1_recv, 3)
    back1 = nn(grad1_bf, win_out_t[...]).astype(BF16)
    back1_t = nt(win_out[...], grad1_bf).astype(BF16).astype(F32)
    upstream, delta = [], []
    for p in range(PAIRS):
        upstream.append(stacked(back1[:, lanes(p)]))
        product = ot1[p] * back1_t[lanes(p)]
        halves = [jnp.sum(product[h : h + 64], axis=0, keepdims=True) for h in (0, 64)]
        delta.append(jnp.concatenate(halves, axis=1))

    def window_back(part):
        d_scores, d_key, d_value = [], [], []
        for p in range(PAIRS):
            weights = weights1[p, part]
            d_weights = nt(kv1[part, lanes(p, C)], upstream[p])
            d_scores.append((weights.astype(F32) * (d_weights - delta[p])).astype(BF16))
            d_key.append(nn(d_scores[p], q1[p]).astype(BF16))
            d_value.append(nn(weights, upstream[p]).astype(BF16))
        d_kv = jnp.concatenate(d_value + d_key, axis=1)
        return d_scores, nn(d_kv, win_kv_t[...])

    push = []

    def send_back(index):
        dx, dy = SIDES[index]
        if dy == 0:
            rows = slice(8 * (index - 6), 8 * (index - 5))
        else:
            rows = slice(16 + 2 * index, 18 + 2 * index)
        copy = pltpu.make_async_remote_copy(
            src_ref=dn_send.at[rows],
            dst_ref=dn_recv.at[rows],
            send_sem=push_send.at[index],
            recv_sem=push_recv.at[index],
            device_id=at(-dx, -dy),
            device_id_type=MESH,
        )
        copy.start()
        push.append(copy)

    scores_edges, dn = window_back(EDGES)
    dn_send[16:28] = dn.astype(BF16).reshape(12, 16, C)
    for index in range(6):
        send_back(index)
    scores_around, dn = window_back(AROUND)
    dn_send[0:16] = dn.astype(BF16).reshape(16, 16, C)
    for index in range(6, 8):
        send_back(index)

    scores_own, d_normed = window_back(OWN)
    d_query = []
    for p in range(PAIRS):
        both = nn(kt1[p, :, EDGES], scores_edges[p]) + nn(kt1[p, :, AROUND], scores_around[p])
        both = both + nn(kt1[p, :, OWN], scores_own[p])
        d_query.append((diagonal(both) * 0.125).astype(BF16))
    d_query = nt(to_xyz, jnp.concatenate(d_query, axis=0)).astype(BF16)
    d_normed = d_normed + nt(d_query, win_qkv[:, 0:C])
    field_f = own[...].reshape(TOK, C).astype(F32)
    r1 = inverse_rms(field_f)
    grad_ref[...] = nn(to_xyz, grad1_bf)
    out_ref[...] = nn(to_xyz, arrived(lo_send, lo_recv, 2)).astype(BF16)
    for copy in push:
        copy.wait_recv()
    d_normed = d_normed + (dn_recv[0:8].astype(F32) + dn_recv[8:16].astype(F32)).reshape(TOK, C)
    first, last = [
        sum(
            dn_recv[16 + 2 * i : 18 + 2 * i].astype(F32)
            for i, (_, dy) in enumerate(SIDES)
            if dy == way
        )
        for way in (-1, 1)
    ]
    none = jnp.zeros((32, C), F32)
    rims = jnp.concatenate([first[0], none, last[0], first[1], none, last[1]], axis=0)
    grad_ref[...] += norm_back(field_f, r1, d_normed + rims)

    for copy in halo + cot_copies + s1_copies + lo_copies + g1_copies + push:
        copy.wait_send()


def store(out_ref, grad_ref, out_hbm, grad_hbm, sem):
    copies = [
        pltpu.make_async_copy(grad_ref, grad_hbm, sem.at[0]),
        pltpu.make_async_copy(out_ref, out_hbm, sem.at[1]),
    ]
    for copy in copies:
        copy.start()
    for copy in copies:
        copy.wait()


def shards(nx, ny, field, cotangent, *rest):
    block = (2, 4, 16, C)
    tiles = (8, 16, C)
    vmem = pltpu.VMEM
    dma = pltpu.SemaphoreType.DMA
    weights, pattern = rest[:6], rest[6]
    in_hbm = pl.BlockSpec(memory_space=pltpu.HBM)
    in_vmem = pl.BlockSpec(memory_space=pltpu.VMEM)
    results = pl.pallas_call(
        functools.partial(kernel, nx, ny),
        out_shape=(pltpu.VMEM((TOK, C), BF16), pltpu.VMEM((TOK, C), F32)),
        in_specs=[in_hbm] * 9,
        out_specs=(in_vmem, in_vmem),
        scratch_shapes=[vmem(w.shape, BF16) for w in weights]
        + [vmem((n, C), BF16) for n in (C, 2 * C, C, 3 * C, FF)]
        + [pltpu.SMEM((3, 6), jnp.int32), vmem(block, BF16)]
        + [vmem((2,) + block, BF16), vmem((6, 2, 1, 16, C), BF16)]
        + [vmem(tiles, BF16)] * 9
        + [
            vmem((28, 16, C), BF16),
            vmem((28, 16, C), BF16),
            vmem((PAIRS, KEYS, 256), BF16),
            vmem((KEYS, 2 * C), BF16),
            vmem((PAIRS, TOK, KEYS), BF16),
            vmem((PAIRS, TOK, KEYS), BF16),
            vmem((PAIRS, TOK, TOK), F32),
            vmem((PAIRS, KEYS, 256), F32),
            vmem((KEYS, TOK), F32),
            vmem((PAIRS, 256, TOK), BF16),
            dma((9,)),
            dma((8,)),
            dma((8,)),
            dma((4, 8)),
            dma((4, 8)),
            dma((8,)),
            dma((8,)),
        ],
        compiler_params=pltpu.CompilerParams(
            collective_id=0, has_side_effects=True, vmem_limit_bytes=60 * 1024 * 1024
        ),
    )(field.reshape(block), cotangent.reshape(tiles), *weights, pattern.T)
    layer_output, field_grad = pl.pallas_call(
        store,
        out_shape=(
            jax.ShapeDtypeStruct((TOK, C), BF16),
            jax.ShapeDtypeStruct((TOK, C), F32),
        ),
        in_specs=[in_vmem] * 2,
        out_specs=(in_hbm, in_hbm),
        scratch_shapes=[dma((2,))],
        compiler_params=pltpu.CompilerParams(vmem_limit_bytes=4 * 1024 * 1024),
    )(*results)
    return layer_output.reshape(field.shape), field_grad.reshape(field.shape)


def solution(mesh):
    split = P("gx", "gy", None, None)
    return jax.shard_map(
        functools.partial(shards, mesh.shape["gx"], mesh.shape["gy"]),
        mesh=mesh,
        in_specs=(split, split) + (P(),) * 7,
        out_specs=(split, split),
        check_vma=False,
    )
```

```python
import functools

import jax
import jax.numpy as jnp
from jax import lax
from jax.experimental import pallas as pl
from jax.experimental.pallas import tpu as pltpu
from jax.sharding import PartitionSpec as P

F32 = jnp.float32
BF16 = jnp.bfloat16
C = 384
FF = 1536
CHUNK = 512
PAIRS = 3
TOK = 128
KEYS = 576
OWN, AROUND, EARLY, EDGES = slice(0, 128), slice(128, 384), slice(0, 384), slice(384, 576)
EPSILON = 1e-06
MASKED = -1e30
MESH = pl.DeviceIdType.MESH

SIDES = [(1, 1), (-1, -1), (1, -1), (-1, 1), (0, 1), (0, -1), (1, 0), (-1, 0)]
PEERS = [2, 6, 1, 3, 5, 7, 0, 4]


def nn(a, b):
    return lax.dot_general(a, b, (((1,), (0,)), ((), ())), preferred_element_type=F32)


def nt(a, b):
    return lax.dot_general(a, b, (((1,), (1,)), ((), ())), preferred_element_type=F32)


def inverse_rms(v):
    return lax.rsqrt(jnp.sum(v * v, axis=-1, keepdims=True) * (1.0 / C) + EPSILON)


def norm_back(v, r, upstream):
    inner = jnp.sum(v * upstream, axis=-1, keepdims=True) * (1.0 / C)
    return r * upstream - v * (r * r * r * inner)


def iota(shape, dim):
    return lax.broadcasted_iota(jnp.int32, shape, dim)


def diagonal(both):
    return jnp.concatenate([both[:64, :128], both[64:, 128:]], axis=0)


def abreast(both):
    return jnp.concatenate([both[:TOK], both[TOK:]], axis=1)


def lanes(p, base=0):
    return slice(base + 128 * p, base + 128 * (p + 1))


def kernel(
    nx,
    ny,
    field,
    cot,
    win_qkv_h,
    win_out_h,
    axial_qkv_h,
    axial_out_h,
    mlp_in_h,
    mlp_out_h,
    pattern_h,
    out_ref,
    grad_ref,
    win_qkv,
    win_out,
    axial_qkv,
    axial_out,
    mlp_in,
    mlp_out,
    win_out_t,
    win_kv_t,
    axial_out_t,
    axial_qkv_t,
    mlp_in_t,
    pattern,
    own,
    sides,
    edges,
    cot_own,
    cot_send,
    cot_recv,
    s1_send,
    s1_recv,
    lo_send,
    lo_recv,
    g1_send,
    g1_recv,
    dn_send,
    dn_recv,
    weights1,
    kv1,
    kt1,
    vt1,
    ot1,
    scores1,
    bias1,
    q1,
    local_sem,
    halo_send,
    halo_recv,
    a2a_send,
    a2a_recv,
    push_send,
    push_recv,
):
    gx = lax.axis_index("gx")
    gy = lax.axis_index("gy")

    partner = gx + 2 - 4 * ((gx >> 1) & 1)

    def step(index, by, size):
        moved = index + by
        if by > 0:
            return jnp.where(moved >= size, moved - size, moved)
        return jnp.where(moved < 0, moved + size, moved) if by else index

    def at(dx, dy):
        return (step(gx, dx, nx), step(gy, dy, ny))

    barrier = pltpu.get_barrier_semaphore()
    greeted = [at(dx, dy) for dx, dy in SIDES] + [(partner, step(gy, d, ny)) for d in PEERS]
    for device in greeted:
        pl.semaphore_signal(barrier, inc=1, device_id=device, device_id_type=MESH)

    local = [
        pltpu.make_async_copy(src, dst, local_sem.at[index])
        for index, (src, dst) in enumerate(
            [
                (field, own),
                (cot, cot_own),
                (win_qkv_h, win_qkv),
                (win_out_h, win_out),
                (axial_qkv_h, axial_qkv),
                (axial_out_h, axial_out),
                (mlp_in_h, mlp_in),
                (mlp_out_h, mlp_out),
                (pattern_h, pattern),
            ]
        )
    ]
    for copy in local[:2]:
        copy.start()
    local[0].wait()
    pl.semaphore_wait(barrier, len(greeted))

    own_y = {0: slice(0, 4), 1: slice(3, 4), -1: slice(0, 1)}
    halo = []
    for index, (dx, dy) in enumerate(SIDES):
        copy = pltpu.make_async_remote_copy(
            src_ref=own.at[:, own_y[dy]],
            dst_ref=sides.at[index - 6] if dy == 0 else edges.at[index],
            send_sem=halo_send.at[index],
            recv_sem=halo_recv.at[index],
            device_id=at(dx, dy),
            device_id_type=MESH,
        )
        copy.start()
        halo.append(copy)
    for copy in local[2:]:
        copy.start()

    def exchange(send, recv, group):
        copies = []
        for d in PEERS:
            peer = step(gy, d, ny)
            copy = pltpu.make_async_remote_copy(
                src_ref=send.at[peer],
                dst_ref=recv.at[gy],
                send_sem=a2a_send.at[group, d],
                recv_sem=a2a_recv.at[group, d],
                device_id=(partner, peer),
                device_id_type=MESH,
            )
            copy.start()
            copies.append(copy)
        return copies

    def arrived(send, recv, group):
        for d in PEERS:
            source = step(gy, -d, ny)
            pltpu.make_async_remote_copy(
                src_ref=send.at[source],
                dst_ref=recv.at[source],
                send_sem=a2a_send.at[group, d],
                recv_sem=a2a_recv.at[group, d],
                device_id=(partner, source),
                device_id_type=MESH,
            ).wait_recv()
        return recv[...].reshape(TOK, C)

    row, col = iota((TOK, TOK), 0), iota((TOK, TOK), 1)
    to_zxy = jnp.where(row == (col & 7) * 16 + (col >> 3), 1.0, 0.0).astype(BF16)
    to_xyz = jnp.where(col == (row & 7) * 16 + (row >> 3), 1.0, 0.0).astype(BF16)
    eye = jnp.where(row == col, 1.0, 0.0).astype(BF16)
    head0 = jnp.where(col < 64, 1.0, 0.0).astype(BF16)
    head1 = jnp.where(col < 64, 0.0, 1.0).astype(BF16)

    def stacked(pair):
        return jnp.concatenate([pair * head0, pair * head1], axis=0)

    local[1].wait()
    cot_send[...] = nn(to_zxy, cot_own[...].reshape(TOK, C)).astype(BF16).reshape(8, 16, C)

    def near(rows, bits, x_base, y_base):
        key, query = iota((rows, TOK), 0), iota((rows, TOK), 1)
        gap_x = (key >> (3 + bits)) + x_base - ((query >> 3) & 1)
        gap_y = ((key >> 3) & ((1 << bits) - 1)) + y_base - (query & 7)
        gap_z = ((key & 7) - (query >> 4) + 2) & 7
        inside = (jnp.abs(gap_x) <= 2) & (jnp.abs(gap_y) <= 2) & (gap_z <= 4)
        return jnp.where(inside, 0.0, MASKED)

    bias1[OWN, :] = near(TOK, 3, 0, 0)
    for index, (dx, dy) in enumerate(SIDES):
        if dy == 0:
            start = 128 * (index - 5)
            bias1[start : start + 128, :] = near(128, 3, -2 * dx, 0)
        else:
            start = 384 + 32 * index
            bias1[start : start + 32, :] = near(32, 1, -2 * dx, -2 if dy == 1 else 8)

    def window_scores(part, tokens):
        values = tokens.astype(F32)
        normed = (values * inverse_rms(values)).astype(BF16)
        kv = nn(normed, win_qkv[:, C : 3 * C]).astype(BF16)
        kv1[part] = kv
        bias = jnp.concatenate([bias1[part, :], bias1[part, :]], axis=1)
        for p in range(PAIRS):
            scores1[p, part] = nt(kv[:, lanes(p)], q1[p]) + bias
            vt1[p, :, part] = nt(eye, kv[:, lanes(p, C)]).astype(BF16)
        return normed

    field_own = own[...].reshape(TOK, C)
    field_zxy = nn(to_zxy, field_own)
    normed1_zxy = (field_zxy * inverse_rms(field_zxy)).astype(BF16)
    local[2].wait()
    query1 = nn(normed1_zxy, win_qkv[:, 0:C]).astype(BF16) * 0.125
    for p in range(PAIRS):
        q1[p] = stacked(query1[:, lanes(p)])
    window_scores(OWN, field_own)
    for copy in local[5:7]:
        copy.wait()
    axial_out_t[...] = axial_out[...].T
    mlp_in_t[...] = mlp_in[...].T
    for copy in halo[6:]:
        copy.wait_recv()
    window_scores(AROUND, sides[...].reshape(256, C))
    tops, sums, outs = [], [], []
    for p in range(PAIRS):
        scores = scores1[p, EARLY]
        tops.append(jnp.max(scores, axis=0, keepdims=True))
        e = jnp.exp(scores - tops[p])
        scores1[p, EARLY] = e
        sums.append(jnp.sum(e, axis=0, keepdims=True))
        outs.append(diagonal(nn(vt1[p, :, EARLY], e.astype(BF16))))
    for copy in halo[:6]:
        copy.wait_recv()
    cot_copies = exchange(cot_send, cot_recv, 0)
    window_scores(EDGES, edges[...].reshape(192, C))
    attended, early_scale = [], []
    for p in range(PAIRS):
        scores = scores1[p, EDGES]
        top = jnp.maximum(tops[p], jnp.max(scores, axis=0, keepdims=True))
        e = jnp.exp(scores - top)
        shrink = jnp.exp(tops[p] - top)
        scale = 1.0 / (shrink * sums[p] + jnp.sum(e, axis=0, keepdims=True))
        weights = (e * scale).astype(BF16)
        weights1[p, EDGES] = weights
        early_scale.append(shrink * scale)
        early = jnp.concatenate(
            [
                outs[p][:64] * early_scale[p][:, :TOK],
                outs[p][64:] * early_scale[p][:, TOK:],
            ],
            axis=0,
        )
        ot = early + diagonal(nn(vt1[p, :, EDGES], weights))
        ot1[p] = ot
        attended.append(ot.astype(BF16).T)
    attended = jnp.concatenate(attended, axis=1)
    local[3].wait()
    s1_send[...] = (field_zxy + nn(attended, win_out[...])).astype(BF16).reshape(8, 16, C)
    s1_copies = exchange(s1_send, s1_recv, 1)

    for p in range(PAIRS):
        weights1[p, EARLY] = (scores1[p, EARLY] * early_scale[p]).astype(BF16)
        kt1[p] = nt(eye, kv1[:, lanes(p)]).astype(BF16)
    for copy in (local[4], local[7], local[8]):
        copy.wait()
    axial_qkv_t[...] = axial_qkv[...].T
    off = ((col >> 4) - (row >> 4)) & 7
    same_line = ((row ^ col) & 8) == 0
    bias2 = []
    for head in range(2 * PAIRS):
        hit = off == 0
        for j in range(3):
            hit = hit | (off == pattern[j, head])
        bias2.append(jnp.where(hit & same_line, 0.0, MASKED))

    gradient_bf = arrived(cot_send, cot_recv, 0)
    gradient = gradient_bf.astype(F32)
    d_hidden = nt(gradient_bf, mlp_out[...])
    stream1 = arrived(s1_send, s1_recv, 1).astype(F32)
    r2 = inverse_rms(stream1)
    triple2 = nn((stream1 * r2).astype(BF16), axial_qkv[...]).astype(BF16)
    query2 = triple2[:, 0:C] * 0.125
    q2 = [stacked(query2[:, lanes(p)]) for p in range(PAIRS)]
    weights2 = []
    attended2 = []
    for p in range(PAIRS):
        pair_bias = jnp.concatenate([bias2[2 * p], bias2[2 * p + 1]], axis=0)
        scores = nt(q2[p], triple2[:, lanes(p, C)]) + pair_bias
        e = jnp.exp(scores - jnp.max(scores, axis=1, keepdims=True))
        weights = (e * (1.0 / jnp.sum(e, axis=1, keepdims=True))).astype(BF16)
        weights2.append(weights)
        values = stacked(triple2[:, lanes(p, 2 * C)])
        attended2.append(nn(abreast(weights), values))
    attended2 = jnp.concatenate(attended2, axis=1).astype(BF16)
    stream2 = (stream1 + nn(attended2, axial_out[...])).astype(BF16).astype(F32)

    r3 = inverse_rms(stream2)
    normed3 = (stream2 * r3).astype(BF16)
    hidden, d_inner = [], []
    for c in range(FF // CHUNK):
        part = slice(CHUNK * c, CHUNK * (c + 1))
        a = nn(normed3, mlp_in[:, part])
        square = a * a
        t = jnp.tanh(a * (0.7978845608028654 + (0.044715 * 0.7978845608028654) * square))
        half = 0.5 + 0.5 * t
        hidden.append((a * half).astype(BF16))
        steep = a * (2 * 0.7978845608028654 + (6 * 0.044715 * 0.7978845608028654) * square)
        slope = half + (half - half * half) * steep
        d_inner.append((d_hidden[:, part] * slope).astype(BF16))
    back = nn(jnp.concatenate(d_inner, axis=1), mlp_in_t[...])
    grad2 = gradient + norm_back(stream2, r3, back)

    back2 = nn(grad2.astype(BF16), axial_out_t[...]).astype(BF16)
    d_query, d_key, d_value = [], [], []
    for p in range(PAIRS):
        upstream = stacked(back2[:, lanes(p)])
        keys = stacked(triple2[:, lanes(p, C)])
        weights = weights2[p].astype(F32)
        d_weights = nt(upstream, triple2[:, lanes(p, 2 * C)])
        delta = jnp.sum(weights * d_weights, axis=1, keepdims=True)
        d_scores = (weights * (d_weights - delta)).astype(BF16)
        d_query.append(nn(abreast(d_scores), keys) * 0.125)
        d_key.append(nn(d_scores.T, q2[p]))
        d_value.append(nn(weights2[p].T, upstream))
    d_triple2 = jnp.concatenate(d_query + d_key + d_value, axis=1).astype(BF16)
    grad1 = grad2 + norm_back(stream1, r2, nn(d_triple2, axial_qkv_t[...]))
    g1_send[...] = grad1.astype(BF16).reshape(8, 16, C)
    g1_copies = exchange(g1_send, g1_recv, 3)

    hidden_out = nn(jnp.concatenate(hidden, axis=1), mlp_out[...])
    lo_send[...] = (stream2 + hidden_out).astype(BF16).reshape(8, 16, C)
    lo_copies = exchange(lo_send, lo_recv, 2)
    win_out_t[...] = win_out[...].T
    win_kv_t[0:C] = win_qkv[:, 2 * C : 3 * C].T
    win_kv_t[C : 2 * C] = win_qkv[:, C : 2 * C].T

    grad1_bf = arrived(g1_send, g1_recv, 3)
    back1 = nn(grad1_bf, win_out_t[...]).astype(BF16)
    back1_t = nt(win_out[...], grad1_bf).astype(BF16).astype(F32)
    upstream, delta = [], []
    for p in range(PAIRS):
        upstream.append(stacked(back1[:, lanes(p)]))
        product = ot1[p] * back1_t[lanes(p)]
        halves = [jnp.sum(product[h : h + 64], axis=0, keepdims=True) for h in (0, 64)]
        delta.append(jnp.concatenate(halves, axis=1))

    def window_back(part):
        d_scores, d_key, d_value = [], [], []
        for p in range(PAIRS):
            weights = weights1[p, part]
            d_weights = nt(kv1[part, lanes(p, C)], upstream[p])
            d_scores.append((weights.astype(F32) * (d_weights - delta[p])).astype(BF16))
            d_key.append(nn(d_scores[p], q1[p]).astype(BF16))
            d_value.append(nn(weights, upstream[p]).astype(BF16))
        d_kv = jnp.concatenate(d_value + d_key, axis=1)
        return d_scores, nn(d_kv, win_kv_t[...])

    push = []

    def send_back(index):
        dx, dy = SIDES[index]
        if dy == 0:
            rows = slice(8 * (index - 6), 8 * (index - 5))
        else:
            rows = slice(16 + 2 * index, 18 + 2 * index)
        copy = pltpu.make_async_remote_copy(
            src_ref=dn_send.at[rows],
            dst_ref=dn_recv.at[rows],
            send_sem=push_send.at[index],
            recv_sem=push_recv.at[index],
            device_id=at(-dx, -dy),
            device_id_type=MESH,
        )
        copy.start()
        push.append(copy)

    scores_edges, dn = window_back(EDGES)
    dn_send[16:28] = dn.astype(BF16).reshape(12, 16, C)
    for index in range(6):
        send_back(index)
    scores_around, dn = window_back(AROUND)
    dn_send[0:16] = dn.astype(BF16).reshape(16, 16, C)
    for index in range(6, 8):
        send_back(index)

    scores_own, d_normed = window_back(OWN)
    d_query = []
    for p in range(PAIRS):
        both = nn(kt1[p, :, EDGES], scores_edges[p]) + nn(kt1[p, :, AROUND], scores_around[p])
        both = both + nn(kt1[p, :, OWN], scores_own[p])
        d_query.append((diagonal(both) * 0.125).astype(BF16))
    d_query = nt(to_xyz, jnp.concatenate(d_query, axis=0)).astype(BF16)
    d_normed = d_normed + nt(d_query, win_qkv[:, 0:C])
    field_f = own[...].reshape(TOK, C).astype(F32)
    r1 = inverse_rms(field_f)
    grad_ref[...] = nn(to_xyz, grad1_bf)
    out_ref[...] = nn(to_xyz, arrived(lo_send, lo_recv, 2)).astype(BF16)
    for copy in push:
        copy.wait_recv()
    d_normed = d_normed + (dn_recv[0:8].astype(F32) + dn_recv[8:16].astype(F32)).reshape(TOK, C)
    first, last = [
        sum(
            dn_recv[16 + 2 * i : 18 + 2 * i].astype(F32)
            for i, (_, dy) in enumerate(SIDES)
            if dy == way
        )
        for way in (-1, 1)
    ]
    none = jnp.zeros((32, C), F32)
    rims = jnp.concatenate([first[0], none, last[0], first[1], none, last[1]], axis=0)
    grad_ref[...] += norm_back(field_f, r1, d_normed + rims)

    for copy in halo + cot_copies + s1_copies + lo_copies + g1_copies + push:
        copy.wait_send()


def store(out_ref, grad_ref, out_hbm, grad_hbm, sem):
    copies = [
        pltpu.make_async_copy(grad_ref, grad_hbm, sem.at[0]),
        pltpu.make_async_copy(out_ref, out_hbm, sem.at[1]),
    ]
    for copy in copies:
        copy.start()
    for copy in copies:
        copy.wait()


def shards(nx, ny, field, cotangent, *rest):
    block = (2, 4, 16, C)
    tiles = (8, 16, C)
    vmem = pltpu.VMEM
    dma = pltpu.SemaphoreType.DMA
    weights, pattern = rest[:6], rest[6]
    in_hbm = pl.BlockSpec(memory_space=pltpu.HBM)
    in_vmem = pl.BlockSpec(memory_space=pltpu.VMEM)
    results = pl.pallas_call(
        functools.partial(kernel, nx, ny),
        out_shape=(pltpu.VMEM((TOK, C), BF16), pltpu.VMEM((TOK, C), F32)),
        in_specs=[in_hbm] * 9,
        out_specs=(in_vmem, in_vmem),
        scratch_shapes=[vmem(w.shape, BF16) for w in weights]
        + [vmem((n, C), BF16) for n in (C, 2 * C, C, 3 * C, FF)]
        + [pltpu.SMEM((3, 6), jnp.int32), vmem(block, BF16)]
        + [vmem((2,) + block, BF16), vmem((6, 2, 1, 16, C), BF16)]
        + [vmem(tiles, BF16)] * 9
        + [
            vmem((28, 16, C), BF16),
            vmem((28, 16, C), BF16),
            vmem((PAIRS, KEYS, 256), BF16),
            vmem((KEYS, 2 * C), BF16),
            vmem((PAIRS, TOK, KEYS), BF16),
            vmem((PAIRS, TOK, KEYS), BF16),
            vmem((PAIRS, TOK, TOK), F32),
            vmem((PAIRS, KEYS, 256), F32),
            vmem((KEYS, TOK), F32),
            vmem((PAIRS, 256, TOK), BF16),
            dma((9,)),
            dma((8,)),
            dma((8,)),
            dma((4, 8)),
            dma((4, 8)),
            dma((8,)),
            dma((8,)),
        ],
        compiler_params=pltpu.CompilerParams(
            collective_id=0, has_side_effects=True, vmem_limit_bytes=60 * 1024 * 1024
        ),
    )(field.reshape(block), cotangent.reshape(tiles), *weights, pattern.T)
    layer_output, field_grad = pl.pallas_call(
        store,
        out_shape=(
            jax.ShapeDtypeStruct((TOK, C), BF16),
            jax.ShapeDtypeStruct((TOK, C), F32),
        ),
        in_specs=[in_vmem] * 2,
        out_specs=(in_hbm, in_hbm),
        scratch_shapes=[dma((2,))],
        compiler_params=pltpu.CompilerParams(vmem_limit_bytes=4 * 1024 * 1024),
    )(*results)
    return layer_output.reshape(field.shape), field_grad.reshape(field.shape)


def solution(mesh):
    split = P("gx", "gy", None, None)
    return jax.shard_map(
        functools.partial(shards, mesh.shape["gx"], mesh.shape["gy"]),
        mesh=mesh,
        in_specs=(split, split) + (P(),) * 7,
        out_specs=(split, split),
        check_vma=False,
    )
```
